32 devices in a mesh: tile: 8 (over z, y), filt: 2 (over x), mc: 2 (over core).
Axes of the slice: x: 2, y: 2, z: 4, core: 2. Of those that a mesh axis runs over, the one named last changes fastest.
Arguments:
- sky_mean: float32 [8, 6, 256, 256], P('tile', 'filt'), may hold values from -6 to 6
- sky_log_scale: float32 [8, 6, 256, 256], P('tile', 'filt'), may hold values from -2.5 to -0.5
- noise_draw: bfloat16 [2, 8, 6, 256, 256], P('mc', 'tile', 'filt'), may hold values from -5 to 5
- observed: bfloat16 [8, 6, 256, 256], P('tile', 'filt'), may hold values from -6 to 6
- inv_var: bfloat16 [8, 6, 256, 256], P('tile', 'filt'), may hold values from 0.5 to 4
- intersections: int32 [8, 6, 3, 9], replicated, may hold values from -128 to 128, as said below
- counts: int32 [8, 6], replicated, may hold values from 1 to 3, as said below
- kernels: float32 [8, 2, 25], replicated, may hold values from 0 to 0.08
- psf_coeffs: bfloat16 [8, 6, 6, 3], replicated, may hold values from -0.5 to 1
- prior_prec: float32 [6, 6], replicated, as said below
Outputs:
- grad_mu: float32 [8, 6, 256, 256], P('tile', 'filt')
- grad_rho: float32 [8, 6, 256, 256], P('tile', 'filt')
The draws below stay inside these ranges and needn't reach their ends.
Inputs may be any that keep to these rules, and one draw needn't show every extreme that they name: `intersections`: for tile t and filter f the first counts[t, f] slots name distinct exposures within 2 of t; later slots hold values in the same ranges and are not used. Offsets lie in -128 .. 128 and kernel indices in 0 .. 7. counts[t, f] never exceeds the number of exposures within 2 of tile t. `prior_prec`: Symmetric; each diagonal entry exceeds the sum of the magnitudes of the other entries of its row.
All inputs are finite; a program needn't handle non-finite values.
Results may differ from the reference program's by a relative error of at most 0.00086.
Values may be sent and summed in bfloat16 or wider, within the bound.
No kernel may reach another device: no remote copies, remote signals or barrier semaphores. Data moves between devices by JAX's collectives and lax.ppermute only.
A program may use at most 64 MiB of HBM per device.

```python
import math
import jax
import jax.numpy as jnp
from jax import lax

PIX = 256
FILTERS = 6
NB = 6
NBASIS = 8
HW = 12
K = 3
REACH = 2
TILES = 8
EXPOS = 8
MC = 2


def draw_intersections(key, part):
    window_len = 2 * REACH + 1
    tile_ids = jnp.arange(TILES, dtype=jnp.int32)[:, None, None]
    offsets = jnp.arange(window_len, dtype=jnp.int32)[None, None, :] - REACH
    target = tile_ids + offsets
    outside = (target < 0) | (target >= TILES)
    scores = jax.random.randint(jax.random.fold_in(key, 11), (TILES, FILTERS, window_len), 0, 1 << 20) * window_len
    scores = scores + jnp.arange(window_len, dtype=jnp.int32)[None, None, :]
    scores = scores + outside.astype(jnp.int32) * (1 << 26)
    ranked = jnp.argsort(scores, axis=2, stable=True)[:, :, :K].astype(jnp.int32)
    exposure = jnp.clip(tile_ids + ranked - REACH, 0, TILES - 1)
    shifts = jax.random.randint(jax.random.fold_in(key, 12), (TILES, FILTERS, K, 2), -(PIX // 2), PIX // 2 + 1)
    basis_ids = jax.random.randint(jax.random.fold_in(key, 13), (TILES, FILTERS, K, NB), 0, NBASIS)
    return jnp.concatenate([exposure[..., None], shifts, basis_ids], axis=3).astype(jnp.int32)


def draw_counts(key, part):
    tile_ids = jnp.arange(TILES, dtype=jnp.int32)[:, None]
    in_range = jnp.minimum(tile_ids, REACH) + jnp.minimum(TILES - 1 - tile_ids, REACH) + 1
    chosen = jax.random.randint(jax.random.fold_in(key, 21), (TILES, FILTERS), 1, K + 1)
    chosen = jnp.minimum(chosen, in_range)
    forced = (tile_ids == TILES // 2) & (jnp.arange(FILTERS, dtype=jnp.int32)[None, :] == 0)
    return jnp.where(forced, K, chosen).astype(jnp.int32)


def draw_prior_prec(key, part):
    raw_off = jax.random.uniform(jax.random.fold_in(key, 31), (FILTERS, FILTERS), jnp.float32, -0.25, 0.25)
    diag_values = jax.random.uniform(jax.random.fold_in(key, 32), (FILTERS,), jnp.float32, 1.5, 2.5)
    identity = jnp.eye(FILTERS, dtype=jnp.float32)
    symmetric = 0.5 * (raw_off + raw_off.T) * (1.0 - identity)
    return (symmetric + identity * diag_values[:, None]).astype(jnp.float32)


def steps_of(key, extent, pieces, smallest, largest):
    def one(axis_at, shards_of):
        steps = jax.random.uniform(jax.random.fold_in(jax.random.fold_in(key, 6), axis_at), (shards_of,), jnp.float32, smallest / len(pieces), largest / len(pieces))
        return jnp.repeat(jnp.exp(steps), extent[axis_at] // shards_of).reshape((-1,) + (1,) * (len(extent) - axis_at - 1))

    gain = one(*pieces[0])
    for cut in pieces[1:]:
        gain = gain * one(*cut)
    return gain


def bell_draw(own_key, dims, spread, most, split=(), kind=jnp.bfloat16):
    drawn = jax.random.normal(own_key, dims, jnp.float32) * spread
    if len(split) > 0:
        drawn = steps_of(own_key, dims, split, -0.22, 0.18) * drawn
    return jnp.clip(drawn, min=-most, max=most).astype(kind)


def setup_inputs(seed: int = 0) -> dict:
    seeds = jax.random.split(jax.random.key(seed), 11)
    return {
        "sky_mean": bell_draw(seeds[0], (TILES, FILTERS, PIX, PIX), 1.0, 6.0, ((0, 8), (1, 2)), jnp.float32),
        "sky_log_scale": jnp.clip(-2.5 + 2.0 * jax.random.uniform(seeds[1], (TILES, FILTERS, PIX, PIX), jnp.float32) ** steps_of(seeds[1], (TILES, FILTERS, PIX, PIX), ((0, 8), (1, 2)), -0.2, 0.2), -2.5, -0.5),
        "noise_draw": bell_draw(seeds[2], (MC, TILES, FILTERS, PIX, PIX), 1.0, 5.0, ((0, 2), (1, 8), (2, 2))),
        "observed": bell_draw(seeds[3], (EXPOS, FILTERS, PIX, PIX), 1.0, 6.0, ((0, 8), (1, 2))),
        "inv_var": jnp.clip(jnp.exp(math.log(4.0) - 2.0794415 * jax.random.uniform(seeds[4], (EXPOS, FILTERS, PIX, PIX), jnp.float32) ** steps_of(seeds[4], (EXPOS, FILTERS, PIX, PIX), ((0, 8), (1, 2)), -0.2, 0.2)), 0.5, 4.0).astype(jnp.bfloat16),
        "intersections": draw_intersections(jax.random.fold_in(seeds[10], 71), 0),
        "counts": draw_counts(jax.random.fold_in(seeds[10], 71), 0),
        "kernels": jnp.clip(jax.random.uniform(seeds[7], (NBASIS, 2, 2 * HW + 1), jnp.float32, 0.0, 0.08), 0.0, 0.08),
        "psf_coeffs": jnp.clip(jax.random.uniform(seeds[8], (EXPOS, FILTERS, NB, 3), jnp.float32, -0.5, 1.0), -0.5, 1.0).astype(jnp.bfloat16),
        "prior_prec": draw_prior_prec(jax.random.fold_in(seeds[10], 71), 0),
    }


def build_padded(kernels, tile_side):
    tap_count = kernels.shape[2]
    half_span = (tap_count - 1) // 2
    offsets = jnp.arange(tile_side)[:, None] - jnp.arange(tile_side)[None, :] + half_span
    summed = jnp.zeros((kernels.shape[0], 2, tile_side, tile_side), jnp.float32)
    for tap_id in range(tap_count):
        summed = summed + kernels[:, :, tap_id][:, :, None, None] * (offsets == tap_id).astype(jnp.float32)
    return jnp.pad(summed.astype(jnp.bfloat16), ((0, 0), (0, 0), (tile_side, tile_side), (0, 0)))


def shifted_basis(basis_pad, basis_id, side_id, offset, tile_side):
    starts = (basis_id.astype(jnp.int32), jnp.int32(side_id), (tile_side - offset).astype(jnp.int32), jnp.int32(0))
    return lax.dynamic_slice(basis_pad, starts, (1, 1, tile_side, tile_side))[0, 0]


def weight_map(coeff_row, tile_side):
    centred = (2.0 * jnp.arange(tile_side, dtype=jnp.float32) + 1.0 - tile_side) / tile_side
    coeff_f = coeff_row.astype(jnp.float32)
    return coeff_f[0] + coeff_f[1] * centred[:, None] + coeff_f[2] * centred[None, :]


def contribution(basis_pad, image, slot_entry, coeff_rows, tile_side):
    summed = jnp.zeros((tile_side, tile_side), jnp.float32)
    for component in range(NB):
        basis_id = slot_entry[3 + component]
        rows_matrix = shifted_basis(basis_pad, basis_id, 0, slot_entry[1], tile_side)
        cols_matrix = shifted_basis(basis_pad, basis_id, 1, slot_entry[2], tile_side)
        half_blur = jnp.dot(rows_matrix, image, preferred_element_type=jnp.float32).astype(jnp.bfloat16)
        blurred = lax.dot_general(half_blur, cols_matrix, (((1,), (1,)), ((), ())), preferred_element_type=jnp.float32)
        summed = summed + weight_map(coeff_rows[component], tile_side) * blurred
    return summed.astype(jnp.bfloat16)


def adjoint_term(basis_pad, resid_img, slot_entry, coeff_rows, tile_side):
    summed = jnp.zeros((tile_side, tile_side), jnp.float32)
    for component in range(NB):
        basis_id = slot_entry[3 + component]
        rows_matrix = shifted_basis(basis_pad, basis_id, 0, slot_entry[1], tile_side)
        cols_matrix = shifted_basis(basis_pad, basis_id, 1, slot_entry[2], tile_side)
        weighted = (weight_map(coeff_rows[component], tile_side) * resid_img.astype(jnp.float32)).astype(jnp.bfloat16)
        back_half = lax.dot_general(rows_matrix, weighted, (((0,), (0,)), ((), ())), preferred_element_type=jnp.float32).astype(jnp.bfloat16)
        summed = summed + jnp.dot(back_half, cols_matrix, preferred_element_type=jnp.float32)
    return summed


def reference(sky_mean, sky_log_scale, noise_draw, observed, inv_var, intersections, counts, kernels, psf_coeffs, prior_prec):
    tile_side = sky_mean.shape[2]
    n_tiles = sky_mean.shape[0]
    n_filters = sky_mean.shape[1]
    n_samples = noise_draw.shape[0]
    basis_pad = build_padded(kernels, tile_side)
    scale_map = jnp.exp(sky_log_scale)
    live = (jnp.arange(K, dtype=jnp.int32)[None, None, :] < counts[:, :, None]).astype(jnp.float32)
    filt_col = jnp.arange(n_filters, dtype=jnp.int32)[:, None]
    forward_slots = jax.vmap(contribution, (None, None, 0, 0, None))
    forward_all = jax.vmap(forward_slots, (None, 0, 0, 0, None))
    backward_slots = jax.vmap(adjoint_term, (None, 0, 0, 0, None))
    backward_all = jax.vmap(backward_slots, (None, 0, 0, 0, None))
    tile_ids = jnp.arange(n_tiles, dtype=jnp.int32)
    sum_mean = jnp.zeros(sky_mean.shape, jnp.float32)
    sum_scale = jnp.zeros(sky_mean.shape, jnp.float32)
    for sample_id in range(n_samples):
        eps_float = noise_draw[sample_id].astype(jnp.float32)
        sample = sky_mean + scale_map * eps_float
        sample_b = sample.astype(jnp.bfloat16)

        def forward_tile(predicted, tile_id):
            slot_rows = intersections[tile_id]
            coeffs = psf_coeffs[slot_rows[:, :, 0], filt_col]
            contrib = forward_all(basis_pad, sample_b[tile_id], slot_rows, coeffs, tile_side)
            masked = contrib.astype(jnp.float32) * live[tile_id][:, :, None, None]
            return predicted.at[slot_rows[:, :, 0], filt_col].add(masked), None

        predicted = lax.scan(forward_tile, jnp.zeros(sky_mean.shape, jnp.float32), tile_ids)[0]
        residual = (inv_var.astype(jnp.float32) * (observed.astype(jnp.float32) - predicted)).astype(jnp.bfloat16)

        def adjoint_tile(tile_id):
            slot_rows = intersections[tile_id]
            coeffs = psf_coeffs[slot_rows[:, :, 0], filt_col]
            resid_imgs = residual[slot_rows[:, :, 0], filt_col]
            terms = backward_all(basis_pad, resid_imgs, slot_rows, coeffs, tile_side)
            return jnp.sum(terms * live[tile_id][:, :, None, None], axis=1)

        data_grad = lax.map(adjoint_tile, tile_ids)
        prior_grad = jnp.einsum("fg,tgij->tfij", prior_prec, sample, precision=lax.Precision.HIGHEST)
        sample_grad = data_grad - prior_grad
        sum_mean = sum_mean + sample_grad
        sum_scale = sum_scale + sample_grad * scale_map * eps_float
    return sum_mean / n_samples, sum_scale / n_samples + 1.0
```

```python
import functools

import jax
import jax.numpy as jnp
from jax import lax
from jax.experimental import pallas as pl
from jax.experimental.pallas import tpu as pltpu
from jax.sharding import PartitionSpec as P

NB = 6
K = 3
REACH = 2
HEAD = 3
VMEM_BYTES = 48 * 1024 * 1024
VMEM = pl.BlockSpec(memory_space=pltpu.VMEM)
SMEM = pl.BlockSpec(memory_space=pltpu.SMEM)


def shifted(x, axis, by):
    length = lax.axis_size(axis)
    pairs = [(i, i + by) for i in range(length) if 0 <= i + by < length]
    return lax.ppermute(x, axis, pairs)


def rotated(x, axis, by):
    length = lax.axis_size(axis)
    return lax.ppermute(x, axis, [(i, (i + by) % length) for i in range(length)])


def tap_rows(kernels, side, flip):
    half = (kernels.shape[1] - 1) // 2
    taps = kernels[:, ::-1] if flip else kernels
    zeros = jnp.zeros((kernels.shape[0], side - 2 * half - 1), kernels.dtype)
    return jnp.concatenate([taps[:, half:], zeros, taps[:, :half]], 1)


def build_basis(taps_ref, basis_ref, half):
    count, side = taps_ref.shape[0], taps_ref.shape[1]
    apart = lax.broadcasted_iota(jnp.int32, (side, side), 0) - lax.broadcasted_iota(
        jnp.int32, (side, side), 1
    )
    band = jnp.abs(apart) <= half

    def one(n, carry):
        rows = jnp.broadcast_to(taps_ref[pl.ds(n, 1), :], (side, side))
        turned = pltpu.roll(rows, 0, 1, stride=1, stride_axis=0)
        basis_ref[n] = jnp.where(band, turned, 0.0).astype(jnp.bfloat16)
        return carry

    lax.fori_loop(0, count, one, 0)


def find_slot(inter_ref, counts_ref, tile, expo, filt, sizes):
    tiles, filters, fields = sizes
    inside = (tile >= 0) & (tile < tiles) & (expo >= 0) & (expo < tiles)
    pair = jnp.clip(tile, 0, tiles - 1) * filters + filt
    live = counts_ref[pair]
    base = jnp.int32(0)
    found = jnp.int32(0)
    for q in range(K):
        here = (pair * K + q) * fields
        hit = (q < live) & (inter_ref[here] == expo) & inside
        base = jnp.where(hit, here, base)
        found = jnp.where(hit, 1, found)
    return found, base


def weight(coeff_ref, at, row_centred, col_centred):
    return (coeff_ref[at] + coeff_ref[at + 1] * row_centred) + coeff_ref[at + 2] * col_centred


def centred_axes(side, oy, ox):
    rows = lax.broadcasted_iota(jnp.int32, (side, 1), 0) + oy
    cols = lax.broadcasted_iota(jnp.int32, (1, side), 1) + ox
    return (
        (2 * rows + 1 - side).astype(jnp.float32) / side,
        (2 * cols + 1 - side).astype(jnp.float32) / side,
    )


def diagonal(side, by):
    apart = lax.broadcasted_iota(jnp.int32, (side, side), 1) - lax.broadcasted_iota(
        jnp.int32, (side, side), 0
    )
    return (apart == by).astype(jnp.float32).astype(jnp.bfloat16)


def dot(a, b):
    return jnp.dot(a, b, preferred_element_type=jnp.float32)


def add_contribution(inter_ref, coeff_ref, basis_ref, base, coeff_base, image, pred_ref, f):
    side = image.shape[0]
    kinds = basis_ref.shape[0] // 2
    oy, ox = inter_ref[base + 1], inter_ref[base + 2]
    row_centred, col_centred = centred_axes(side, oy, ox)
    total = jnp.zeros((side, side), jnp.float32)
    for b in range(NB):
        k = inter_ref[base + HEAD + b]
        half_blur = dot(basis_ref[k], image).astype(jnp.bfloat16)
        blurred = dot(half_blur, basis_ref[kinds + k])
        total = total + weight(coeff_ref, coeff_base + 3 * b, row_centred, col_centred) * blurred
    across = dot(total.astype(jnp.bfloat16), diagonal(side, ox)).astype(jnp.bfloat16)
    pred_ref[f] = pred_ref[f] + dot(diagonal(side, -oy), across)


def add_adjoint(inter_ref, coeff_ref, basis_ref, base, coeff_base, image, grad_ref, f):
    side = image.shape[0]
    kinds = basis_ref.shape[0] // 2
    oy, ox = inter_ref[base + 1], inter_ref[base + 2]
    row_centred, col_centred = centred_axes(side, oy, ox)
    across = dot(image, diagonal(side, -ox)).astype(jnp.bfloat16)
    moved = dot(diagonal(side, oy), across)
    total = jnp.zeros((side, side), jnp.float32)
    for b in range(NB):
        k = inter_ref[base + HEAD + b]
        w = weight(coeff_ref, coeff_base + 3 * b, row_centred, col_centred)
        back_half = dot(basis_ref[k], (w * moved).astype(jnp.bfloat16)).astype(jnp.bfloat16)
        total = total + dot(back_half, basis_ref[kinds + k])
    grad_ref[f] = grad_ref[f] + total


def forward_kernel(sizes, half, inter_ref, counts_ref, coeff_ref, taps_ref, *refs):
    window = 2 * REACH + 1
    images = refs[:window]
    observed_ref, inv_ref, resid_ref, basis_ref, pred_ref = refs[window:]
    tiles, filters, fields = sizes
    local, side = observed_ref.shape[0], observed_ref.shape[1]
    expo = lax.axis_index("tile")
    first = lax.axis_index("filt") * local
    build_basis(taps_ref, basis_ref, half)
    pred_ref[...] = jnp.zeros_like(pred_ref)
    for w in range(window):
        tile = expo + w - REACH

        def one(f, carry):
            found, base = find_slot(inter_ref, counts_ref, tile, expo, first + f, sizes)

            @pl.when(found == 1)
            def _():
                coeff_base = (expo * filters + first + f) * NB * 3
                add_contribution(
                    inter_ref, coeff_ref, basis_ref, base, coeff_base, images[w][f], pred_ref, f
                )

            return carry

        lax.fori_loop(0, local, one, 0)
    for f in range(local):
        pred = pred_ref[f]
        resid = inv_ref[f].astype(jnp.float32) * (observed_ref[f].astype(jnp.float32) - pred)
        resid_ref[f] = resid.astype(jnp.bfloat16)


def backward_kernel(
    sizes, half, inter_ref, counts_ref, coeff_ref, prec_ref, taps_ref, sample_ref, *refs
):
    window = 2 * REACH + 1
    images = refs[:window]
    others = refs[window:-2]
    grad_ref, basis_ref = refs[-2:]
    tiles, filters, fields = sizes
    local, side = sample_ref.shape[0], sample_ref.shape[1]
    tile = lax.axis_index("tile")
    part = lax.axis_index("filt")
    parts = filters // local
    first = part * local
    build_basis(taps_ref, basis_ref, half)
    for f in range(local):
        prior = jnp.zeros((side, side), jnp.float32)
        row = (first + f) * filters
        for g in range(local):
            prior = prior + prec_ref[row + first + g] * sample_ref[g]
        for r in range(1, parts):
            source = lax.rem(part + parts - r, parts) * local
            for g in range(local):
                prior = prior + prec_ref[row + source + g] * others[r - 1][g].astype(jnp.float32)
        grad_ref[f] = -prior
    for w in range(window):
        expo = tile + w - REACH

        def one(f, carry):
            found, base = find_slot(inter_ref, counts_ref, tile, expo, first + f, sizes)

            @pl.when(found == 1)
            def _():
                coeff_base = (expo * filters + first + f) * NB * 3
                add_adjoint(
                    inter_ref, coeff_ref, basis_ref, base, coeff_base, images[w][f], grad_ref, f
                )

            return carry

        lax.fori_loop(0, local, one, 0)


def body(
    sky_mean,
    sky_log_scale,
    noise_draw,
    observed,
    inv_var,
    intersections,
    counts,
    kernels,
    psf_coeffs,
    prior_prec,
):
    side = sky_mean.shape[2]
    local = sky_mean.shape[1]
    tiles, filters = counts.shape
    sizes = (tiles, filters, intersections.shape[3])
    half = (kernels.shape[2] - 1) // 2
    kinds = kernels.shape[0]
    moves = [amount for amount in range(-REACH, REACH + 1) if amount != 0]
    samples = lax.axis_size("mc")
    parts = lax.axis_size("filt")

    scale_map = jnp.exp(sky_log_scale[0])
    noise = noise_draw[0, 0]
    eps_float = noise.astype(jnp.float32)
    sample = sky_mean[0] + scale_map * eps_float
    sample_b = sample.astype(jnp.bfloat16)
    inter_flat = intersections.reshape(-1)
    counts_flat = counts.reshape(-1)
    coeff_flat = psf_coeffs.astype(jnp.float32).reshape(-1)
    prec_flat = prior_prec.reshape(-1)
    rows_plain = tap_rows(kernels[:, 0], side, True)
    rows_trans = tap_rows(kernels[:, 0], side, False)
    cols_plain = tap_rows(kernels[:, 1], side, True)
    cols_trans = tap_rows(kernels[:, 1], side, False)
    taps_forward = jnp.concatenate([rows_plain, cols_trans], 0)
    taps_backward = jnp.concatenate([rows_trans, cols_plain], 0)

    def cost(slots):
        return pl.CostEstimate(
            flops=slots * NB * 4 * side**3, bytes_accessed=8 * local * side * side, transcendentals=0
        )

    params = pltpu.CompilerParams(vmem_limit_bytes=VMEM_BYTES)
    near = [shifted(sample_b, "tile", REACH - w) if w != REACH else sample_b for w in range(2 * REACH + 1)]
    other_samples = [rotated(sample_b, "filt", r) for r in range(1, parts)]
    other_noise = [rotated(noise, "mc", r) for r in range(1, samples)]
    residual = pl.pallas_call(
        functools.partial(forward_kernel, sizes, half),
        out_shape=jax.ShapeDtypeStruct((local, side, side), jnp.bfloat16),
        in_specs=[SMEM] * 3 + [VMEM] * (1 + len(near) + 2),
        out_specs=VMEM,
        scratch_shapes=[
            pltpu.VMEM((2 * kinds, side, side), jnp.bfloat16),
            pltpu.VMEM((local, side, side), jnp.float32),
        ],
        compiler_params=params,
        cost_estimate=cost(3 * local),
        name="forward",
    )(inter_flat, counts_flat, coeff_flat, taps_forward, *near, observed[0], inv_var[0])
    near_resid = [
        shifted(residual, "tile", REACH - w) if w != REACH else residual for w in range(2 * REACH + 1)
    ]
    sample_grad = pl.pallas_call(
        functools.partial(backward_kernel, sizes, half),
        out_shape=jax.ShapeDtypeStruct((local, side, side), jnp.float32),
        in_specs=[SMEM] * 4 + [VMEM] * (2 + len(near_resid) + len(other_samples)),
        out_specs=VMEM,
        scratch_shapes=[
            pltpu.VMEM((2 * kinds, side, side), jnp.bfloat16),
        ],
        compiler_params=params,
        cost_estimate=cost(3 * local),
        name="backward",
    )(
        inter_flat,
        counts_flat,
        coeff_flat,
        prec_flat,
        taps_backward,
        sample,
        *near_resid,
        *other_samples,
    )
    mean_sum = sample_grad
    scale_sum = sample_grad * scale_map * eps_float
    for r in range(1, samples):
        other_grad = rotated(sample_grad, "mc", r)
        mean_sum = mean_sum + other_grad
        scale_sum = scale_sum + other_grad * scale_map * other_noise[r - 1].astype(jnp.float32)
    return ((mean_sum / samples)[None], (scale_sum / samples + 1.0)[None])


def solution(mesh):
    placed = (
        P("tile", "filt", None, None),
        P("tile", "filt", None, None),
        P("mc", "tile", "filt", None, None),
        P("tile", "filt", None, None),
        P("tile", "filt", None, None),
        P(),
        P(),
        P(),
        P(),
        P(),
    )
    return jax.shard_map(
        body,
        mesh=mesh,
        in_specs=placed,
        out_specs=(P("tile", "filt", None, None), P("tile", "filt", None, None)),
        check_vma=False,
    )
```

```python
import functools

import jax
import jax.numpy as jnp
from jax import lax
from jax.experimental import pallas as pl
from jax.experimental.pallas import tpu as pltpu
from jax.sharding import PartitionSpec as P

NB = 6
K = 3
REACH = 2
HEAD = 3
VMEM_BYTES = 48 * 1024 * 1024
VMEM = pl.BlockSpec(memory_space=pltpu.VMEM)
SMEM = pl.BlockSpec(memory_space=pltpu.SMEM)


def shifted(x, axis, by):
    length = lax.axis_size(axis)
    pairs = [(i, i + by) for i in range(length) if 0 <= i + by < length]
    return lax.ppermute(x, axis, pairs)


def rotated(x, axis, by):
    length = lax.axis_size(axis)
    return lax.ppermute(x, axis, [(i, (i + by) % length) for i in range(length)])


def tap_rows(kernels, side, flip):
    half = (kernels.shape[1] - 1) // 2
    taps = kernels[:, ::-1] if flip else kernels
    zeros = jnp.zeros((kernels.shape[0], side - 2 * half - 1), kernels.dtype)
    return jnp.concatenate([taps[:, half:], zeros, taps[:, :half]], 1)


def build_basis(taps_ref, basis_ref, half):
    count, side = taps_ref.shape[0], taps_ref.shape[1]
    apart = lax.broadcasted_iota(jnp.int32, (side, side), 0) - lax.broadcasted_iota(
        jnp.int32, (side, side), 1
    )
    band = jnp.abs(apart) <= half

    def one(n, carry):
        rows = jnp.broadcast_to(taps_ref[pl.ds(n, 1), :], (side, side))
        turned = pltpu.roll(rows, 0, 1, stride=1, stride_axis=0)
        basis_ref[n] = jnp.where(band, turned, 0.0).astype(jnp.bfloat16)
        return carry

    lax.fori_loop(0, count, one, 0)


def find_slot(inter_ref, counts_ref, tile, expo, filt, sizes):
    tiles, filters, fields = sizes
    inside = (tile >= 0) & (tile < tiles) & (expo >= 0) & (expo < tiles)
    pair = jnp.clip(tile, 0, tiles - 1) * filters + filt
    live = counts_ref[pair]
    base = jnp.int32(0)
    found = jnp.int32(0)
    for q in range(K):
        here = (pair * K + q) * fields
        hit = (q < live) & (inter_ref[here] == expo) & inside
        base = jnp.where(hit, here, base)
        found = jnp.where(hit, 1, found)
    return found, base


def weight(coeff_ref, at, row_centred, col_centred):
    return (coeff_ref[at] + coeff_ref[at + 1] * row_centred) + coeff_ref[at + 2] * col_centred


def centred_axes(side, oy, ox):
    rows = lax.broadcasted_iota(jnp.int32, (side, 1), 0) + oy
    cols = lax.broadcasted_iota(jnp.int32, (1, side), 1) + ox
    return (
        (2 * rows + 1 - side).astype(jnp.float32) / side,
        (2 * cols + 1 - side).astype(jnp.float32) / side,
    )


def diagonal(side, by):
    apart = lax.broadcasted_iota(jnp.int32, (side, side), 1) - lax.broadcasted_iota(
        jnp.int32, (side, side), 0
    )
    return (apart == by).astype(jnp.float32).astype(jnp.bfloat16)


def dot(a, b):
    return jnp.dot(a, b, preferred_element_type=jnp.float32)


def add_contribution(inter_ref, coeff_ref, basis_ref, base, coeff_base, image, pred_ref, f):
    side = image.shape[0]
    kinds = basis_ref.shape[0] // 2
    oy, ox = inter_ref[base + 1], inter_ref[base + 2]
    row_centred, col_centred = centred_axes(side, oy, ox)
    total = jnp.zeros((side, side), jnp.float32)
    for b in range(NB):
        k = inter_ref[base + HEAD + b]
        half_blur = dot(basis_ref[k], image).astype(jnp.bfloat16)
        blurred = dot(half_blur, basis_ref[kinds + k])
        total = total + weight(coeff_ref, coeff_base + 3 * b, row_centred, col_centred) * blurred
    across = dot(total.astype(jnp.bfloat16), diagonal(side, ox)).astype(jnp.bfloat16)
    pred_ref[f] = pred_ref[f] + dot(diagonal(side, -oy), across)


def add_adjoint(inter_ref, coeff_ref, basis_ref, base, coeff_base, image, grad_ref, f):
    side = image.shape[0]
    kinds = basis_ref.shape[0] // 2
    oy, ox = inter_ref[base + 1], inter_ref[base + 2]
    row_centred, col_centred = centred_axes(side, oy, ox)
    across = dot(image, diagonal(side, -ox)).astype(jnp.bfloat16)
    moved = dot(diagonal(side, oy), across)
    total = jnp.zeros((side, side), jnp.float32)
    for b in range(NB):
        k = inter_ref[base + HEAD + b]
        w = weight(coeff_ref, coeff_base + 3 * b, row_centred, col_centred)
        back_half = dot(basis_ref[k], (w * moved).astype(jnp.bfloat16)).astype(jnp.bfloat16)
        total = total + dot(back_half, basis_ref[kinds + k])
    grad_ref[f] = grad_ref[f] + total


def source_of(own, move):
    distance, parity = move
    return own + jnp.where(lax.rem(own // distance, 2) == parity, distance, -distance)


def flipped(x, axis, move):
    distance, parity = move
    length = lax.axis_size(axis)
    firsts = [i for i in range(length - distance) if (i // distance) % 2 == parity]
    pairs = [(i, i + distance) for i in firsts] + [(i + distance, i) for i in firsts]
    return lax.ppermute(x, axis, pairs)


def forward_slots(sizes, move, inter_ref, counts_ref, coeff_ref, basis_ref, image_ref, pred_ref):
    tiles, filters, fields = sizes
    local = image_ref.shape[0]
    expo = lax.axis_index("tile")
    tile = expo if move is None else source_of(expo, move)
    first = lax.axis_index("filt") * local

    def one(f, carry):
        found, base = find_slot(inter_ref, counts_ref, tile, expo, first + f, sizes)

        @pl.when(found == 1)
        def _():
            coeff_base = (expo * filters + first + f) * NB * 3
            add_contribution(
                inter_ref, coeff_ref, basis_ref, base, coeff_base, image_ref[f], pred_ref, f
            )

        return carry

    lax.fori_loop(0, local, one, 0)


def backward_slots(sizes, move, inter_ref, counts_ref, coeff_ref, basis_ref, image_ref, grad_ref):
    tiles, filters, fields = sizes
    local = image_ref.shape[0]
    tile = lax.axis_index("tile")
    expo = tile if move is None else source_of(tile, move)
    first = lax.axis_index("filt") * local

    def one(f, carry):
        found, base = find_slot(inter_ref, counts_ref, tile, expo, first + f, sizes)

        @pl.when(found == 1)
        def _():
            coeff_base = (expo * filters + first + f) * NB * 3
            add_adjoint(
                inter_ref, coeff_ref, basis_ref, base, coeff_base, image_ref[f], grad_ref, f
            )

        return carry

    lax.fori_loop(0, local, one, 0)


def forward_own(sizes, half, inter_ref, counts_ref, coeff_ref, taps_ref, image_ref, *outs):
    pred_ref, basis_ref = outs
    build_basis(taps_ref, basis_ref, half)
    pred_ref[...] = jnp.zeros_like(pred_ref)
    forward_slots(sizes, None, inter_ref, counts_ref, coeff_ref, basis_ref, image_ref, pred_ref)


def forward_next(
    sizes, move, inter_ref, counts_ref, coeff_ref, basis_ref, image_ref, before_ref, pred_ref
):
    del before_ref
    forward_slots(sizes, move, inter_ref, counts_ref, coeff_ref, basis_ref, image_ref, pred_ref)


def forward_last(
    sizes,
    move,
    inter_ref,
    counts_ref,
    coeff_ref,
    basis_ref,
    image_ref,
    before_ref,
    observed_ref,
    inv_ref,
    pred_ref,
    resid_ref,
):
    del before_ref
    forward_slots(sizes, move, inter_ref, counts_ref, coeff_ref, basis_ref, image_ref, pred_ref)
    for f in range(observed_ref.shape[0]):
        gap = observed_ref[f].astype(jnp.float32) - pred_ref[f]
        resid_ref[f] = (inv_ref[f].astype(jnp.float32) * gap).astype(jnp.bfloat16)


def backward_own(
    sizes,
    half,
    samples,
    inter_ref,
    counts_ref,
    coeff_ref,
    prec_ref,
    taps_ref,
    image_ref,
    sample_ref,
    scale_ref,
    *refs,
):
    noises, refs = refs[:samples], refs[samples:]
    turns, refs = refs[-samples:], refs[:-samples]
    others, (grad_ref, basis_ref) = refs[:-2], refs[-2:]
    tiles, filters, fields = sizes
    local, side = sample_ref.shape[0], sample_ref.shape[1]
    part = lax.axis_index("filt")
    parts = filters // local
    first = part * local
    build_basis(taps_ref, basis_ref, half)
    for noise_ref, turn_ref in zip(noises, turns):
        turn_ref[...] = scale_ref[...] * noise_ref[...].astype(jnp.float32)
    for f in range(local):
        prior = jnp.zeros((side, side), jnp.float32)
        row = (first + f) * filters
        for g in range(local):
            prior = prior + prec_ref[row + first + g] * sample_ref[g]
        for r in range(1, parts):
            source = lax.rem(part + parts - r, parts) * local
            for g in range(local):
                prior = prior + prec_ref[row + source + g] * others[r - 1][g].astype(jnp.float32)
        grad_ref[f] = -prior
    backward_slots(sizes, None, inter_ref, counts_ref, coeff_ref, basis_ref, image_ref, grad_ref)


def backward_next(
    sizes, move, inter_ref, counts_ref, coeff_ref, basis_ref, image_ref, before_ref, grad_ref
):
    del before_ref
    backward_slots(sizes, move, inter_ref, counts_ref, coeff_ref, basis_ref, image_ref, grad_ref)


def body(
    sky_mean,
    sky_log_scale,
    noise_draw,
    observed,
    inv_var,
    intersections,
    counts,
    kernels,
    psf_coeffs,
    prior_prec,
):
    side = sky_mean.shape[2]
    local = sky_mean.shape[1]
    tiles, filters = counts.shape
    sizes = (tiles, filters, intersections.shape[3])
    half = (kernels.shape[2] - 1) // 2
    kinds = kernels.shape[0]
    started = [(d, parity) for d in range(1, REACH + 1) for parity in (0, 1)]
    used = [(1, 0)] + [m for m in started if m[0] > 1] + [(1, 1)]
    samples = lax.axis_size("mc")
    parts = lax.axis_size("filt")

    scale_map = jnp.exp(sky_log_scale[0])
    noise = noise_draw[0, 0]
    eps_float = noise.astype(jnp.float32)
    sample = sky_mean[0] + scale_map * eps_float
    sample_b = sample.astype(jnp.bfloat16)
    inter_flat = intersections.reshape(-1)
    counts_flat = counts.reshape(-1)
    coeff_flat = psf_coeffs.astype(jnp.float32).reshape(-1)
    prec_flat = prior_prec.reshape(-1)
    tables = (inter_flat, counts_flat, coeff_flat)
    rows_plain = tap_rows(kernels[:, 0], side, True)
    rows_trans = tap_rows(kernels[:, 0], side, False)
    cols_plain = tap_rows(kernels[:, 1], side, True)
    cols_trans = tap_rows(kernels[:, 1], side, False)
    taps_forward = jnp.concatenate([rows_plain, cols_trans], 0)
    taps_backward = jnp.concatenate([rows_trans, cols_plain], 0)

    image_f32 = jax.ShapeDtypeStruct((local, side, side), jnp.float32)
    image_b16 = jax.ShapeDtypeStruct((local, side, side), jnp.bfloat16)
    basis_type = jax.ShapeDtypeStruct((2 * kinds, side, side), jnp.bfloat16)
    cost = pl.CostEstimate(
        flops=2 * NB * 4 * side**3, bytes_accessed=8 * local * side * side, transcendentals=0
    )

    def call(kernel, name, outs, smem, vmem, aliases={}):
        return pl.pallas_call(
            kernel,
            out_shape=outs,
            in_specs=[SMEM] * len(smem) + [VMEM] * len(vmem),
            out_specs=[VMEM] * len(outs),
            input_output_aliases=aliases,
            compiler_params=pltpu.CompilerParams(vmem_limit_bytes=VMEM_BYTES),
            cost_estimate=cost,
            name=name,
        )(*smem, *vmem)

    near = {move: flipped(sample_b, "tile", move) for move in started}
    other_samples = [rotated(sample_b, "filt", r) for r in range(1, parts)]
    other_noise = [rotated(noise, "mc", r) for r in range(1, samples)]
    pred, basis = call(
        functools.partial(forward_own, sizes, half),
        "forward_own",
        [image_f32, basis_type],
        tables,
        (taps_forward, sample_b),
    )
    for move in used[:-1]:
        (pred,) = call(
            functools.partial(forward_next, sizes, move),
            f"forward_{move[0]}_{move[1]}",
            [image_f32],
            tables,
            (basis, near[move], pred),
            {len(tables) + 2: 0},
        )
    _, residual = call(
        functools.partial(forward_last, sizes, used[-1]),
        "forward_last",
        [image_f32, image_b16],
        tables,
        (basis, near[used[-1]], pred, observed[0], inv_var[0]),
        {len(tables) + 2: 0},
    )
    near_resid = {move: flipped(residual, "tile", move) for move in started}
    grad, basis, turn, *other_turns = call(
        functools.partial(backward_own, sizes, half, samples),
        "backward_own",
        [image_f32, basis_type] + [image_f32] * samples,
        tables + (prec_flat,),
        (taps_backward, residual, sample, scale_map, noise, *other_noise, *other_samples),
    )
    for move in used:
        (grad,) = call(
            functools.partial(backward_next, sizes, move),
            f"backward_{move[0]}_{move[1]}",
            [image_f32],
            tables,
            (basis, near_resid[move], grad),
            {len(tables) + 2: 0},
        )
    mean_sum = grad
    scale_sum = grad * turn
    for r in range(1, samples):
        other_grad = rotated(grad, "mc", r)
        mean_sum = mean_sum + other_grad
        scale_sum = scale_sum + other_grad * other_turns[r - 1]
    return ((mean_sum / samples)[None], (scale_sum / samples + 1.0)[None])

def solution(mesh):
    placed = (
        P("tile", "filt", None, None),
        P("tile", "filt", None, None),
        P("mc", "tile", "filt", None, None),
        P("tile", "filt", None, None),
        P("tile", "filt", None, None),
        P(),
        P(),
        P(),
        P(),
        P(),
    )
    return jax.shard_map(
        body,
        mesh=mesh,
        in_specs=placed,
        out_specs=(P("tile", "filt", None, None), P("tile", "filt", None, None)),
        check_vma=False,
    )
```

```python
import functools

import jax
import jax.numpy as jnp
from jax import lax
from jax.experimental import pallas as pl
from jax.experimental.pallas import tpu as pltpu
from jax.sharding import PartitionSpec as P

NB = 6
K = 3
REACH = 2
HEAD = 3
VMEM_BYTES = 16 * 1024 * 1024
VMEM = pl.BlockSpec(memory_space=pltpu.VMEM)
SMEM = pl.BlockSpec(memory_space=pltpu.SMEM)


def shifted(x, axis, by):
    length = lax.axis_size(axis)
    pairs = [(i, i + by) for i in range(length) if 0 <= i + by < length]
    return lax.ppermute(x, axis, pairs)


def rotated(x, axis, by):
    length = lax.axis_size(axis)
    return lax.ppermute(x, axis, [(i, (i + by) % length) for i in range(length)])


def build_basis(taps_ref, lines_ref, basis_ref, adjoint):
    kinds, side = basis_ref.shape[0] // 2, basis_ref.shape[1]
    count = taps_ref.shape[1]
    half = (count - 1) // 2
    taps = taps_ref[...].astype(jnp.bfloat16)
    tap = lax.broadcasted_iota(jnp.int32, (count, side), 0)
    lane = lax.broadcasted_iota(jnp.int32, (count, side), 1)
    lane = jnp.where(lane < side // 2, lane, lane - side)
    plain = (lane == half - tap).astype(jnp.float32).astype(jnp.bfloat16)
    turned = (lane == tap - half).astype(jnp.float32).astype(jnp.bfloat16)
    lines_ref[0] = dot(taps, turned if adjoint else plain)
    lines_ref[1] = dot(taps, plain if adjoint else turned)
    apart = lax.broadcasted_iota(jnp.int32, (side, side), 0) - lax.broadcasted_iota(
        jnp.int32, (side, side), 1
    )
    band = jnp.abs(apart) <= half

    def one(k, carry):
        for c in range(2):
            line = jnp.broadcast_to(lines_ref[c, pl.ds(2 * k + c, 1), :], (side, side))
            rows = pltpu.roll(line, 0, 1, stride=1, stride_axis=0)
            basis_ref[c * kinds + k] = jnp.where(band, rows, 0.0).astype(jnp.bfloat16)
        return carry

    lax.fori_loop(0, kinds, one, 0)


def find_slot(inter_ref, counts_ref, tile, expo, filt, sizes):
    tiles, filters, fields = sizes
    inside = (tile >= 0) & (tile < tiles) & (expo >= 0) & (expo < tiles)
    pair = jnp.clip(tile, 0, tiles - 1) * filters + filt
    live = counts_ref[pair]
    base = jnp.int32(0)
    found = jnp.int32(0)
    for q in range(K):
        here = (pair * K + q) * fields
        hit = (q < live) & (inter_ref[here] == expo) & inside
        base = jnp.where(hit, here, base)
        found = jnp.where(hit, 1, found)
    return found, base


def weight(coeff_ref, at, row_centred, col_centred):
    return (coeff_ref[at] + coeff_ref[at + 1] * row_centred) + coeff_ref[at + 2] * col_centred


def centred_axes(side, oy, ox):
    rows = lax.broadcasted_iota(jnp.int32, (side, 1), 0) + oy
    cols = lax.broadcasted_iota(jnp.int32, (1, side), 1) + ox
    return (
        (2 * rows + 1 - side).astype(jnp.float32) / side,
        (2 * cols + 1 - side).astype(jnp.float32) / side,
    )


def diagonal(side, by):
    apart = lax.broadcasted_iota(jnp.int32, (side, side), 1) - lax.broadcasted_iota(
        jnp.int32, (side, side), 0
    )
    return (apart == by).astype(jnp.float32).astype(jnp.bfloat16)


def dot(a, b):
    return jnp.dot(a, b, preferred_element_type=jnp.float32)


def settle_contribution(image, oy, ox, pred_ref, f):
    side = image.shape[0]
    across = dot(image, diagonal(side, ox)).astype(jnp.bfloat16)
    pred_ref[f] = pred_ref[f] + dot(diagonal(side, -oy), across)


def contribution(inter_ref, coeff_ref, basis_ref, base, coeff_base, image):
    side = image.shape[0]
    kinds = basis_ref.shape[0] // 2
    row_centred, col_centred = centred_axes(side, inter_ref[base + 1], inter_ref[base + 2])
    total = jnp.zeros((side, side), jnp.float32)
    for b in range(NB):
        k = inter_ref[base + HEAD + b]
        half_blur = dot(basis_ref[k], image).astype(jnp.bfloat16)
        blurred = dot(half_blur, basis_ref[kinds + k])
        total = total + weight(coeff_ref, coeff_base + 3 * b, row_centred, col_centred) * blurred
    return total.astype(jnp.bfloat16)


def bring_residual(image, oy, ox):
    side = image.shape[0]
    across = dot(image, diagonal(side, -ox)).astype(jnp.bfloat16)
    return dot(diagonal(side, oy), across)


def adjoint_term(inter_ref, coeff_ref, basis_ref, base, coeff_base, moved):
    side = moved.shape[0]
    kinds = basis_ref.shape[0] // 2
    row_centred, col_centred = centred_axes(side, inter_ref[base + 1], inter_ref[base + 2])
    total = jnp.zeros((side, side), jnp.float32)
    for b in range(NB):
        k = inter_ref[base + HEAD + b]
        w = weight(coeff_ref, coeff_base + 3 * b, row_centred, col_centred)
        back_half = dot(basis_ref[k], (w * moved).astype(jnp.bfloat16)).astype(jnp.bfloat16)
        total = total + dot(back_half, basis_ref[kinds + k])
    return total


def source_of(own, move):
    distance, parity = move
    return own + jnp.where(lax.rem(own // distance, 2) == parity, distance, -distance)


def flipped(x, axis, move):
    distance, parity = move
    length = lax.axis_size(axis)
    firsts = [i for i in range(length - distance) if (i // distance) % 2 == parity]
    pairs = [(i, i + distance) for i in firsts] + [(i + distance, i) for i in firsts]
    return lax.ppermute(x, axis, pairs)


def gather_live(sizes, moves, backward, inter_ref, counts_ref, images, list_ref, held_ref):
    tiles, filters, fields = sizes
    local = images[0].shape[0]
    own = lax.axis_index("tile")
    first = lax.axis_index("filt") * local
    live = jnp.int32(0)
    for move, image_ref in zip(moves, images):
        far = own if move is None else source_of(own, move)
        tile, expo = (own, far) if backward else (far, own)
        for f in range(local):
            found, base = find_slot(inter_ref, counts_ref, tile, expo, first + f, sizes)

            @pl.when(found == 1)
            def _():
                list_ref[0, live] = f
                list_ref[1, live] = base
                list_ref[2, live] = (expo * filters + first + f) * NB * 3
                held_ref[live] = image_ref[f]

            live = live + found
    return live


def forward_slots(
    sizes, moves, inter_ref, counts_ref, coeff_ref, basis_ref, images, pred_ref, scratch
):
    list_ref, held_ref, ready_ref = scratch
    live = gather_live(
        sizes, moves, False, inter_ref, counts_ref, images, list_ref, held_ref
    )

    @pl.when(live > 0)
    def _():
        def blur(n):
            ready_ref[...] = contribution(
                inter_ref, coeff_ref, basis_ref, list_ref[1, n], list_ref[2, n], held_ref[n]
            )

        def settle(n):
            base = list_ref[1, n]
            settle_contribution(
                ready_ref[...], inter_ref[base + 1], inter_ref[base + 2], pred_ref, list_ref[0, n]
            )

        def one(n, carry):
            settle(n - 1)
            blur(n)
            return carry

        blur(0)
        lax.fori_loop(1, live, one, 0)
        settle(live - 1)


def backward_slots(
    sizes, moves, inter_ref, counts_ref, coeff_ref, basis_ref, images, grad_ref, scratch
):
    list_ref, held_ref, ready_ref = scratch
    live = gather_live(
        sizes, moves, True, inter_ref, counts_ref, images, list_ref, held_ref
    )

    @pl.when(live > 0)
    def _():
        def bring(n):
            base = list_ref[1, n]
            return bring_residual(held_ref[n], inter_ref[base + 1], inter_ref[base + 2])

        def take(n):
            f = list_ref[0, n]
            grad_ref[f] = grad_ref[f] + adjoint_term(
                inter_ref, coeff_ref, basis_ref, list_ref[1, n], list_ref[2, n], ready_ref[...]
            )

        def one(n, carry):
            following = bring(n)
            take(n - 1)
            ready_ref[...] = following
            return carry

        ready_ref[...] = bring(0)
        lax.fori_loop(1, live, one, 0)
        take(live - 1)


def forward_own(sizes, inter_ref, counts_ref, coeff_ref, taps_ref, image_ref, *refs):
    pred_ref, basis_ref, lines_ref, *scratch = refs
    build_basis(taps_ref, lines_ref, basis_ref, False)
    pred_ref[...] = jnp.zeros_like(pred_ref)
    forward_slots(
        sizes, [None], inter_ref, counts_ref, coeff_ref, basis_ref, [image_ref], pred_ref, scratch
    )


def forward_next(sizes, moves, inter_ref, counts_ref, coeff_ref, basis_ref, *refs):
    images, (before_ref, pred_ref, *scratch) = refs[: len(moves)], refs[len(moves) :]
    del before_ref
    forward_slots(
        sizes, moves, inter_ref, counts_ref, coeff_ref, basis_ref, images, pred_ref, scratch
    )


def forward_last(sizes, moves, inter_ref, counts_ref, coeff_ref, basis_ref, *refs):
    images, refs = refs[: len(moves)], refs[len(moves) :]
    before_ref, observed_ref, inv_ref, pred_ref, resid_ref, *scratch = refs
    del before_ref
    forward_slots(
        sizes, moves, inter_ref, counts_ref, coeff_ref, basis_ref, images, pred_ref, scratch
    )
    for f in range(observed_ref.shape[0]):
        gap = observed_ref[f].astype(jnp.float32) - pred_ref[f]
        resid_ref[f] = (inv_ref[f].astype(jnp.float32) * gap).astype(jnp.bfloat16)


def backward_own(
    sizes,
    samples,
    inter_ref,
    counts_ref,
    coeff_ref,
    prec_ref,
    taps_ref,
    image_ref,
    sample_ref,
    scale_ref,
    *refs,
):
    tiles, filters, fields = sizes
    local, side = sample_ref.shape[0], sample_ref.shape[1]
    part = lax.axis_index("filt")
    parts = filters // local
    first = part * local
    noises, refs = refs[:samples], refs[samples:]
    others, refs = refs[: parts - 1], refs[parts - 1 :]
    grad_ref, basis_ref, *refs = refs
    turns, (lines_ref, *scratch) = refs[:samples], refs[samples:]
    build_basis(taps_ref, lines_ref, basis_ref, True)
    for noise_ref, turn_ref in zip(noises, turns):
        turn_ref[...] = scale_ref[...] * noise_ref[...].astype(jnp.float32)
    for f in range(local):
        prior = jnp.zeros((side, side), jnp.float32)
        for g in range(local):
            prior = prior + prec_ref[first + f, first + g] * sample_ref[g]
        for r in range(1, parts):
            source = lax.rem(part + parts - r, parts) * local
            for g in range(local):
                far = others[r - 1][g].astype(jnp.float32)
                prior = prior + prec_ref[first + f, source + g] * far
        grad_ref[f] = -prior
    backward_slots(
        sizes, [None], inter_ref, counts_ref, coeff_ref, basis_ref, [image_ref], grad_ref, scratch
    )


def backward_next(sizes, moves, inter_ref, counts_ref, coeff_ref, basis_ref, *refs):
    images, (before_ref, grad_ref, *scratch) = refs[: len(moves)], refs[len(moves) :]
    del before_ref
    backward_slots(
        sizes, moves, inter_ref, counts_ref, coeff_ref, basis_ref, images, grad_ref, scratch
    )


def body(
    sky_mean,
    sky_log_scale,
    noise_draw,
    observed,
    inv_var,
    intersections,
    counts,
    kernels,
    psf_coeffs,
    prior_prec,
):
    side = sky_mean.shape[2]
    local = sky_mean.shape[1]
    tiles, filters = counts.shape
    sizes = (tiles, filters, intersections.shape[3])
    kinds = kernels.shape[0]
    started = [(d, parity) for d in range(1, REACH + 1) for parity in (0, 1)]
    last = (1, 1)
    early = [move for move in started if move != last]
    samples = lax.axis_size("mc")
    parts = lax.axis_size("filt")

    scale_map = jnp.exp(sky_log_scale[0])
    noise = noise_draw[0, 0]
    eps_float = noise.astype(jnp.float32)
    sample = sky_mean[0] + scale_map * eps_float
    sample_b = sample.astype(jnp.bfloat16)
    inter_flat = intersections.reshape(-1)
    counts_flat = counts.reshape(-1)
    coeff_flat = psf_coeffs.astype(jnp.float32).reshape(-1)
    tables = (inter_flat, counts_flat, coeff_flat)
    taps = kernels.reshape(2 * kinds, kernels.shape[2])

    image_f32 = jax.ShapeDtypeStruct((local, side, side), jnp.float32)
    image_b16 = jax.ShapeDtypeStruct((local, side, side), jnp.bfloat16)
    basis_type = jax.ShapeDtypeStruct((2 * kinds, side, side), jnp.bfloat16)
    cost = pl.CostEstimate(
        flops=2 * NB * 4 * side**3, bytes_accessed=8 * local * side * side, transcendentals=0
    )

    lines = pltpu.VMEM((2, 2 * kinds, side), jnp.float32)

    def slot_scratch(groups, ready):
        return [
            pltpu.SMEM((3, groups * local), jnp.int32),
            pltpu.VMEM((groups * local, side, side), jnp.bfloat16),
            pltpu.VMEM((side, side), ready),
        ]

    def call(kernel, name, outs, smem, vmem, scratch, aliases={}):
        return pl.pallas_call(
            kernel,
            out_shape=outs,
            in_specs=[SMEM] * len(smem) + [VMEM] * len(vmem),
            out_specs=[VMEM] * len(outs),
            scratch_shapes=scratch,
            input_output_aliases=aliases,
            compiler_params=pltpu.CompilerParams(vmem_limit_bytes=VMEM_BYTES),
            cost_estimate=cost,
            name=name,
        )(*smem, *vmem)

    near = {move: flipped(sample_b, "tile", move) for move in started}
    other_samples = [rotated(sample_b, "filt", r) for r in range(1, parts)]
    other_noise = [rotated(noise, "mc", r) for r in range(1, samples)]
    pred, basis = call(
        functools.partial(forward_own, sizes),
        "forward_own",
        [image_f32, basis_type],
        tables,
        (taps, sample_b),
        [lines] + slot_scratch(1, jnp.bfloat16),
    )
    (pred,) = call(
        functools.partial(forward_next, sizes, early),
        "forward_next",
        [image_f32],
        tables,
        (basis, *[near[move] for move in early], pred),
        slot_scratch(len(early), jnp.bfloat16),
        {len(tables) + 1 + len(early): 0},
    )
    _, residual = call(
        functools.partial(forward_last, sizes, [last]),
        "forward_last",
        [image_f32, image_b16],
        tables,
        (basis, near[last], pred, observed[0], inv_var[0]),
        slot_scratch(1, jnp.bfloat16),
        {len(tables) + 2: 0},
    )
    near_resid = {move: flipped(residual, "tile", move) for move in started}
    grad, basis, turn, *other_turns = call(
        functools.partial(backward_own, sizes, samples),
        "backward_own",
        [image_f32, basis_type] + [image_f32] * samples,
        tables + (prior_prec,),
        (taps, residual, sample, scale_map, noise, *other_noise, *other_samples),
        [lines] + slot_scratch(1, jnp.float32),
    )
    (grad,) = call(
        functools.partial(backward_next, sizes, early),
        "backward_next",
        [image_f32],
        tables,
        (basis, *[near_resid[move] for move in early], grad),
        slot_scratch(len(early), jnp.float32),
        {len(tables) + 1 + len(early): 0},
    )
    (grad,) = call(
        functools.partial(backward_next, sizes, [last]),
        "backward_last",
        [image_f32],
        tables,
        (basis, near_resid[last], grad),
        slot_scratch(1, jnp.float32),
        {len(tables) + 2: 0},
    )
    mean_sum = grad
    scale_sum = grad * turn
    for r in range(1, samples):
        other_grad = rotated(grad, "mc", r)
        mean_sum = mean_sum + other_grad
        scale_sum = scale_sum + other_grad * other_turns[r - 1]
    return ((mean_sum / samples)[None], (scale_sum / samples + 1.0)[None])

def solution(mesh):
    placed = (
        P("tile", "filt", None, None),
        P("tile", "filt", None, None),
        P("mc", "tile", "filt", None, None),
        P("tile", "filt", None, None),
        P("tile", "filt", None, None),
        P(),
        P(),
        P(),
        P(),
        P(),
    )
    return jax.shard_map(
        body,
        mesh=mesh,
        in_specs=placed,
        out_specs=(P("tile", "filt", None, None), P("tile", "filt", None, None)),
        check_vma=False,
    )
```

```python
import functools

import jax
import jax.numpy as jnp
from jax import lax
from jax.experimental import pallas as pl
from jax.experimental.pallas import tpu as pltpu
from jax.sharding import PartitionSpec as P

NB = 6
K = 3
REACH = 2
HEAD = 3
STEP = 16
LANES = 128
VMEM_BYTES = 16 * 1024 * 1024
VMEM = pl.BlockSpec(memory_space=pltpu.VMEM)
SMEM = pl.BlockSpec(memory_space=pltpu.SMEM)


def shifted(x, axis, by):
    length = lax.axis_size(axis)
    pairs = [(i, i + by) for i in range(length) if 0 <= i + by < length]
    return lax.ppermute(x, axis, pairs)


def rotated(x, axis, by):
    length = lax.axis_size(axis)
    return lax.ppermute(x, axis, [(i, (i + by) % length) for i in range(length)])


def build_basis(taps_ref, lines_ref, basis_ref, adjoint):
    kinds, side = basis_ref.shape[0] // 2, basis_ref.shape[1]
    count = taps_ref.shape[1]
    half = (count - 1) // 2
    taps = taps_ref[...].astype(jnp.bfloat16)
    tap = lax.broadcasted_iota(jnp.int32, (count, side), 0)
    lane = lax.broadcasted_iota(jnp.int32, (count, side), 1)
    lane = jnp.where(lane < side // 2, lane, lane - side)
    plain = (lane == half - tap).astype(jnp.float32).astype(jnp.bfloat16)
    turned = (lane == tap - half).astype(jnp.float32).astype(jnp.bfloat16)
    lines_ref[0] = dot(taps, turned if adjoint else plain)
    lines_ref[1] = dot(taps, plain if adjoint else turned)
    apart = lax.broadcasted_iota(jnp.int32, (side, side), 0) - lax.broadcasted_iota(
        jnp.int32, (side, side), 1
    )
    band = jnp.abs(apart) <= half

    def one(k, carry):
        for c in range(2):
            line = jnp.broadcast_to(lines_ref[c, pl.ds(2 * k + c, 1), :], (side, side))
            rows = pltpu.roll(line, 0, 1, stride=1, stride_axis=0)
            basis_ref[c * kinds + k] = jnp.where(band, rows, 0.0).astype(jnp.bfloat16)
        return carry

    lax.fori_loop(0, kinds, one, 0)


def fill_tables(sizes, inter_ref, counts_ref, coeff_ref, slots_ref, weights_ref):
    tiles, filters, local = sizes
    fields = inter_ref.shape[3]
    own = lax.axis_index("tile")
    first = lax.axis_index("filt") * local
    row_id = lax.broadcasted_iota(jnp.int32, (tiles, NB), 0)
    lane_id = lax.broadcasted_iota(jnp.int32, (1, filters), 1)
    for w in range(2 * REACH + 1):
        tile = jnp.clip(own + w - REACH, 0, tiles - 1)
        live = counts_ref[pl.ds(tile, 1), :]
        for f in range(local):
            row = w * local + f
            for q in range(K):
                entry = inter_ref[first + f, q, pl.ds(tile, 1), :]
                slots_ref[row : row + 1, STEP * q : STEP * q + fields] = entry
            count = jnp.sum(jnp.where(lane_id == first + f, live, 0).astype(jnp.float32), 1, keepdims=True)
            slots_ref[row : row + 1, STEP * K : STEP * K + 1] = count.astype(jnp.int32)
            for c in range(3):
                block = coeff_ref[first + f, c].astype(jnp.float32)
                picked = jnp.sum(jnp.where(row_id == tile, block, 0.0), 0, keepdims=True)
                weights_ref[row : row + 1, STEP * c : STEP * c + NB] = picked


def find_slot(slots_ref, row, expo):
    live = slots_ref[row, STEP * K]
    base = jnp.int32(0)
    found = jnp.int32(0)
    for q in range(K):
        hit = (q < live) & (slots_ref[row, STEP * q] == expo)
        base = jnp.where(hit, STEP * q, base)
        found = jnp.where(hit, 1, found)
    return found, base


def weight(weights_ref, row, b, row_centred, col_centred):
    flat = weights_ref[row, b] + weights_ref[row, STEP + b] * row_centred
    return flat + weights_ref[row, 2 * STEP + b] * col_centred


def centred_axes(side, oy, ox):
    rows = lax.broadcasted_iota(jnp.int32, (side, 1), 0) + oy
    cols = lax.broadcasted_iota(jnp.int32, (1, side), 1) + ox
    return (
        (2 * rows + 1 - side).astype(jnp.float32) / side,
        (2 * cols + 1 - side).astype(jnp.float32) / side,
    )


def diagonal(side, by):
    apart = lax.broadcasted_iota(jnp.int32, (side, side), 1) - lax.broadcasted_iota(
        jnp.int32, (side, side), 0
    )
    return (apart == by).astype(jnp.float32).astype(jnp.bfloat16)


def dot(a, b):
    half = a.shape[0] // 2
    return jnp.concatenate(
        [
            jnp.dot(a[:half], b, preferred_element_type=jnp.float32),
            jnp.dot(a[half:], b, preferred_element_type=jnp.float32),
        ],
        0,
    )


def settle_contribution(image, oy, ox, pred_ref, f):
    side = image.shape[0]
    across = dot(image, diagonal(side, ox)).astype(jnp.bfloat16)
    pred_ref[f] = pred_ref[f] + dot(diagonal(side, -oy), across)


def contribution(slots_ref, weights_ref, basis_ref, row, base, place, image):
    side = image.shape[0]
    kinds = basis_ref.shape[0] // 2
    row_centred, col_centred = centred_axes(
        side, slots_ref[row, base + 1], slots_ref[row, base + 2]
    )
    total = jnp.zeros((side, side), jnp.float32)
    for b in range(NB):
        k = slots_ref[row, base + HEAD + b]
        half_blur = dot(basis_ref[k], image).astype(jnp.bfloat16)
        blurred = dot(half_blur, basis_ref[kinds + k])
        total = total + weight(weights_ref, place, b, row_centred, col_centred) * blurred
    return total.astype(jnp.bfloat16)


def bring_residual(image, oy, ox):
    side = image.shape[0]
    across = dot(image, diagonal(side, -ox)).astype(jnp.bfloat16)
    return dot(diagonal(side, oy), across)


def adjoint_term(slots_ref, weights_ref, basis_ref, row, base, place, moved):
    side = moved.shape[0]
    kinds = basis_ref.shape[0] // 2
    row_centred, col_centred = centred_axes(
        side, slots_ref[row, base + 1], slots_ref[row, base + 2]
    )
    total = jnp.zeros((side, side), jnp.float32)
    for b in range(NB):
        k = slots_ref[row, base + HEAD + b]
        w = weight(weights_ref, place, b, row_centred, col_centred)
        back_half = dot(basis_ref[k], (w * moved).astype(jnp.bfloat16)).astype(jnp.bfloat16)
        total = total + dot(back_half, basis_ref[kinds + k])
    return total


def source_of(own, move):
    distance, parity = move
    return own + jnp.where(lax.rem(own // distance, 2) == parity, distance, -distance)


def flipped(x, axis, move):
    distance, parity = move
    length = lax.axis_size(axis)
    firsts = [i for i in range(length - distance) if (i // distance) % 2 == parity]
    pairs = [(i, i + distance) for i in firsts] + [(i + distance, i) for i in firsts]
    return lax.ppermute(x, axis, pairs)


def gather_live(sizes, moves, backward, slots_ref, images, list_ref, held_ref):
    tiles, filters, local = sizes
    own = lax.axis_index("tile")
    live = jnp.int32(0)
    for move, image_ref in zip(moves, images):
        far = own if move is None else source_of(own, move)
        inside = jnp.where((far >= 0) & (far < tiles), 1, 0)
        here, there = REACH * local, jnp.clip(far - own + REACH, 0, 2 * REACH) * local
        tile_at, expo_at = (here, there) if backward else (there, here)
        expo = far if backward else own
        for f in range(local):
            found, base = find_slot(slots_ref, tile_at + f, expo)
            found = found * inside

            @pl.when(found == 1)
            def _():
                list_ref[0, live] = f
                list_ref[1, live] = tile_at + f
                list_ref[2, live] = base
                list_ref[3, live] = expo_at + f
                held_ref[live] = image_ref[f]

            live = live + found
    return live


def forward_slots(sizes, moves, slots_ref, weights_ref, basis_ref, images, pred_ref, scratch):
    list_ref, held_ref, ready_ref = scratch
    live = gather_live(sizes, moves, False, slots_ref, images, list_ref, held_ref)

    @pl.when(live > 0)
    def _():
        def blur(n):
            ready_ref[...] = contribution(
                slots_ref,
                weights_ref,
                basis_ref,
                list_ref[1, n],
                list_ref[2, n],
                list_ref[3, n],
                held_ref[n],
            )

        def settle(n):
            row, base = list_ref[1, n], list_ref[2, n]
            oy, ox = slots_ref[row, base + 1], slots_ref[row, base + 2]
            settle_contribution(ready_ref[...], oy, ox, pred_ref, list_ref[0, n])

        def one(n, carry):
            settle(n - 1)
            blur(n)
            return carry

        blur(0)
        lax.fori_loop(1, live, one, 0)
        settle(live - 1)


def backward_slots(sizes, moves, slots_ref, weights_ref, basis_ref, images, grad_ref, scratch):
    list_ref, held_ref, ready_ref = scratch
    live = gather_live(sizes, moves, True, slots_ref, images, list_ref, held_ref)

    @pl.when(live > 0)
    def _():
        def bring(n):
            row, base = list_ref[1, n], list_ref[2, n]
            return bring_residual(held_ref[n], slots_ref[row, base + 1], slots_ref[row, base + 2])

        def take(n):
            f = list_ref[0, n]
            grad_ref[f] = grad_ref[f] + adjoint_term(
                slots_ref,
                weights_ref,
                basis_ref,
                list_ref[1, n],
                list_ref[2, n],
                list_ref[3, n],
                ready_ref[...],
            )

        def one(n, carry):
            following = bring(n)
            take(n - 1)
            ready_ref[...] = following
            return carry

        ready_ref[...] = bring(0)
        lax.fori_loop(1, live, one, 0)
        take(live - 1)


def prepare(sizes, inter_ref, counts_ref, coeff_ref, taps_ref, *refs):
    slots_ref, weights_ref, forth_ref, back_ref, lines_ref = refs
    fill_tables(sizes, inter_ref, counts_ref, coeff_ref, slots_ref, weights_ref)
    build_basis(taps_ref, lines_ref, forth_ref, False)
    build_basis(taps_ref, lines_ref, back_ref, True)


def forward_own(sizes, slots_ref, weights_ref, basis_ref, image_ref, *refs):
    pred_ref, *scratch = refs
    pred_ref[...] = jnp.zeros_like(pred_ref)
    forward_slots(sizes, [None], slots_ref, weights_ref, basis_ref, [image_ref], pred_ref, scratch)


def forward_next(sizes, moves, slots_ref, weights_ref, basis_ref, *refs):
    images, (before_ref, pred_ref, *scratch) = refs[: len(moves)], refs[len(moves) :]
    del before_ref
    forward_slots(sizes, moves, slots_ref, weights_ref, basis_ref, images, pred_ref, scratch)


def forward_last(sizes, moves, slots_ref, weights_ref, basis_ref, *refs):
    images, refs = refs[: len(moves)], refs[len(moves) :]
    before_ref, observed_ref, inv_ref, pred_ref, resid_ref, *scratch = refs
    del before_ref
    forward_slots(sizes, moves, slots_ref, weights_ref, basis_ref, images, pred_ref, scratch)
    for f in range(observed_ref.shape[0]):
        gap = observed_ref[f].astype(jnp.float32) - pred_ref[f]
        resid_ref[f] = (inv_ref[f].astype(jnp.float32) * gap).astype(jnp.bfloat16)


def backward_own(
    sizes, samples, slots_ref, weights_ref, prec_ref, basis_ref, image_ref, *refs
):
    sample_ref, scale_ref, *refs = refs
    tiles, filters, local = sizes
    side = sample_ref.shape[1]
    part = lax.axis_index("filt")
    parts = filters // local
    first = part * local
    noises, refs = refs[:samples], refs[samples:]
    others, refs = refs[: parts - 1], refs[parts - 1 :]
    grad_ref, *refs = refs
    turns, scratch = refs[:samples], refs[samples:]
    for noise_ref, turn_ref in zip(noises, turns):
        turn_ref[...] = scale_ref[...] * noise_ref[...].astype(jnp.float32)
    for f in range(local):
        prior = jnp.zeros((side, side), jnp.float32)
        for g in range(local):
            prior = prior + prec_ref[first + f, first + g] * sample_ref[g]
        for r in range(1, parts):
            source = lax.rem(part + parts - r, parts) * local
            for g in range(local):
                far = others[r - 1][g].astype(jnp.float32)
                prior = prior + prec_ref[first + f, source + g] * far
        grad_ref[f] = -prior
    backward_slots(
        sizes, [None], slots_ref, weights_ref, basis_ref, [image_ref], grad_ref, scratch
    )


def backward_next(sizes, moves, slots_ref, weights_ref, basis_ref, *refs):
    images, (before_ref, grad_ref, *scratch) = refs[: len(moves)], refs[len(moves) :]
    del before_ref
    backward_slots(sizes, moves, slots_ref, weights_ref, basis_ref, images, grad_ref, scratch)


def body(
    sky_mean,
    sky_log_scale,
    noise_draw,
    observed,
    inv_var,
    intersections,
    counts,
    kernels,
    psf_coeffs,
    prior_prec,
):
    side = sky_mean.shape[2]
    local = sky_mean.shape[1]
    tiles, filters = counts.shape
    sizes = (tiles, filters, local)
    kinds = kernels.shape[0]
    started = [(d, parity) for d in range(1, REACH + 1) for parity in (0, 1)]
    last = (1, 1)
    early = [move for move in started if move != last]
    samples = lax.axis_size("mc")
    parts = lax.axis_size("filt")

    scale_map = jnp.exp(sky_log_scale[0])
    noise = noise_draw[0, 0]
    eps_float = noise.astype(jnp.float32)
    sample = sky_mean[0] + scale_map * eps_float
    sample_b = sample.astype(jnp.bfloat16)
    taps = kernels.reshape(2 * kinds, kernels.shape[2])

    image_f32 = jax.ShapeDtypeStruct((local, side, side), jnp.float32)
    image_b16 = jax.ShapeDtypeStruct((local, side, side), jnp.bfloat16)
    basis_type = jax.ShapeDtypeStruct((2 * kinds, side, side), jnp.bfloat16)
    cost = pl.CostEstimate(
        flops=2 * NB * 4 * side**3, bytes_accessed=8 * local * side * side, transcendentals=0
    )

    lines = pltpu.VMEM((2, 2 * kinds, side), jnp.float32)

    def slot_scratch(groups, ready):
        return [
            pltpu.SMEM((4, groups * local), jnp.int32),
            pltpu.VMEM((groups * local, side, side), jnp.bfloat16),
            pltpu.VMEM((side, side), ready),
        ]

    def call(kernel, name, outs, smem, vmem, scratch, aliases={}):
        return pl.pallas_call(
            kernel,
            out_shape=outs,
            in_specs=[SMEM] * len(smem) + [VMEM] * len(vmem),
            out_specs=[VMEM] * len(outs),
            scratch_shapes=scratch,
            input_output_aliases=aliases,
            compiler_params=pltpu.CompilerParams(vmem_limit_bytes=VMEM_BYTES),
            cost_estimate=cost,
            name=name,
        )(*smem, *vmem)

    near = {move: flipped(sample_b, "tile", move) for move in started}
    other_samples = [rotated(sample_b, "filt", r) for r in range(1, parts)]
    other_noise = [rotated(noise, "mc", r) for r in range(1, samples)]
    rows = -(-(2 * REACH + 1) * local // 8) * 8
    slots, weights, forth, back = call(
        functools.partial(prepare, sizes),
        "prepare",
        [
            jax.ShapeDtypeStruct((rows, LANES), jnp.int32),
            jax.ShapeDtypeStruct((rows, LANES), jnp.float32),
            basis_type,
            basis_type,
        ],
        (),
        (intersections.transpose(1, 2, 0, 3), counts, psf_coeffs.transpose(1, 3, 0, 2), taps),
        [lines],
    )
    tables = (slots, weights)
    (pred,) = call(
        functools.partial(forward_own, sizes),
        "forward_own",
        [image_f32],
        tables,
        (forth, sample_b),
        slot_scratch(1, jnp.bfloat16),
    )
    (pred,) = call(
        functools.partial(forward_next, sizes, early),
        "forward_next",
        [image_f32],
        tables,
        (forth, *[near[move] for move in early], pred),
        slot_scratch(len(early), jnp.bfloat16),
        {len(tables) + 1 + len(early): 0},
    )
    _, residual = call(
        functools.partial(forward_last, sizes, [last]),
        "forward_last",
        [image_f32, image_b16],
        tables,
        (forth, near[last], pred, observed[0], inv_var[0]),
        slot_scratch(1, jnp.bfloat16),
        {len(tables) + 2: 0},
    )
    near_resid = {move: flipped(residual, "tile", move) for move in started}
    grad, turn, *other_turns = call(
        functools.partial(backward_own, sizes, samples),
        "backward_own",
        [image_f32] * (1 + samples),
        tables + (prior_prec,),
        (back, residual, sample, scale_map, noise, *other_noise, *other_samples),
        slot_scratch(1, jnp.float32),
    )
    (grad,) = call(
        functools.partial(backward_next, sizes, early),
        "backward_next",
        [image_f32],
        tables,
        (back, *[near_resid[move] for move in early], grad),
        slot_scratch(len(early), jnp.float32),
        {len(tables) + 1 + len(early): 0},
    )
    (grad,) = call(
        functools.partial(backward_next, sizes, [last]),
        "backward_last",
        [image_f32],
        tables,
        (back, near_resid[last], grad),
        slot_scratch(1, jnp.float32),
        {len(tables) + 2: 0},
    )
    mean_sum = grad
    scale_sum = grad * turn
    for r in range(1, samples):
        other_grad = rotated(grad, "mc", r)
        mean_sum = mean_sum + other_grad
        scale_sum = scale_sum + other_grad * other_turns[r - 1]
    return ((mean_sum / samples)[None], (scale_sum / samples + 1.0)[None])

def solution(mesh):
    placed = (
        P("tile", "filt", None, None),
        P("tile", "filt", None, None),
        P("mc", "tile", "filt", None, None),
        P("tile", "filt", None, None),
        P("tile", "filt", None, None),
        P(),
        P(),
        P(),
        P(),
        P(),
    )
    return jax.shard_map(
        body,
        mesh=mesh,
        in_specs=placed,
        out_specs=(P("tile", "filt", None, None), P("tile", "filt", None, None)),
        check_vma=False,
    )
```

```python
import functools

import jax
import jax.numpy as jnp
from jax import lax
from jax.experimental import pallas as pl
from jax.experimental.pallas import tpu as pltpu
from jax.sharding import PartitionSpec as P

NB = 6
K = 3
REACH = 2
HEAD = 3
STEP = 16
LANES = 128
VMEM_BYTES = 16 * 1024 * 1024
VMEM = pl.BlockSpec(memory_space=pltpu.VMEM)
SMEM = pl.BlockSpec(memory_space=pltpu.SMEM)


def shifted(x, axis, by):
    length = lax.axis_size(axis)
    pairs = [(i, i + by) for i in range(length) if 0 <= i + by < length]
    return lax.ppermute(x, axis, pairs)


def rotated(x, axis, by):
    length = lax.axis_size(axis)
    return lax.ppermute(x, axis, [(i, (i + by) % length) for i in range(length)])


def build_basis(taps_ref, lines_ref, basis_ref, adjoint):
    kinds, side = basis_ref.shape[0] // 2, basis_ref.shape[1]
    count = taps_ref.shape[1]
    half = (count - 1) // 2
    taps = taps_ref[...].astype(jnp.bfloat16)
    tap = lax.broadcasted_iota(jnp.int32, (count, side), 0)
    lane = lax.broadcasted_iota(jnp.int32, (count, side), 1)
    lane = jnp.where(lane < side // 2, lane, lane - side)
    plain = (lane == half - tap).astype(jnp.float32).astype(jnp.bfloat16)
    turned = (lane == tap - half).astype(jnp.float32).astype(jnp.bfloat16)
    lines_ref[0] = dot(taps, turned if adjoint else plain)
    lines_ref[1] = dot(taps, plain if adjoint else turned)
    apart = lax.broadcasted_iota(jnp.int32, (side, side), 0) - lax.broadcasted_iota(
        jnp.int32, (side, side), 1
    )
    band = jnp.abs(apart) <= half

    def one(k, carry):
        for c in range(2):
            line = jnp.broadcast_to(lines_ref[c, pl.ds(2 * k + c, 1), :], (side, side))
            rows = pltpu.roll(line, 0, 1, stride=1, stride_axis=0)
            basis_ref[c * kinds + k] = jnp.where(band, rows, 0.0).astype(jnp.bfloat16)
        return carry

    lax.fori_loop(0, kinds, one, 0)


def fill_tables(sizes, inter_ref, counts_ref, coeff_ref, slots_ref, weights_ref):
    tiles, filters, local = sizes
    fields = inter_ref.shape[3]
    own = lax.axis_index("tile")
    first = lax.axis_index("filt") * local
    row_id = lax.broadcasted_iota(jnp.int32, (tiles, NB), 0)
    lane_id = lax.broadcasted_iota(jnp.int32, (1, filters), 1)
    for w in range(2 * REACH + 1):
        tile = jnp.clip(own + w - REACH, 0, tiles - 1)
        live = counts_ref[pl.ds(tile, 1), :]
        for f in range(local):
            row = w * local + f
            for q in range(K):
                entry = inter_ref[first + f, q, pl.ds(tile, 1), :]
                slots_ref[row : row + 1, STEP * q : STEP * q + fields] = entry
            count = jnp.sum(jnp.where(lane_id == first + f, live, 0).astype(jnp.float32), 1, keepdims=True)
            slots_ref[row : row + 1, STEP * K : STEP * K + 1] = count.astype(jnp.int32)
            for c in range(3):
                block = coeff_ref[first + f, c].astype(jnp.float32)
                picked = jnp.sum(jnp.where(row_id == tile, block, 0.0), 0, keepdims=True)
                weights_ref[row : row + 1, STEP * c : STEP * c + NB] = picked


def find_slot(slots_ref, row, expo):
    live = slots_ref[row, STEP * K]
    base = jnp.int32(0)
    found = jnp.int32(0)
    for q in range(K):
        hit = (q < live) & (slots_ref[row, STEP * q] == expo)
        base = jnp.where(hit, STEP * q, base)
        found = jnp.where(hit, 1, found)
    return found, base


def weight(weights_ref, row, b, row_centred, col_centred):
    flat = weights_ref[row, b] + weights_ref[row, STEP + b] * row_centred
    return flat + weights_ref[row, 2 * STEP + b] * col_centred


def centred_axes(side, oy, ox):
    rows = lax.broadcasted_iota(jnp.int32, (side, 1), 0) + oy
    cols = lax.broadcasted_iota(jnp.int32, (1, side), 1) + ox
    return (
        (2 * rows + 1 - side).astype(jnp.float32) / side,
        (2 * cols + 1 - side).astype(jnp.float32) / side,
    )


def diagonal(side, by):
    apart = lax.broadcasted_iota(jnp.int32, (side, side), 1) - lax.broadcasted_iota(
        jnp.int32, (side, side), 0
    )
    return (apart == by).astype(jnp.float32).astype(jnp.bfloat16)


def dot(a, b):
    return jnp.dot(a, b, preferred_element_type=jnp.float32)


def settle_contribution(image, oy, ox, pred_ref, f):
    side = image.shape[0]
    across = dot(image, diagonal(side, ox)).astype(jnp.bfloat16)
    pred_ref[f] = pred_ref[f] + dot(diagonal(side, -oy), across)


def contribution(slots_ref, weights_ref, basis_ref, row, base, place, image):
    side = image.shape[0]
    kinds = basis_ref.shape[0] // 2
    row_centred, col_centred = centred_axes(
        side, slots_ref[row, base + 1], slots_ref[row, base + 2]
    )
    total = jnp.zeros((side, side), jnp.float32)
    chosen = [slots_ref[row, base + HEAD + b] for b in range(NB)]
    half_blurs = dot(jnp.concatenate([basis_ref[k] for k in chosen], 0), image).astype(jnp.bfloat16)
    for b in range(NB):
        blurred = dot(half_blurs[b * side : (b + 1) * side], basis_ref[kinds + chosen[b]])
        total = total + weight(weights_ref, place, b, row_centred, col_centred) * blurred
    return total.astype(jnp.bfloat16)


def bring_residual(image, oy, ox):
    side = image.shape[0]
    across = dot(image, diagonal(side, -ox)).astype(jnp.bfloat16)
    return dot(diagonal(side, oy), across)


def adjoint_term(slots_ref, weights_ref, basis_ref, row, base, place, moved):
    side = moved.shape[0]
    kinds = basis_ref.shape[0] // 2
    row_centred, col_centred = centred_axes(
        side, slots_ref[row, base + 1], slots_ref[row, base + 2]
    )
    total = jnp.zeros((side, side), jnp.float32)
    for b in range(NB):
        k = slots_ref[row, base + HEAD + b]
        w = weight(weights_ref, place, b, row_centred, col_centred)
        back_half = dot(basis_ref[k], (w * moved).astype(jnp.bfloat16)).astype(jnp.bfloat16)
        total = total + dot(back_half, basis_ref[kinds + k])
    return total


def source_of(own, move):
    distance, parity = move
    return own + jnp.where(lax.rem(own // distance, 2) == parity, distance, -distance)


def flipped(x, axis, move):
    distance, parity = move
    length = lax.axis_size(axis)
    firsts = [i for i in range(length - distance) if (i // distance) % 2 == parity]
    pairs = [(i, i + distance) for i in firsts] + [(i + distance, i) for i in firsts]
    return lax.ppermute(x, axis, pairs)


def gather_live(sizes, moves, backward, slots_ref, images, list_ref, held_ref):
    tiles, filters, local = sizes
    own = lax.axis_index("tile")
    live = jnp.int32(0)
    for move, image_ref in zip(moves, images):
        far = own if move is None else source_of(own, move)
        inside = jnp.where((far >= 0) & (far < tiles), 1, 0)
        here, there = REACH * local, jnp.clip(far - own + REACH, 0, 2 * REACH) * local
        tile_at, expo_at = (here, there) if backward else (there, here)
        expo = far if backward else own
        for f in range(local):
            found, base = find_slot(slots_ref, tile_at + f, expo)
            found = found * inside

            @pl.when(found == 1)
            def _():
                list_ref[0, live] = f
                list_ref[1, live] = tile_at + f
                list_ref[2, live] = base
                list_ref[3, live] = expo_at + f
                held_ref[live] = image_ref[f]

            live = live + found
    return live


def forward_slots(sizes, moves, slots_ref, weights_ref, basis_ref, images, pred_ref, scratch):
    list_ref, held_ref, ready_ref = scratch
    live = gather_live(sizes, moves, False, slots_ref, images, list_ref, held_ref)

    @pl.when(live > 0)
    def _():
        def blur(n):
            ready_ref[...] = contribution(
                slots_ref,
                weights_ref,
                basis_ref,
                list_ref[1, n],
                list_ref[2, n],
                list_ref[3, n],
                held_ref[n],
            )

        def settle(n):
            row, base = list_ref[1, n], list_ref[2, n]
            oy, ox = slots_ref[row, base + 1], slots_ref[row, base + 2]
            settle_contribution(ready_ref[...], oy, ox, pred_ref, list_ref[0, n])

        def one(n, carry):
            settle(n - 1)
            blur(n)
            return carry

        blur(0)
        lax.fori_loop(1, live, one, 0)
        settle(live - 1)


def backward_slots(sizes, moves, slots_ref, weights_ref, basis_ref, images, grad_ref, scratch):
    list_ref, held_ref, ready_ref = scratch
    live = gather_live(sizes, moves, True, slots_ref, images, list_ref, held_ref)

    @pl.when(live > 0)
    def _():
        def bring(n):
            row, base = list_ref[1, n], list_ref[2, n]
            return bring_residual(held_ref[n], slots_ref[row, base + 1], slots_ref[row, base + 2])

        def take(n):
            f = list_ref[0, n]
            grad_ref[f] = grad_ref[f] + adjoint_term(
                slots_ref,
                weights_ref,
                basis_ref,
                list_ref[1, n],
                list_ref[2, n],
                list_ref[3, n],
                ready_ref[...],
            )

        def one(n, carry):
            following = bring(n)
            take(n - 1)
            ready_ref[...] = following
            return carry

        ready_ref[...] = bring(0)
        lax.fori_loop(1, live, one, 0)
        take(live - 1)


def prepare(sizes, inter_ref, counts_ref, coeff_ref, taps_ref, *refs):
    slots_ref, weights_ref, forth_ref, back_ref, lines_ref = refs
    fill_tables(sizes, inter_ref, counts_ref, coeff_ref, slots_ref, weights_ref)
    build_basis(taps_ref, lines_ref, forth_ref, False)
    build_basis(taps_ref, lines_ref, back_ref, True)


def forward_own(sizes, slots_ref, weights_ref, basis_ref, image_ref, *refs):
    pred_ref, *scratch = refs
    pred_ref[...] = jnp.zeros_like(pred_ref)
    forward_slots(sizes, [None], slots_ref, weights_ref, basis_ref, [image_ref], pred_ref, scratch)


def forward_next(sizes, moves, slots_ref, weights_ref, basis_ref, *refs):
    images, (before_ref, pred_ref, *scratch) = refs[: len(moves)], refs[len(moves) :]
    del before_ref
    forward_slots(sizes, moves, slots_ref, weights_ref, basis_ref, images, pred_ref, scratch)


def forward_last(sizes, moves, slots_ref, weights_ref, basis_ref, *refs):
    images, refs = refs[: len(moves)], refs[len(moves) :]
    before_ref, observed_ref, inv_ref, pred_ref, resid_ref, *scratch = refs
    del before_ref
    forward_slots(sizes, moves, slots_ref, weights_ref, basis_ref, images, pred_ref, scratch)
    for f in range(observed_ref.shape[0]):
        gap = observed_ref[f].astype(jnp.float32) - pred_ref[f]
        resid_ref[f] = (inv_ref[f].astype(jnp.float32) * gap).astype(jnp.bfloat16)


def subtract_prior(sizes, prec_ref, sample_ref, others, grad_ref):
    tiles, filters, local = sizes
    part = lax.axis_index("filt")
    parts = filters // local
    first = part * local
    for f in range(local):
        grad = grad_ref[f]
        for g in range(local):
            grad = grad - prec_ref[first + f, first + g] * sample_ref[g]
        for r in range(1, parts):
            source = lax.rem(part + parts - r, parts) * local
            for g in range(local):
                far = others[r - 1][g].astype(jnp.float32)
                grad = grad - prec_ref[first + f, source + g] * far
        grad_ref[f] = grad


def backward_own(sizes, samples, slots_ref, weights_ref, basis_ref, image_ref, *refs):
    scale_ref, *refs = refs
    noises, (grad_ref, *refs) = refs[:samples], refs[samples:]
    turns, scratch = refs[:samples], refs[samples:]
    for noise_ref, turn_ref in zip(noises, turns):
        turn_ref[...] = scale_ref[...] * noise_ref[...].astype(jnp.float32)
    grad_ref[...] = jnp.zeros_like(grad_ref)
    backward_slots(
        sizes, [None], slots_ref, weights_ref, basis_ref, [image_ref], grad_ref, scratch
    )


def backward_prior(sizes, prec_ref, before_ref, sample_ref, *refs):
    others, (grad_ref,) = refs[:-1], refs[-1:]
    del before_ref
    subtract_prior(sizes, prec_ref, sample_ref, others, grad_ref)


def backward_next(sizes, moves, slots_ref, weights_ref, basis_ref, *refs):
    images, (before_ref, grad_ref, *scratch) = refs[: len(moves)], refs[len(moves) :]
    del before_ref
    backward_slots(sizes, moves, slots_ref, weights_ref, basis_ref, images, grad_ref, scratch)


def body(
    sky_mean,
    sky_log_scale,
    noise_draw,
    observed,
    inv_var,
    intersections,
    counts,
    kernels,
    psf_coeffs,
    prior_prec,
):
    side = sky_mean.shape[2]
    local = sky_mean.shape[1]
    tiles, filters = counts.shape
    sizes = (tiles, filters, local)
    kinds = kernels.shape[0]
    started = [(d, parity) for d in range(1, REACH + 1) for parity in (0, 1)]
    last = (1, 1)
    early = [move for move in started if move != last]
    samples = lax.axis_size("mc")
    parts = lax.axis_size("filt")

    scale_map = jnp.exp(sky_log_scale[0])
    noise = noise_draw[0, 0]
    eps_float = noise.astype(jnp.float32)
    sample = sky_mean[0] + scale_map * eps_float
    sample_b = sample.astype(jnp.bfloat16)
    taps = kernels.reshape(2 * kinds, kernels.shape[2])

    image_f32 = jax.ShapeDtypeStruct((local, side, side), jnp.float32)
    image_b16 = jax.ShapeDtypeStruct((local, side, side), jnp.bfloat16)
    basis_type = jax.ShapeDtypeStruct((2 * kinds, side, side), jnp.bfloat16)
    cost = pl.CostEstimate(
        flops=2 * NB * 4 * side**3, bytes_accessed=8 * local * side * side, transcendentals=0
    )

    lines = pltpu.VMEM((2, 2 * kinds, side), jnp.float32)

    def slot_scratch(groups, ready):
        return [
            pltpu.SMEM((4, groups * local), jnp.int32),
            pltpu.VMEM((groups * local, side, side), jnp.bfloat16),
            pltpu.VMEM((side, side), ready),
        ]

    def call(kernel, name, outs, smem, vmem, scratch, aliases={}):
        return pl.pallas_call(
            kernel,
            out_shape=outs,
            in_specs=[SMEM] * len(smem) + [VMEM] * len(vmem),
            out_specs=[VMEM] * len(outs),
            scratch_shapes=scratch,
            input_output_aliases=aliases,
            compiler_params=pltpu.CompilerParams(vmem_limit_bytes=VMEM_BYTES),
            cost_estimate=cost,
            name=name,
        )(*smem, *vmem)

    near = {move: flipped(sample_b, "tile", move) for move in started}
    other_noise = [rotated(noise, "mc", r) for r in range(1, samples)]
    rows = -(-(2 * REACH + 1) * local // 8) * 8
    slots, weights, forth, back = call(
        functools.partial(prepare, sizes),
        "prepare",
        [
            jax.ShapeDtypeStruct((rows, LANES), jnp.int32),
            jax.ShapeDtypeStruct((rows, LANES), jnp.float32),
            basis_type,
            basis_type,
        ],
        (),
        (intersections.transpose(1, 2, 0, 3), counts, psf_coeffs.transpose(1, 3, 0, 2), taps),
        [lines],
    )
    tables = (slots, weights)
    (pred,) = call(
        functools.partial(forward_own, sizes),
        "forward_own",
        [image_f32],
        tables,
        (forth, sample_b),
        slot_scratch(1, jnp.bfloat16),
    )
    (pred,) = call(
        functools.partial(forward_next, sizes, early),
        "forward_next",
        [image_f32],
        tables,
        (forth, *[near[move] for move in early], pred),
        slot_scratch(len(early), jnp.bfloat16),
        {len(tables) + 1 + len(early): 0},
    )
    _, residual = call(
        functools.partial(forward_last, sizes, [last]),
        "forward_last",
        [image_f32, image_b16],
        tables,
        (forth, near[last], pred, observed[0], inv_var[0]),
        slot_scratch(1, jnp.bfloat16),
        {len(tables) + 2: 0},
    )
    near_resid = {move: flipped(residual, "tile", move) for move in started}
    grad, turn, *other_turns = call(
        functools.partial(backward_own, sizes, samples),
        "backward_own",
        [image_f32] * (1 + samples),
        tables,
        (back, residual, scale_map, noise, *other_noise),
        slot_scratch(1, jnp.float32),
    )
    late_b, grad = lax.optimization_barrier((sample_b, grad))
    other_samples = [rotated(late_b, "filt", r) for r in range(1, parts)]
    (grad,) = call(
        functools.partial(backward_next, sizes, early),
        "backward_next",
        [image_f32],
        tables,
        (back, *[near_resid[move] for move in early], grad),
        slot_scratch(len(early), jnp.float32),
        {len(tables) + 1 + len(early): 0},
    )
    (grad,) = call(
        functools.partial(backward_prior, sizes),
        "backward_prior",
        [image_f32],
        (prior_prec,),
        (grad, sample, *other_samples),
        [],
        {1: 0},
    )
    (grad,) = call(
        functools.partial(backward_next, sizes, [last]),
        "backward_last",
        [image_f32],
        tables,
        (back, near_resid[last], grad),
        slot_scratch(1, jnp.float32),
        {len(tables) + 2: 0},
    )
    mean_sum = grad
    scale_sum = grad * turn
    for r in range(1, samples):
        other_grad = rotated(grad, "mc", r)
        mean_sum = mean_sum + other_grad
        scale_sum = scale_sum + other_grad * other_turns[r - 1]
    return ((mean_sum / samples)[None], (scale_sum / samples + 1.0)[None])

def solution(mesh):
    placed = (
        P("tile", "filt", None, None),
        P("tile", "filt", None, None),
        P("mc", "tile", "filt", None, None),
        P("tile", "filt", None, None),
        P("tile", "filt", None, None),
        P(),
        P(),
        P(),
        P(),
        P(),
    )
    return jax.shard_map(
        body,
        mesh=mesh,
        in_specs=placed,
        out_specs=(P("tile", "filt", None, None), P("tile", "filt", None, None)),
        check_vma=False,
    )
```

```python
import functools

import jax
import jax.numpy as jnp
from jax import lax
from jax.experimental import pallas as pl
from jax.experimental.pallas import tpu as pltpu
from jax.sharding import PartitionSpec as P

NB = 6
K = 3
REACH = 2
HEAD = 3
STEP = 16
LANES = 128
VMEM_BYTES = 16 * 1024 * 1024
VMEM = pl.BlockSpec(memory_space=pltpu.VMEM)
SMEM = pl.BlockSpec(memory_space=pltpu.SMEM)


def shifted(x, axis, by):
    length = lax.axis_size(axis)
    pairs = [(i, i + by) for i in range(length) if 0 <= i + by < length]
    return lax.ppermute(x, axis, pairs)


def rotated(x, axis, by):
    length = lax.axis_size(axis)
    return lax.ppermute(x, axis, [(i, (i + by) % length) for i in range(length)])


def build_basis(taps_ref, lines_ref, basis_ref, adjoint):
    kinds, side = basis_ref.shape[0] // 2, basis_ref.shape[1]
    count = taps_ref.shape[1]
    half = (count - 1) // 2
    taps = taps_ref[...].astype(jnp.bfloat16)
    tap = lax.broadcasted_iota(jnp.int32, (count, side), 0)
    lane = lax.broadcasted_iota(jnp.int32, (count, side), 1)
    lane = jnp.where(lane < side // 2, lane, lane - side)
    plain = (lane == half - tap).astype(jnp.float32).astype(jnp.bfloat16)
    turned = (lane == tap - half).astype(jnp.float32).astype(jnp.bfloat16)
    lines_ref[0] = dot(taps, turned if adjoint else plain)
    lines_ref[1] = dot(taps, plain if adjoint else turned)
    apart = lax.broadcasted_iota(jnp.int32, (side, side), 0) - lax.broadcasted_iota(
        jnp.int32, (side, side), 1
    )
    band = jnp.abs(apart) <= half

    def one(k, carry):
        for c in range(2):
            line = jnp.broadcast_to(lines_ref[c, pl.ds(2 * k + c, 1), :], (side, side))
            rows = pltpu.roll(line, 0, 1, stride=1, stride_axis=0)
            basis_ref[c * kinds + k] = jnp.where(band, rows, 0.0).astype(jnp.bfloat16)
        return carry

    lax.fori_loop(0, kinds, one, 0)


def fill_tables(sizes, inter_ref, counts_ref, coeff_ref, slots_ref, weights_ref):
    tiles, filters, local = sizes
    fields = inter_ref.shape[3]
    own = lax.axis_index("tile")
    first = lax.axis_index("filt") * local
    row_id = lax.broadcasted_iota(jnp.int32, (tiles, NB), 0)
    lane_id = lax.broadcasted_iota(jnp.int32, (1, filters), 1)
    for w in range(2 * REACH + 1):
        tile = jnp.clip(own + w - REACH, 0, tiles - 1)
        live = counts_ref[pl.ds(tile, 1), :]
        for f in range(local):
            row = w * local + f
            for q in range(K):
                entry = inter_ref[first + f, q, pl.ds(tile, 1), :]
                slots_ref[row : row + 1, STEP * q : STEP * q + fields] = entry
            count = jnp.sum(jnp.where(lane_id == first + f, live, 0).astype(jnp.float32), 1, keepdims=True)
            slots_ref[row : row + 1, STEP * K : STEP * K + 1] = count.astype(jnp.int32)
            for c in range(3):
                block = coeff_ref[first + f, c].astype(jnp.float32)
                picked = jnp.sum(jnp.where(row_id == tile, block, 0.0), 0, keepdims=True)
                weights_ref[row : row + 1, STEP * c : STEP * c + NB] = picked


def find_slot(slots_ref, row, expo):
    live = slots_ref[row, STEP * K]
    base = jnp.int32(0)
    found = jnp.int32(0)
    for q in range(K):
        hit = (q < live) & (slots_ref[row, STEP * q] == expo)
        base = jnp.where(hit, STEP * q, base)
        found = jnp.where(hit, 1, found)
    return found, base


def weight(weights_ref, row, b, row_centred, col_centred):
    flat = weights_ref[row, b] + weights_ref[row, STEP + b] * row_centred
    return flat + weights_ref[row, 2 * STEP + b] * col_centred


def centred_axes(side, oy, ox):
    rows = lax.broadcasted_iota(jnp.int32, (side, 1), 0) + oy
    cols = lax.broadcasted_iota(jnp.int32, (1, side), 1) + ox
    return (
        (2 * rows + 1 - side).astype(jnp.float32) / side,
        (2 * cols + 1 - side).astype(jnp.float32) / side,
    )


def diagonal(side, by):
    apart = lax.broadcasted_iota(jnp.int32, (side, side), 1) - lax.broadcasted_iota(
        jnp.int32, (side, side), 0
    )
    return (apart == by).astype(jnp.float32).astype(jnp.bfloat16)


def dot(a, b):
    return jnp.dot(a, b, preferred_element_type=jnp.float32)


def settle_contribution(image, oy, ox, pred_ref, f):
    side = image.shape[0]
    across = dot(image, diagonal(side, ox)).astype(jnp.bfloat16)
    pred_ref[f] = pred_ref[f] + dot(diagonal(side, -oy), across)


def contribution(slots_ref, weights_ref, basis_ref, row, base, place, image):
    side = image.shape[0]
    kinds = basis_ref.shape[0] // 2
    row_centred, col_centred = centred_axes(
        side, slots_ref[row, base + 1], slots_ref[row, base + 2]
    )
    total = jnp.zeros((side, side), jnp.float32)
    chosen = [slots_ref[row, base + HEAD + b] for b in range(NB)]
    half_blurs = dot(jnp.concatenate([basis_ref[k] for k in chosen], 0), image).astype(jnp.bfloat16)
    for b in range(NB):
        blurred = dot(half_blurs[b * side : (b + 1) * side], basis_ref[kinds + chosen[b]])
        total = total + weight(weights_ref, place, b, row_centred, col_centred) * blurred
    return total.astype(jnp.bfloat16)


def bring_residual(image, oy, ox):
    side = image.shape[0]
    across = dot(image, diagonal(side, -ox)).astype(jnp.bfloat16)
    return dot(diagonal(side, oy), across)


def adjoint_term(slots_ref, weights_ref, basis_ref, row, base, place, moved):
    side = moved.shape[0]
    kinds = basis_ref.shape[0] // 2
    row_centred, col_centred = centred_axes(
        side, slots_ref[row, base + 1], slots_ref[row, base + 2]
    )
    total = jnp.zeros((side, side), jnp.float32)
    for b in range(NB):
        k = slots_ref[row, base + HEAD + b]
        w = weight(weights_ref, place, b, row_centred, col_centred)
        back_half = dot(basis_ref[k], (w * moved).astype(jnp.bfloat16)).astype(jnp.bfloat16)
        total = total + dot(back_half, basis_ref[kinds + k])
    return total


def source_of(own, move):
    distance, parity = move
    return own + jnp.where(lax.rem(own // distance, 2) == parity, distance, -distance)


def flipped(x, axis, move):
    distance, parity = move
    length = lax.axis_size(axis)
    firsts = [i for i in range(length - distance) if (i // distance) % 2 == parity]
    pairs = [(i, i + distance) for i in firsts] + [(i + distance, i) for i in firsts]
    return lax.ppermute(x, axis, pairs)


def relay_onward(near, count):
    length = lax.axis_size("tile")
    pairs = [(i, i + 2) for i in range(0, length - 2, 2)]
    pairs += [(i, i - 2) for i in range(3, length, 2)]
    return lax.ppermute(near[1, 0][:count], "tile", pairs)


def relay_across(near, count):
    own = lax.axis_index("tile")
    first = lax.rem(own, 2) == lax.rem(own // 2, 2)
    image = jnp.where(first, near[2, 0][count:], near[2, 1][count:])
    return flipped(image, "tile", (1, 0))


def gather_live(sizes, moves, backward, slots_ref, images, list_ref, held_ref):
    tiles, filters, local = sizes
    own = lax.axis_index("tile")
    live = jnp.int32(0)
    for (move, f_first), image_ref in zip(moves, images):
        far = own if move is None else source_of(own, move)
        inside = jnp.where((far >= 0) & (far < tiles), 1, 0)
        here, there = REACH * local, jnp.clip(far - own + REACH, 0, 2 * REACH) * local
        tile_at, expo_at = (here, there) if backward else (there, here)
        expo = far if backward else own
        for f in range(f_first, f_first + image_ref.shape[0]):
            found, base = find_slot(slots_ref, tile_at + f, expo)
            found = found * inside

            @pl.when(found == 1)
            def _():
                list_ref[0, live] = f
                list_ref[1, live] = tile_at + f
                list_ref[2, live] = base
                list_ref[3, live] = expo_at + f
                held_ref[live] = image_ref[f - f_first]

            live = live + found
    return live


def forward_slots(sizes, moves, slots_ref, weights_ref, basis_ref, images, pred_ref, scratch):
    list_ref, held_ref, ready_ref = scratch
    live = gather_live(sizes, moves, False, slots_ref, images, list_ref, held_ref)

    @pl.when(live > 0)
    def _():
        def blur(n):
            ready_ref[...] = contribution(
                slots_ref,
                weights_ref,
                basis_ref,
                list_ref[1, n],
                list_ref[2, n],
                list_ref[3, n],
                held_ref[n],
            )

        def settle(n):
            row, base = list_ref[1, n], list_ref[2, n]
            oy, ox = slots_ref[row, base + 1], slots_ref[row, base + 2]
            settle_contribution(ready_ref[...], oy, ox, pred_ref, list_ref[0, n])

        def one(n, carry):
            settle(n - 1)
            blur(n)
            return carry

        blur(0)
        lax.fori_loop(1, live, one, 0)
        settle(live - 1)


def backward_slots(sizes, moves, slots_ref, weights_ref, basis_ref, images, grad_ref, scratch):
    list_ref, held_ref, ready_ref = scratch
    live = gather_live(sizes, moves, True, slots_ref, images, list_ref, held_ref)

    @pl.when(live > 0)
    def _():
        def bring(n):
            row, base = list_ref[1, n], list_ref[2, n]
            return bring_residual(held_ref[n], slots_ref[row, base + 1], slots_ref[row, base + 2])

        def take(n):
            f = list_ref[0, n]
            grad_ref[f] = grad_ref[f] + adjoint_term(
                slots_ref,
                weights_ref,
                basis_ref,
                list_ref[1, n],
                list_ref[2, n],
                list_ref[3, n],
                ready_ref[...],
            )

        def one(n, carry):
            following = bring(n)
            take(n - 1)
            ready_ref[...] = following
            return carry

        ready_ref[...] = bring(0)
        lax.fori_loop(1, live, one, 0)
        take(live - 1)


def prepare(sizes, inter_ref, counts_ref, coeff_ref, taps_ref, *refs):
    slots_ref, weights_ref, forth_ref, back_ref, lines_ref = refs
    fill_tables(sizes, inter_ref, counts_ref, coeff_ref, slots_ref, weights_ref)
    build_basis(taps_ref, lines_ref, forth_ref, False)
    build_basis(taps_ref, lines_ref, back_ref, True)


def forward_own(sizes, slots_ref, weights_ref, basis_ref, image_ref, *refs):
    pred_ref, *scratch = refs
    pred_ref[...] = jnp.zeros_like(pred_ref)
    forward_slots(sizes, [(None, 0)], slots_ref, weights_ref, basis_ref, [image_ref], pred_ref, scratch)


def forward_next(sizes, moves, slots_ref, weights_ref, basis_ref, *refs):
    images, (before_ref, pred_ref, *scratch) = refs[: len(moves)], refs[len(moves) :]
    del before_ref
    forward_slots(sizes, moves, slots_ref, weights_ref, basis_ref, images, pred_ref, scratch)


def forward_last(sizes, moves, slots_ref, weights_ref, basis_ref, *refs):
    images, refs = refs[: len(moves)], refs[len(moves) :]
    before_ref, observed_ref, inv_ref, pred_ref, resid_ref, *scratch = refs
    del before_ref
    forward_slots(sizes, moves, slots_ref, weights_ref, basis_ref, images, pred_ref, scratch)
    for f in range(observed_ref.shape[0]):
        gap = observed_ref[f].astype(jnp.float32) - pred_ref[f]
        resid_ref[f] = (inv_ref[f].astype(jnp.float32) * gap).astype(jnp.bfloat16)


def subtract_prior(sizes, prec_ref, sample_ref, others, grad_ref):
    tiles, filters, local = sizes
    part = lax.axis_index("filt")
    parts = filters // local
    first = part * local
    for f in range(local):
        grad = grad_ref[f]
        for g in range(local):
            grad = grad - prec_ref[first + f, first + g] * sample_ref[g]
        for r in range(1, parts):
            source = lax.rem(part + parts - r, parts) * local
            for g in range(local):
                far = others[r - 1][g].astype(jnp.float32)
                grad = grad - prec_ref[first + f, source + g] * far
        grad_ref[f] = grad


def backward_own(sizes, samples, slots_ref, weights_ref, basis_ref, image_ref, *refs):
    scale_ref, *refs = refs
    noises, (grad_ref, *refs) = refs[:samples], refs[samples:]
    turns, scratch = refs[:samples], refs[samples:]
    for noise_ref, turn_ref in zip(noises, turns):
        turn_ref[...] = scale_ref[...] * noise_ref[...].astype(jnp.float32)
    grad_ref[...] = jnp.zeros_like(grad_ref)
    backward_slots(
        sizes, [(None, 0)], slots_ref, weights_ref, basis_ref, [image_ref], grad_ref, scratch
    )


def backward_prior(sizes, prec_ref, before_ref, sample_ref, *refs):
    others, (grad_ref,) = refs[:-1], refs[-1:]
    del before_ref
    subtract_prior(sizes, prec_ref, sample_ref, others, grad_ref)


def backward_next(sizes, moves, slots_ref, weights_ref, basis_ref, *refs):
    images, (before_ref, grad_ref, *scratch) = refs[: len(moves)], refs[len(moves) :]
    del before_ref
    backward_slots(sizes, moves, slots_ref, weights_ref, basis_ref, images, grad_ref, scratch)


def body(
    sky_mean,
    sky_log_scale,
    noise_draw,
    observed,
    inv_var,
    intersections,
    counts,
    kernels,
    psf_coeffs,
    prior_prec,
):
    side = sky_mean.shape[2]
    local = sky_mean.shape[1]
    tiles, filters = counts.shape
    sizes = (tiles, filters, local)
    kinds = kernels.shape[0]
    early = [(1, 0), (2, 0), (2, 1)]
    early_moves = [(move, 0) for move in early]
    onward = local - local // 3
    last_moves = [((1, 1), 0)] + ([((1, 1), onward)] if onward < local else [])

    def last_images(near):
        across = [relay_across(near, onward)] if onward < local else []
        return [relay_onward(near, onward), *across]

    samples = lax.axis_size("mc")
    parts = lax.axis_size("filt")

    scale_map = jnp.exp(sky_log_scale[0])
    noise = noise_draw[0, 0]
    eps_float = noise.astype(jnp.float32)
    sample = sky_mean[0] + scale_map * eps_float
    sample_b = sample.astype(jnp.bfloat16)
    taps = kernels.reshape(2 * kinds, kernels.shape[2])

    image_f32 = jax.ShapeDtypeStruct((local, side, side), jnp.float32)
    image_b16 = jax.ShapeDtypeStruct((local, side, side), jnp.bfloat16)
    basis_type = jax.ShapeDtypeStruct((2 * kinds, side, side), jnp.bfloat16)
    cost = pl.CostEstimate(
        flops=2 * NB * 4 * side**3, bytes_accessed=8 * local * side * side, transcendentals=0
    )

    lines = pltpu.VMEM((2, 2 * kinds, side), jnp.float32)

    def slot_scratch(groups, ready):
        return [
            pltpu.SMEM((4, groups * local), jnp.int32),
            pltpu.VMEM((groups * local, side, side), jnp.bfloat16),
            pltpu.VMEM((side, side), ready),
        ]

    def call(kernel, name, outs, smem, vmem, scratch, aliases={}):
        return pl.pallas_call(
            kernel,
            out_shape=outs,
            in_specs=[SMEM] * len(smem) + [VMEM] * len(vmem),
            out_specs=[VMEM] * len(outs),
            scratch_shapes=scratch,
            input_output_aliases=aliases,
            compiler_params=pltpu.CompilerParams(vmem_limit_bytes=VMEM_BYTES),
            cost_estimate=cost,
            name=name,
        )(*smem, *vmem)

    near = {move: flipped(sample_b, "tile", move) for move in early}
    other_noise = [rotated(noise, "mc", r) for r in range(1, samples)]
    rows = -(-(2 * REACH + 1) * local // 8) * 8
    slots, weights, forth, back = call(
        functools.partial(prepare, sizes),
        "prepare",
        [
            jax.ShapeDtypeStruct((rows, LANES), jnp.int32),
            jax.ShapeDtypeStruct((rows, LANES), jnp.float32),
            basis_type,
            basis_type,
        ],
        (),
        (intersections.transpose(1, 2, 0, 3), counts, psf_coeffs.transpose(1, 3, 0, 2), taps),
        [lines],
    )
    tables = (slots, weights)
    (pred,) = call(
        functools.partial(forward_own, sizes),
        "forward_own",
        [image_f32],
        tables,
        (forth, sample_b),
        slot_scratch(1, jnp.bfloat16),
    )
    near[1, 0], pred = lax.optimization_barrier((near[1, 0], pred))
    near_last = last_images(near)
    (pred,) = call(
        functools.partial(forward_next, sizes, early_moves),
        "forward_next",
        [image_f32],
        tables,
        (forth, *[near[move] for move in early], pred),
        slot_scratch(len(early), jnp.bfloat16),
        {len(tables) + 1 + len(early): 0},
    )
    _, residual = call(
        functools.partial(forward_last, sizes, last_moves),
        "forward_last",
        [image_f32, image_b16],
        tables,
        (forth, *near_last, pred, observed[0], inv_var[0]),
        slot_scratch(1, jnp.bfloat16),
        {len(tables) + 1 + len(near_last): 0},
    )
    near_resid = {move: flipped(residual, "tile", move) for move in early}
    grad, turn, *other_turns = call(
        functools.partial(backward_own, sizes, samples),
        "backward_own",
        [image_f32] * (1 + samples),
        tables,
        (back, residual, scale_map, noise, *other_noise),
        slot_scratch(1, jnp.float32),
    )
    late_b, near_resid[1, 0], grad = lax.optimization_barrier((sample_b, near_resid[1, 0], grad))
    near_resid_last = last_images(near_resid)
    other_samples = [rotated(late_b, "filt", r) for r in range(1, parts)]
    (grad,) = call(
        functools.partial(backward_next, sizes, early_moves),
        "backward_next",
        [image_f32],
        tables,
        (back, *[near_resid[move] for move in early], grad),
        slot_scratch(len(early), jnp.float32),
        {len(tables) + 1 + len(early): 0},
    )
    (grad,) = call(
        functools.partial(backward_prior, sizes),
        "backward_prior",
        [image_f32],
        (prior_prec,),
        (grad, sample, *other_samples),
        [],
        {1: 0},
    )
    (grad,) = call(
        functools.partial(backward_next, sizes, last_moves),
        "backward_last",
        [image_f32],
        tables,
        (back, *near_resid_last, grad),
        slot_scratch(1, jnp.float32),
        {len(tables) + 1 + len(near_resid_last): 0},
    )
    mean_sum = grad
    scale_sum = grad * turn
    for r in range(1, samples):
        other_grad = rotated(grad, "mc", r)
        mean_sum = mean_sum + other_grad
        scale_sum = scale_sum + other_grad * other_turns[r - 1]
    return ((mean_sum / samples)[None], (scale_sum / samples + 1.0)[None])

def solution(mesh):
    placed = (
        P("tile", "filt", None, None),
        P("tile", "filt", None, None),
        P("mc", "tile", "filt", None, None),
        P("tile", "filt", None, None),
        P("tile", "filt", None, None),
        P(),
        P(),
        P(),
        P(),
        P(),
    )
    return jax.shard_map(
        body,
        mesh=mesh,
        in_specs=placed,
        out_specs=(P("tile", "filt", None, None), P("tile", "filt", None, None)),
        check_vma=False,
    )
```

```python
import functools

import jax
import jax.numpy as jnp
from jax import lax
from jax.experimental import pallas as pl
from jax.experimental.pallas import tpu as pltpu
from jax.sharding import PartitionSpec as P

NB = 6
K = 3
REACH = 2
HEAD = 3
STEP = 16
LANES = 128
VMEM_BYTES = 16 * 1024 * 1024
VMEM = pl.BlockSpec(memory_space=pltpu.VMEM)
SMEM = pl.BlockSpec(memory_space=pltpu.SMEM)


def shifted(x, axis, by):
    length = lax.axis_size(axis)
    pairs = [(i, i + by) for i in range(length) if 0 <= i + by < length]
    return lax.ppermute(x, axis, pairs)


def rotated(x, axis, by):
    length = lax.axis_size(axis)
    return lax.ppermute(x, axis, [(i, (i + by) % length) for i in range(length)])


def build_basis(taps_ref, lines_ref, basis_ref, adjoint):
    kinds, side = basis_ref.shape[0] // 2, basis_ref.shape[1]
    count = taps_ref.shape[1]
    half = (count - 1) // 2
    taps = taps_ref[...].astype(jnp.bfloat16)
    tap = lax.broadcasted_iota(jnp.int32, (count, side), 0)
    lane = lax.broadcasted_iota(jnp.int32, (count, side), 1)
    lane = jnp.where(lane < side // 2, lane, lane - side)
    plain = (lane == half - tap).astype(jnp.float32).astype(jnp.bfloat16)
    turned = (lane == tap - half).astype(jnp.float32).astype(jnp.bfloat16)
    lines_ref[0] = dot(taps, turned if adjoint else plain)
    lines_ref[1] = dot(taps, plain if adjoint else turned)
    apart = lax.broadcasted_iota(jnp.int32, (side, side), 0) - lax.broadcasted_iota(
        jnp.int32, (side, side), 1
    )
    band = jnp.abs(apart) <= half

    def one(k, carry):
        for c in range(2):
            line = jnp.broadcast_to(lines_ref[c, pl.ds(2 * k + c, 1), :], (side, side))
            rows = pltpu.roll(line, 0, 1, stride=1, stride_axis=0)
            basis_ref[c * kinds + k] = jnp.where(band, rows, 0.0).astype(jnp.bfloat16)
        return carry

    lax.fori_loop(0, kinds, one, 0)


def fill_tables(sizes, inter_ref, counts_ref, coeff_ref, slots_ref, weights_ref):
    tiles, filters, local = sizes
    fields = inter_ref.shape[3]
    own = lax.axis_index("tile")
    first = lax.axis_index("filt") * local
    row_id = lax.broadcasted_iota(jnp.int32, (tiles, NB), 0)
    lane_id = lax.broadcasted_iota(jnp.int32, (1, filters), 1)
    for w in range(2 * REACH + 1):
        tile = jnp.clip(own + w - REACH, 0, tiles - 1)
        live = counts_ref[pl.ds(tile, 1), :]
        for f in range(local):
            row = w * local + f
            for q in range(K):
                entry = inter_ref[first + f, q, pl.ds(tile, 1), :]
                slots_ref[row : row + 1, STEP * q : STEP * q + fields] = entry
            count = jnp.sum(jnp.where(lane_id == first + f, live, 0).astype(jnp.float32), 1, keepdims=True)
            slots_ref[row : row + 1, STEP * K : STEP * K + 1] = count.astype(jnp.int32)
            for c in range(3):
                block = coeff_ref[first + f, c].astype(jnp.float32)
                picked = jnp.sum(jnp.where(row_id == tile, block, 0.0), 0, keepdims=True)
                weights_ref[row : row + 1, STEP * c : STEP * c + NB] = picked


def find_slot(slots_ref, row, expo):
    live = slots_ref[row, STEP * K]
    base = jnp.int32(0)
    found = jnp.int32(0)
    for q in range(K):
        hit = (q < live) & (slots_ref[row, STEP * q] == expo)
        base = jnp.where(hit, STEP * q, base)
        found = jnp.where(hit, 1, found)
    return found, base


def weight(weights_ref, row, b, row_centred, col_centred):
    flat = weights_ref[row, b] + weights_ref[row, STEP + b] * row_centred
    return flat + weights_ref[row, 2 * STEP + b] * col_centred


def centred_axes(side, oy, ox):
    rows = lax.broadcasted_iota(jnp.int32, (side, 1), 0) + oy
    cols = lax.broadcasted_iota(jnp.int32, (1, side), 1) + ox
    return (
        (2 * rows + 1 - side).astype(jnp.float32) / side,
        (2 * cols + 1 - side).astype(jnp.float32) / side,
    )


def diagonal(side, by):
    apart = lax.broadcasted_iota(jnp.int32, (side, side), 1) - lax.broadcasted_iota(
        jnp.int32, (side, side), 0
    )
    return (apart == by).astype(jnp.float32).astype(jnp.bfloat16)


def dot(a, b):
    return jnp.dot(a, b, preferred_element_type=jnp.float32)


def settle_contribution(image, oy, ox, pred_ref, f):
    side = image.shape[0]
    across = dot(image, diagonal(side, ox)).astype(jnp.bfloat16)
    pred_ref[f] = pred_ref[f] + dot(diagonal(side, -oy), across)


def contribution(slots_ref, weights_ref, basis_ref, row, base, place, image):
    side = image.shape[0]
    kinds = basis_ref.shape[0] // 2
    row_centred, col_centred = centred_axes(
        side, slots_ref[row, base + 1], slots_ref[row, base + 2]
    )
    total = jnp.zeros((side, side), jnp.float32)
    chosen = [slots_ref[row, base + HEAD + b] for b in range(NB)]
    half_blurs = dot(jnp.concatenate([basis_ref[k] for k in chosen], 0), image).astype(jnp.bfloat16)
    for b in range(NB):
        blurred = dot(half_blurs[b * side : (b + 1) * side], basis_ref[kinds + chosen[b]])
        total = total + weight(weights_ref, place, b, row_centred, col_centred) * blurred
    return total.astype(jnp.bfloat16)


def bring_residual(image, oy, ox):
    side = image.shape[0]
    across = dot(image, diagonal(side, -ox)).astype(jnp.bfloat16)
    return dot(diagonal(side, oy), across)


def adjoint_term(slots_ref, weights_ref, basis_ref, row, base, place, moved):
    side = moved.shape[0]
    kinds = basis_ref.shape[0] // 2
    row_centred, col_centred = centred_axes(
        side, slots_ref[row, base + 1], slots_ref[row, base + 2]
    )
    total = jnp.zeros((side, side), jnp.float32)
    for b in range(NB):
        k = slots_ref[row, base + HEAD + b]
        w = weight(weights_ref, place, b, row_centred, col_centred)
        back_half = dot(basis_ref[k], (w * moved).astype(jnp.bfloat16)).astype(jnp.bfloat16)
        total = total + dot(back_half, basis_ref[kinds + k])
    return total


def source_of(own, move):
    distance, parity = move
    return own + jnp.where(lax.rem(own // distance, 2) == parity, distance, -distance)


def flipped(x, axis, move):
    distance, parity = move
    length = lax.axis_size(axis)
    firsts = [i for i in range(length - distance) if (i // distance) % 2 == parity]
    pairs = [(i, i + distance) for i in firsts] + [(i + distance, i) for i in firsts]
    return lax.ppermute(x, axis, pairs)


def relay_onward(near, count):
    length = lax.axis_size("tile")
    pairs = [(i, i + 2) for i in range(0, length - 2, 2)]
    pairs += [(i, i - 2) for i in range(3, length, 2)]
    return lax.ppermute(near[1, 0][:count], "tile", pairs)


def relay_across(near, count):
    own = lax.axis_index("tile")
    first = lax.rem(own, 2) == lax.rem(own // 2, 2)
    image = jnp.where(first, near[2, 0][count:], near[2, 1][count:])
    return flipped(image, "tile", (1, 0))


def gather_live(sizes, moves, backward, slots_ref, images, list_ref, held_ref):
    tiles, filters, local = sizes
    own = lax.axis_index("tile")
    live = jnp.int32(0)
    for (move, f_first), image_ref in zip(moves, images):
        far = own if move is None else source_of(own, move)
        inside = jnp.where((far >= 0) & (far < tiles), 1, 0)
        here, there = REACH * local, jnp.clip(far - own + REACH, 0, 2 * REACH) * local
        tile_at, expo_at = (here, there) if backward else (there, here)
        expo = far if backward else own
        for f in range(f_first, f_first + image_ref.shape[0]):
            found, base = find_slot(slots_ref, tile_at + f, expo)
            found = found * inside

            @pl.when(found == 1)
            def _():
                list_ref[0, live] = f
                list_ref[1, live] = tile_at + f
                list_ref[2, live] = base
                list_ref[3, live] = expo_at + f
                held_ref[live] = image_ref[f - f_first]

            live = live + found
    return live


def forward_slots(sizes, moves, slots_ref, weights_ref, basis_ref, images, pred_ref, scratch):
    list_ref, held_ref, ready_ref = scratch
    live = gather_live(sizes, moves, False, slots_ref, images, list_ref, held_ref)

    @pl.when(live > 0)
    def _():
        def blur(n):
            ready_ref[...] = contribution(
                slots_ref,
                weights_ref,
                basis_ref,
                list_ref[1, n],
                list_ref[2, n],
                list_ref[3, n],
                held_ref[n],
            )

        def settle(n):
            row, base = list_ref[1, n], list_ref[2, n]
            oy, ox = slots_ref[row, base + 1], slots_ref[row, base + 2]
            settle_contribution(ready_ref[...], oy, ox, pred_ref, list_ref[0, n])

        def one(n, carry):
            settle(n - 1)
            blur(n)
            return carry

        blur(0)
        lax.fori_loop(1, live, one, 0)
        settle(live - 1)


def backward_slots(sizes, moves, slots_ref, weights_ref, basis_ref, images, grad_ref, scratch):
    list_ref, held_ref, ready_ref = scratch
    live = gather_live(sizes, moves, True, slots_ref, images, list_ref, held_ref)

    @pl.when(live > 0)
    def _():
        def bring(n):
            row, base = list_ref[1, n], list_ref[2, n]
            return bring_residual(held_ref[n], slots_ref[row, base + 1], slots_ref[row, base + 2])

        def take(n):
            f = list_ref[0, n]
            grad_ref[f] = grad_ref[f] + adjoint_term(
                slots_ref,
                weights_ref,
                basis_ref,
                list_ref[1, n],
                list_ref[2, n],
                list_ref[3, n],
                ready_ref[...],
            )

        def one(n, carry):
            following = bring(n)
            take(n - 1)
            ready_ref[...] = following
            return carry

        ready_ref[...] = bring(0)
        lax.fori_loop(1, live, one, 0)
        take(live - 1)


def prepare(sizes, inter_ref, counts_ref, coeff_ref, taps_ref, *refs):
    slots_ref, weights_ref, forth_ref, back_ref, lines_ref = refs
    fill_tables(sizes, inter_ref, counts_ref, coeff_ref, slots_ref, weights_ref)
    build_basis(taps_ref, lines_ref, forth_ref, False)
    build_basis(taps_ref, lines_ref, back_ref, True)


def forward_own(sizes, slots_ref, weights_ref, basis_ref, image_ref, *refs):
    pred_ref, *scratch = refs
    pred_ref[...] = jnp.zeros_like(pred_ref)
    forward_slots(sizes, [(None, 0)], slots_ref, weights_ref, basis_ref, [image_ref], pred_ref, scratch)


def forward_next(sizes, moves, slots_ref, weights_ref, basis_ref, *refs):
    images, (before_ref, pred_ref, *scratch) = refs[: len(moves)], refs[len(moves) :]
    del before_ref
    forward_slots(sizes, moves, slots_ref, weights_ref, basis_ref, images, pred_ref, scratch)


def forward_last(sizes, moves, slots_ref, weights_ref, basis_ref, *refs):
    images, refs = refs[: len(moves)], refs[len(moves) :]
    before_ref, observed_ref, inv_ref, pred_ref, resid_ref, *scratch = refs
    del before_ref
    forward_slots(sizes, moves, slots_ref, weights_ref, basis_ref, images, pred_ref, scratch)
    for f in range(observed_ref.shape[0]):
        gap = observed_ref[f].astype(jnp.float32) - pred_ref[f]
        resid_ref[f] = (inv_ref[f].astype(jnp.float32) * gap).astype(jnp.bfloat16)


def subtract_prior(sizes, prec_ref, sample_ref, others, grad_ref):
    tiles, filters, local = sizes
    part = lax.axis_index("filt")
    parts = filters // local
    first = part * local
    for f in range(local):
        grad = grad_ref[f]
        for g in range(local):
            grad = grad - prec_ref[first + f, first + g] * sample_ref[g]
        for r in range(1, parts):
            source = lax.rem(part + parts - r, parts) * local
            for g in range(local):
                far = others[r - 1][g].astype(jnp.float32)
                grad = grad - prec_ref[first + f, source + g] * far
        grad_ref[f] = grad


def backward_own(sizes, samples, slots_ref, weights_ref, basis_ref, image_ref, *refs):
    scale_ref, *refs = refs
    noises, (grad_ref, *refs) = refs[:samples], refs[samples:]
    turns, scratch = refs[:samples], refs[samples:]
    for noise_ref, turn_ref in zip(noises, turns):
        turn_ref[...] = scale_ref[...] * noise_ref[...].astype(jnp.float32)
    grad_ref[...] = jnp.zeros_like(grad_ref)
    backward_slots(
        sizes, [(None, 0)], slots_ref, weights_ref, basis_ref, [image_ref], grad_ref, scratch
    )


def backward_next(sizes, moves, slots_ref, weights_ref, basis_ref, *refs):
    images, (before_ref, grad_ref, *scratch) = refs[: len(moves)], refs[len(moves) :]
    del before_ref
    backward_slots(sizes, moves, slots_ref, weights_ref, basis_ref, images, grad_ref, scratch)


def backward_last(sizes, moves, slots_ref, weights_ref, prec_ref, basis_ref, *refs):
    parts = sizes[1] // sizes[2]
    images, (before_ref, sample_ref, *refs) = refs[: len(moves)], refs[len(moves) :]
    others, (grad_ref, *scratch) = refs[: parts - 1], refs[parts - 1 :]
    del before_ref
    subtract_prior(sizes, prec_ref, sample_ref, others, grad_ref)
    backward_slots(sizes, moves, slots_ref, weights_ref, basis_ref, images, grad_ref, scratch)


def body(
    sky_mean,
    sky_log_scale,
    noise_draw,
    observed,
    inv_var,
    intersections,
    counts,
    kernels,
    psf_coeffs,
    prior_prec,
):
    side = sky_mean.shape[2]
    local = sky_mean.shape[1]
    tiles, filters = counts.shape
    sizes = (tiles, filters, local)
    kinds = kernels.shape[0]
    early, far_odd = [(1, 0), (2, 0), (2, 1)], (1, 1)
    early_moves = [(move, 0) for move in early]
    onward = local - local // 3
    last_moves = [(far_odd, 0)] + ([(far_odd, onward)] if onward < local else [])

    def last_images(near):
        across = [relay_across(near, onward)] if onward < local else []
        return [relay_onward(near, onward), *across]

    samples = lax.axis_size("mc")
    parts = lax.axis_size("filt")

    scale_map = jnp.exp(sky_log_scale[0])
    noise = noise_draw[0, 0]
    eps_float = noise.astype(jnp.float32)
    sample = sky_mean[0] + scale_map * eps_float
    sample_b = sample.astype(jnp.bfloat16)
    taps = kernels.reshape(2 * kinds, kernels.shape[2])

    image_f32 = jax.ShapeDtypeStruct((local, side, side), jnp.float32)
    image_b16 = jax.ShapeDtypeStruct((local, side, side), jnp.bfloat16)
    basis_type = jax.ShapeDtypeStruct((2 * kinds, side, side), jnp.bfloat16)
    cost = pl.CostEstimate(
        flops=2 * NB * 4 * side**3, bytes_accessed=8 * local * side * side, transcendentals=0
    )
    lines = pltpu.VMEM((2, 2 * kinds, side), jnp.float32)

    def slot_scratch(groups, ready):
        return [
            pltpu.SMEM((4, groups * local), jnp.int32),
            pltpu.VMEM((groups * local, side, side), jnp.bfloat16),
            pltpu.VMEM((side, side), ready),
        ]

    def call(kernel, name, outs, smem, vmem, scratch, aliases={}):
        return pl.pallas_call(
            kernel,
            out_shape=outs,
            in_specs=[SMEM] * len(smem) + [VMEM] * len(vmem),
            out_specs=[VMEM] * len(outs),
            scratch_shapes=scratch,
            input_output_aliases=aliases,
            compiler_params=pltpu.CompilerParams(vmem_limit_bytes=VMEM_BYTES),
            cost_estimate=cost,
            name=name,
        )(*smem, *vmem)

    near = {move: flipped(sample_b, "tile", move) for move in early}
    other_noise = [rotated(noise, "mc", r) for r in range(1, samples)]
    rows = -(-(2 * REACH + 1) * local // 8) * 8
    slots, weights, forth, back = call(
        functools.partial(prepare, sizes),
        "prepare",
        [
            jax.ShapeDtypeStruct((rows, LANES), jnp.int32),
            jax.ShapeDtypeStruct((rows, LANES), jnp.float32),
            basis_type,
            basis_type,
        ],
        (),
        (intersections.transpose(1, 2, 0, 3), counts, psf_coeffs.transpose(1, 3, 0, 2), taps),
        [lines],
    )
    tables = (slots, weights)
    (pred,) = call(
        functools.partial(forward_own, sizes),
        "forward_own",
        [image_f32],
        tables,
        (forth, sample_b),
        slot_scratch(1, jnp.bfloat16),
    )
    near[1, 0], pred = lax.optimization_barrier((near[1, 0], pred))
    near_last = last_images(near)
    (pred,) = call(
        functools.partial(forward_next, sizes, early_moves),
        "forward_next",
        [image_f32],
        tables,
        (forth, *[near[move] for move in early], pred),
        slot_scratch(len(early), jnp.bfloat16),
        {len(tables) + 1 + len(early): 0},
    )
    _, residual = call(
        functools.partial(forward_last, sizes, last_moves),
        "forward_last",
        [image_f32, image_b16],
        tables,
        (forth, *near_last, pred, observed[0], inv_var[0]),
        slot_scratch(1, jnp.bfloat16),
        {len(tables) + 1 + len(near_last): 0},
    )
    near_resid = {move: flipped(residual, "tile", move) for move in [*early, far_odd]}
    late_b, residual = lax.optimization_barrier((sample_b, residual))
    other_samples = [rotated(late_b, "filt", r) for r in range(1, parts)]
    grad, turn, *other_turns = call(
        functools.partial(backward_own, sizes, samples),
        "backward_own",
        [image_f32] * (1 + samples),
        tables,
        (back, residual, scale_map, noise, *other_noise),
        slot_scratch(1, jnp.float32),
    )
    (grad,) = call(
        functools.partial(backward_next, sizes, early_moves),
        "backward_next",
        [image_f32],
        tables,
        (back, *[near_resid[move] for move in early], grad),
        slot_scratch(len(early), jnp.float32),
        {len(tables) + 1 + len(early): 0},
    )
    (grad,) = call(
        functools.partial(backward_last, sizes, [(far_odd, 0)]),
        "backward_last",
        [image_f32],
        tables + (prior_prec,),
        (back, near_resid[far_odd], grad, sample, *other_samples),
        slot_scratch(1, jnp.float32),
        {len(tables) + 3: 0},
    )
    mean_sum = grad
    scale_sum = grad * turn
    for r in range(1, samples):
        other_grad = rotated(grad, "mc", r)
        mean_sum = mean_sum + other_grad
        scale_sum = scale_sum + other_grad * other_turns[r - 1]
    return ((mean_sum / samples)[None], (scale_sum / samples + 1.0)[None])

def solution(mesh):
    placed = (
        P("tile", "filt", None, None),
        P("tile", "filt", None, None),
        P("mc", "tile", "filt", None, None),
        P("tile", "filt", None, None),
        P("tile", "filt", None, None),
        P(),
        P(),
        P(),
        P(),
        P(),
    )
    return jax.shard_map(
        body,
        mesh=mesh,
        in_specs=placed,
        out_specs=(P("tile", "filt", None, None), P("tile", "filt", None, None)),
        check_vma=False,
    )
```

```python
import functools

import jax
import jax.numpy as jnp
from jax import lax
from jax.experimental import pallas as pl
from jax.experimental.pallas import tpu as pltpu
from jax.sharding import PartitionSpec as P

NB = 6
K = 3
REACH = 2
HEAD = 3
STEP = 16
LANES = 128
VMEM_BYTES = 16 * 1024 * 1024
VMEM = pl.BlockSpec(memory_space=pltpu.VMEM)
SMEM = pl.BlockSpec(memory_space=pltpu.SMEM)


def shifted(x, axis, by):
    length = lax.axis_size(axis)
    pairs = [(i, i + by) for i in range(length) if 0 <= i + by < length]
    return lax.ppermute(x, axis, pairs)


def rotated(x, axis, by):
    length = lax.axis_size(axis)
    return lax.ppermute(x, axis, [(i, (i + by) % length) for i in range(length)])


def build_basis(taps_ref, lines_ref, basis_ref, adjoint):
    kinds, side = basis_ref.shape[0] // 2, basis_ref.shape[1]
    count = taps_ref.shape[1]
    half = (count - 1) // 2
    taps = taps_ref[...].astype(jnp.bfloat16)
    tap = lax.broadcasted_iota(jnp.int32, (count, side), 0)
    lane = lax.broadcasted_iota(jnp.int32, (count, side), 1)
    lane = jnp.where(lane < side // 2, lane, lane - side)
    plain = (lane == half - tap).astype(jnp.float32).astype(jnp.bfloat16)
    turned = (lane == tap - half).astype(jnp.float32).astype(jnp.bfloat16)
    lines_ref[0] = dot(taps, turned if adjoint else plain)
    lines_ref[1] = dot(taps, plain if adjoint else turned)
    apart = lax.broadcasted_iota(jnp.int32, (side, side), 0) - lax.broadcasted_iota(
        jnp.int32, (side, side), 1
    )
    band = jnp.abs(apart) <= half

    def one(k, carry):
        for c in range(2):
            line = jnp.broadcast_to(lines_ref[c, pl.ds(2 * k + c, 1), :], (side, side))
            rows = pltpu.roll(line, 0, 1, stride=1, stride_axis=0)
            basis_ref[c * kinds + k] = jnp.where(band, rows, 0.0).astype(jnp.bfloat16)
        return carry

    lax.fori_loop(0, kinds, one, 0)


def fill_tables(sizes, inter_ref, counts_ref, coeff_ref, slots_ref, weights_ref):
    tiles, filters, local = sizes
    fields = inter_ref.shape[3]
    own = lax.axis_index("tile")
    first = lax.axis_index("filt") * local
    row_id = lax.broadcasted_iota(jnp.int32, (tiles, NB), 0)
    lane_id = lax.broadcasted_iota(jnp.int32, (1, filters), 1)
    for w in range(2 * REACH + 1):
        tile = jnp.clip(own + w - REACH, 0, tiles - 1)
        live = counts_ref[pl.ds(tile, 1), :]
        for f in range(local):
            row = w * local + f
            for q in range(K):
                entry = inter_ref[first + f, q, pl.ds(tile, 1), :]
                slots_ref[row : row + 1, STEP * q : STEP * q + fields] = entry
            count = jnp.sum(jnp.where(lane_id == first + f, live, 0).astype(jnp.float32), 1, keepdims=True)
            slots_ref[row : row + 1, STEP * K : STEP * K + 1] = count.astype(jnp.int32)
            for c in range(3):
                block = coeff_ref[first + f, c].astype(jnp.float32)
                picked = jnp.sum(jnp.where(row_id == tile, block, 0.0), 0, keepdims=True)
                weights_ref[row : row + 1, STEP * c : STEP * c + NB] = picked


def find_slot(slots_ref, row, expo):
    live = slots_ref[row, STEP * K]
    base = jnp.int32(0)
    found = jnp.int32(0)
    for q in range(K):
        hit = (q < live) & (slots_ref[row, STEP * q] == expo)
        base = jnp.where(hit, STEP * q, base)
        found = jnp.where(hit, 1, found)
    return found, base


def weight(weights_ref, row, b, row_centred, col_centred):
    flat = weights_ref[row, b] + weights_ref[row, STEP + b] * row_centred
    return flat + weights_ref[row, 2 * STEP + b] * col_centred


def centred_axes(side, oy, ox):
    rows = lax.broadcasted_iota(jnp.int32, (side, 1), 0) + oy
    cols = lax.broadcasted_iota(jnp.int32, (1, side), 1) + ox
    return (
        (2 * rows + 1 - side).astype(jnp.float32) / side,
        (2 * cols + 1 - side).astype(jnp.float32) / side,
    )


def moved_by(image, down, across):
    side = image.shape[0]
    turned = pltpu.roll(image, lax.rem(across + side, side), 1)
    turned = pltpu.roll(turned, lax.rem(down + side, side), 0)
    row = lax.broadcasted_iota(jnp.int32, (side, side), 0) - down
    col = lax.broadcasted_iota(jnp.int32, (side, side), 1) - across
    inside = (row >= 0) & (row < side) & (col >= 0) & (col < side)
    return jnp.where(inside, turned, 0.0)


def dot(a, b):
    return jnp.dot(a, b, preferred_element_type=jnp.float32)


def contribution(slots_ref, weights_ref, basis_ref, row, base, place, image):
    side = image.shape[0]
    kinds = basis_ref.shape[0] // 2
    row_centred, col_centred = centred_axes(
        side, slots_ref[row, base + 1], slots_ref[row, base + 2]
    )
    total = jnp.zeros((side, side), jnp.float32)
    chosen = [slots_ref[row, base + HEAD + b] for b in range(NB)]
    half_blurs = dot(jnp.concatenate([basis_ref[k] for k in chosen], 0), image).astype(jnp.bfloat16)
    for b in range(NB):
        blurred = dot(half_blurs[b * side : (b + 1) * side], basis_ref[kinds + chosen[b]])
        total = total + weight(weights_ref, place, b, row_centred, col_centred) * blurred
    return total.astype(jnp.bfloat16)


def adjoint_term(slots_ref, weights_ref, basis_ref, row, base, place, moved):
    side = moved.shape[0]
    kinds = basis_ref.shape[0] // 2
    row_centred, col_centred = centred_axes(
        side, slots_ref[row, base + 1], slots_ref[row, base + 2]
    )
    total = jnp.zeros((side, side), jnp.float32)
    for b in range(NB):
        k = slots_ref[row, base + HEAD + b]
        w = weight(weights_ref, place, b, row_centred, col_centred)
        back_half = dot(basis_ref[k], (w * moved).astype(jnp.bfloat16)).astype(jnp.bfloat16)
        total = total + dot(back_half, basis_ref[kinds + k])
    return total


def source_of(own, move):
    distance, parity = move
    return own + jnp.where(lax.rem(own // distance, 2) == parity, distance, -distance)


def flipped(x, axis, move):
    distance, parity = move
    length = lax.axis_size(axis)
    firsts = [i for i in range(length - distance) if (i // distance) % 2 == parity]
    pairs = [(i, i + distance) for i in firsts] + [(i + distance, i) for i in firsts]
    return lax.ppermute(x, axis, pairs)


def relay_onward(near, count):
    length = lax.axis_size("tile")
    pairs = [(i, i + 2) for i in range(0, length - 2, 2)]
    pairs += [(i, i - 2) for i in range(3, length, 2)]
    return lax.ppermute(near[1, 0][:count], "tile", pairs)


def relay_across(near, count):
    own = lax.axis_index("tile")
    first = lax.rem(own, 2) == lax.rem(own // 2, 2)
    image = jnp.where(first, near[2, 0][count:], near[2, 1][count:])
    return flipped(image, "tile", (1, 0))


def gather_live(sizes, moves, backward, slots_ref, images, list_ref, held_ref):
    tiles, filters, local = sizes
    own = lax.axis_index("tile")
    live = jnp.int32(0)
    for (move, f_first), image_ref in zip(moves, images):
        far = own if move is None else source_of(own, move)
        inside = jnp.where((far >= 0) & (far < tiles), 1, 0)
        here, there = REACH * local, jnp.clip(far - own + REACH, 0, 2 * REACH) * local
        tile_at, expo_at = (here, there) if backward else (there, here)
        expo = far if backward else own
        for f in range(f_first, f_first + image_ref.shape[0]):
            found, base = find_slot(slots_ref, tile_at + f, expo)
            found = found * inside

            @pl.when(found == 1)
            def _():
                list_ref[0, live] = f
                list_ref[1, live] = tile_at + f
                list_ref[2, live] = base
                list_ref[3, live] = expo_at + f
                held_ref[live] = image_ref[f - f_first]

            live = live + found
    return live


def forward_slots(sizes, moves, slots_ref, weights_ref, basis_ref, images, pred_ref, scratch):
    list_ref, held_ref, ready_ref = scratch
    live = gather_live(sizes, moves, False, slots_ref, images, list_ref, held_ref)

    @pl.when(live > 0)
    def _():
        def blur(n):
            ready_ref[...] = contribution(
                slots_ref,
                weights_ref,
                basis_ref,
                list_ref[1, n],
                list_ref[2, n],
                list_ref[3, n],
                held_ref[n],
            )

        def settle(n):
            row, base = list_ref[1, n], list_ref[2, n]
            oy, ox = slots_ref[row, base + 1], slots_ref[row, base + 2]
            f = list_ref[0, n]
            pred_ref[f] = pred_ref[f] + moved_by(ready_ref[...].astype(jnp.float32), oy, ox)

        def one(n, carry):
            settle(n - 1)
            blur(n)
            return carry

        blur(0)
        lax.fori_loop(1, live, one, 0)
        settle(live - 1)


def backward_slots(sizes, moves, slots_ref, weights_ref, basis_ref, images, grad_ref, scratch):
    list_ref, held_ref, ready_ref = scratch
    live = gather_live(sizes, moves, True, slots_ref, images, list_ref, held_ref)

    @pl.when(live > 0)
    def _():
        def bring(n):
            row, base = list_ref[1, n], list_ref[2, n]
            oy, ox = slots_ref[row, base + 1], slots_ref[row, base + 2]
            return moved_by(held_ref[n].astype(jnp.float32), -oy, -ox)

        def take(n):
            f = list_ref[0, n]
            grad_ref[f] = grad_ref[f] + adjoint_term(
                slots_ref,
                weights_ref,
                basis_ref,
                list_ref[1, n],
                list_ref[2, n],
                list_ref[3, n],
                ready_ref[...],
            )

        def one(n, carry):
            following = bring(n)
            take(n - 1)
            ready_ref[...] = following
            return carry

        ready_ref[...] = bring(0)
        lax.fori_loop(1, live, one, 0)
        take(live - 1)


def prepare(sizes, inter_ref, counts_ref, coeff_ref, taps_ref, *refs):
    slots_ref, weights_ref, forth_ref, back_ref, lines_ref = refs
    fill_tables(sizes, inter_ref, counts_ref, coeff_ref, slots_ref, weights_ref)
    build_basis(taps_ref, lines_ref, forth_ref, False)
    build_basis(taps_ref, lines_ref, back_ref, True)


def forward_own(sizes, slots_ref, weights_ref, basis_ref, image_ref, *refs):
    pred_ref, *scratch = refs
    pred_ref[...] = jnp.zeros_like(pred_ref)
    forward_slots(sizes, [(None, 0)], slots_ref, weights_ref, basis_ref, [image_ref], pred_ref, scratch)


def forward_next(sizes, moves, slots_ref, weights_ref, basis_ref, *refs):
    images, (before_ref, pred_ref, *scratch) = refs[: len(moves)], refs[len(moves) :]
    del before_ref
    forward_slots(sizes, moves, slots_ref, weights_ref, basis_ref, images, pred_ref, scratch)


def forward_last(sizes, moves, slots_ref, weights_ref, basis_ref, *refs):
    images, refs = refs[: len(moves)], refs[len(moves) :]
    before_ref, observed_ref, inv_ref, pred_ref, resid_ref, *scratch = refs
    del before_ref
    forward_slots(sizes, moves, slots_ref, weights_ref, basis_ref, images, pred_ref, scratch)
    for f in range(observed_ref.shape[0]):
        gap = observed_ref[f].astype(jnp.float32) - pred_ref[f]
        resid_ref[f] = (inv_ref[f].astype(jnp.float32) * gap).astype(jnp.bfloat16)


def subtract_prior(sizes, prec_ref, sample_ref, others, grad_ref):
    tiles, filters, local = sizes
    part = lax.axis_index("filt")
    parts = filters // local
    first = part * local
    for f in range(local):
        grad = grad_ref[f]
        for g in range(local):
            grad = grad - prec_ref[first + f, first + g] * sample_ref[g]
        for r in range(1, parts):
            source = lax.rem(part + parts - r, parts) * local
            for g in range(local):
                far = others[r - 1][g].astype(jnp.float32)
                grad = grad - prec_ref[first + f, source + g] * far
        grad_ref[f] = grad


def backward_own(sizes, moves, samples, slots_ref, weights_ref, basis_ref, *refs):
    images, (scale_ref, *refs) = refs[: len(moves)], refs[len(moves) :]
    noises, (grad_ref, *refs) = refs[:samples], refs[samples:]
    turns, scratch = refs[:samples], refs[samples:]
    for noise_ref, turn_ref in zip(noises, turns):
        turn_ref[...] = scale_ref[...] * noise_ref[...].astype(jnp.float32)
    grad_ref[...] = jnp.zeros_like(grad_ref)
    backward_slots(sizes, moves, slots_ref, weights_ref, basis_ref, images, grad_ref, scratch)


def backward_next(sizes, moves, slots_ref, weights_ref, basis_ref, *refs):
    images, (before_ref, grad_ref, *scratch) = refs[: len(moves)], refs[len(moves) :]
    del before_ref
    backward_slots(sizes, moves, slots_ref, weights_ref, basis_ref, images, grad_ref, scratch)


def backward_last(sizes, moves, slots_ref, weights_ref, prec_ref, basis_ref, *refs):
    parts = sizes[1] // sizes[2]
    images, (before_ref, sample_ref, *refs) = refs[: len(moves)], refs[len(moves) :]
    others, (grad_ref, *scratch) = refs[: parts - 1], refs[parts - 1 :]
    del before_ref
    subtract_prior(sizes, prec_ref, sample_ref, others, grad_ref)
    backward_slots(sizes, moves, slots_ref, weights_ref, basis_ref, images, grad_ref, scratch)


def body(
    sky_mean,
    sky_log_scale,
    noise_draw,
    observed,
    inv_var,
    intersections,
    counts,
    kernels,
    psf_coeffs,
    prior_prec,
):
    side = sky_mean.shape[2]
    local = sky_mean.shape[1]
    tiles, filters = counts.shape
    sizes = (tiles, filters, local)
    kinds = kernels.shape[0]
    early, far_odd = [(1, 0), (2, 0), (2, 1)], (1, 1)
    early_moves = [(move, 0) for move in early]
    onward = local - local // 3
    last_moves = [(far_odd, 0)] + ([(far_odd, onward)] if onward < local else [])

    def last_images(near):
        across = [relay_across(near, onward)] if onward < local else []
        return [relay_onward(near, onward), *across]

    samples = lax.axis_size("mc")
    parts = lax.axis_size("filt")

    scale_map = jnp.exp(sky_log_scale[0])
    noise = noise_draw[0, 0]
    eps_float = noise.astype(jnp.float32)
    sample = sky_mean[0] + scale_map * eps_float
    sample_b = sample.astype(jnp.bfloat16)
    taps = kernels.reshape(2 * kinds, kernels.shape[2])

    image_f32 = jax.ShapeDtypeStruct((local, side, side), jnp.float32)
    image_b16 = jax.ShapeDtypeStruct((local, side, side), jnp.bfloat16)
    basis_type = jax.ShapeDtypeStruct((2 * kinds, side, side), jnp.bfloat16)
    cost = pl.CostEstimate(
        flops=2 * NB * 4 * side**3, bytes_accessed=8 * local * side * side, transcendentals=0
    )
    lines = pltpu.VMEM((2, 2 * kinds, side), jnp.float32)

    def slot_scratch(groups, ready):
        return [
            pltpu.SMEM((4, groups * local), jnp.int32),
            pltpu.VMEM((groups * local, side, side), jnp.bfloat16),
            pltpu.VMEM((side, side), ready),
        ]

    def call(kernel, name, outs, smem, vmem, scratch, aliases={}):
        return pl.pallas_call(
            kernel,
            out_shape=outs,
            in_specs=[SMEM] * len(smem) + [VMEM] * len(vmem),
            out_specs=[VMEM] * len(outs),
            scratch_shapes=scratch,
            input_output_aliases=aliases,
            compiler_params=pltpu.CompilerParams(vmem_limit_bytes=VMEM_BYTES),
            cost_estimate=cost,
            name=name,
        )(*smem, *vmem)

    near = {move: flipped(sample_b, "tile", move) for move in early}
    other_noise = [rotated(noise, "mc", r) for r in range(1, samples)]
    rows = -(-(2 * REACH + 1) * local // 8) * 8
    slots, weights, forth, back = call(
        functools.partial(prepare, sizes),
        "prepare",
        [
            jax.ShapeDtypeStruct((rows, LANES), jnp.int32),
            jax.ShapeDtypeStruct((rows, LANES), jnp.float32),
            basis_type,
            basis_type,
        ],
        (),
        (intersections.transpose(1, 2, 0, 3), counts, psf_coeffs.transpose(1, 3, 0, 2), taps),
        [lines],
    )
    tables = (slots, weights)
    (pred,) = call(
        functools.partial(forward_own, sizes),
        "forward_own",
        [image_f32],
        tables,
        (forth, sample_b),
        slot_scratch(1, jnp.bfloat16),
    )
    near[1, 0], pred = lax.optimization_barrier((near[1, 0], pred))
    near_last = last_images(near)
    (pred,) = call(
        functools.partial(forward_next, sizes, early_moves),
        "forward_next",
        [image_f32],
        tables,
        (forth, *[near[move] for move in early], pred),
        slot_scratch(len(early), jnp.bfloat16),
        {len(tables) + 1 + len(early): 0},
    )
    _, residual = call(
        functools.partial(forward_last, sizes, last_moves),
        "forward_last",
        [image_f32, image_b16],
        tables,
        (forth, *near_last, pred, observed[0], inv_var[0]),
        slot_scratch(1, jnp.bfloat16),
        {len(tables) + 1 + len(near_last): 0},
    )
    near_resid = {move: flipped(residual, "tile", move) for move in [*early, far_odd]}
    late_b, residual = lax.optimization_barrier((sample_b, residual))
    other_samples = [rotated(late_b, "filt", r) for r in range(1, parts)]
    grad, turn, *other_turns = call(
        functools.partial(backward_own, sizes, [(None, 0), early_moves[0]], samples),
        "backward_own",
        [image_f32] * (1 + samples),
        tables,
        (back, residual, near_resid[early[0]], scale_map, noise, *other_noise),
        slot_scratch(2, jnp.float32),
    )
    (grad,) = call(
        functools.partial(backward_next, sizes, early_moves[1:]),
        "backward_next",
        [image_f32],
        tables,
        (back, *[near_resid[move] for move in early[1:]], grad),
        slot_scratch(len(early) - 1, jnp.float32),
        {len(tables) + len(early): 0},
    )
    (grad,) = call(
        functools.partial(backward_last, sizes, [(far_odd, 0)]),
        "backward_last",
        [image_f32],
        tables + (prior_prec,),
        (back, near_resid[far_odd], grad, sample, *other_samples),
        slot_scratch(1, jnp.float32),
        {len(tables) + 3: 0},
    )
    mean_sum = grad
    scale_sum = grad * turn
    for r in range(1, samples):
        other_grad = rotated(grad, "mc", r)
        mean_sum = mean_sum + other_grad
        scale_sum = scale_sum + other_grad * other_turns[r - 1]
    return ((mean_sum / samples)[None], (scale_sum / samples + 1.0)[None])

def solution(mesh):
    placed = (
        P("tile", "filt", None, None),
        P("tile", "filt", None, None),
        P("mc", "tile", "filt", None, None),
        P("tile", "filt", None, None),
        P("tile", "filt", None, None),
        P(),
        P(),
        P(),
        P(),
        P(),
    )
    return jax.shard_map(
        body,
        mesh=mesh,
        in_specs=placed,
        out_specs=(P("tile", "filt", None, None), P("tile", "filt", None, None)),
        check_vma=False,
    )
```

```python
import functools

import jax
import jax.numpy as jnp
from jax import lax
from jax.experimental import pallas as pl
from jax.experimental.pallas import tpu as pltpu
from jax.sharding import PartitionSpec as P

NB = 6
K = 3
REACH = 2
HEAD = 3
STEP = 16
LANES = 128
VMEM_BYTES = 16 * 1024 * 1024
VMEM = pl.BlockSpec(memory_space=pltpu.VMEM)
SMEM = pl.BlockSpec(memory_space=pltpu.SMEM)


def shifted(x, axis, by):
    length = lax.axis_size(axis)
    pairs = [(i, i + by) for i in range(length) if 0 <= i + by < length]
    return lax.ppermute(x, axis, pairs)


def rotated(x, axis, by):
    length = lax.axis_size(axis)
    return lax.ppermute(x, axis, [(i, (i + by) % length) for i in range(length)])


def build_basis(taps_ref, lines_ref, basis_ref, adjoint):
    kinds, side = basis_ref.shape[0] // 2, basis_ref.shape[1]
    count = taps_ref.shape[1]
    half = (count - 1) // 2
    taps = taps_ref[...].astype(jnp.bfloat16)
    tap = lax.broadcasted_iota(jnp.int32, (count, side), 0)
    lane = lax.broadcasted_iota(jnp.int32, (count, side), 1)
    lane = jnp.where(lane < side // 2, lane, lane - side)
    plain = (lane == half - tap).astype(jnp.float32).astype(jnp.bfloat16)
    turned = (lane == tap - half).astype(jnp.float32).astype(jnp.bfloat16)
    lines_ref[0] = dot(taps, turned if adjoint else plain)
    lines_ref[1] = dot(taps, plain if adjoint else turned)
    apart = lax.broadcasted_iota(jnp.int32, (side, side), 0) - lax.broadcasted_iota(
        jnp.int32, (side, side), 1
    )
    band = jnp.abs(apart) <= half

    def one(k, carry):
        for c in range(2):
            line = jnp.broadcast_to(lines_ref[c, pl.ds(2 * k + c, 1), :], (side, side))
            rows = pltpu.roll(line, 0, 1, stride=1, stride_axis=0)
            basis_ref[c * kinds + k] = jnp.where(band, rows, 0.0).astype(jnp.bfloat16)
        return carry

    lax.fori_loop(0, kinds, one, 0)


def fill_tables(sizes, inter_ref, counts_ref, coeff_ref, slots_ref, weights_ref):
    tiles, filters, local = sizes
    fields = inter_ref.shape[3]
    own = lax.axis_index("tile")
    first = lax.axis_index("filt") * local
    row_id = lax.broadcasted_iota(jnp.int32, (tiles, NB), 0)
    lane_id = lax.broadcasted_iota(jnp.int32, (1, filters), 1)
    for w in range(2 * REACH + 1):
        tile = jnp.clip(own + w - REACH, 0, tiles - 1)
        live = counts_ref[pl.ds(tile, 1), :]
        for f in range(local):
            row = w * local + f
            for q in range(K):
                entry = inter_ref[first + f, q, pl.ds(tile, 1), :]
                slots_ref[row : row + 1, STEP * q : STEP * q + fields] = entry
            count = jnp.sum(jnp.where(lane_id == first + f, live, 0).astype(jnp.float32), 1, keepdims=True)
            slots_ref[row : row + 1, STEP * K : STEP * K + 1] = count.astype(jnp.int32)
            for c in range(3):
                block = coeff_ref[first + f, c].astype(jnp.float32)
                picked = jnp.sum(jnp.where(row_id == tile, block, 0.0), 0, keepdims=True)
                weights_ref[row : row + 1, STEP * c : STEP * c + NB] = picked


def find_slot(slots_ref, row, expo):
    live = slots_ref[row, STEP * K]
    base = jnp.int32(0)
    found = jnp.int32(0)
    for q in range(K):
        hit = (q < live) & (slots_ref[row, STEP * q] == expo)
        base = jnp.where(hit, STEP * q, base)
        found = jnp.where(hit, 1, found)
    return found, base


def weight(weights_ref, row, b, row_centred, col_centred):
    flat = weights_ref[row, b] + weights_ref[row, STEP + b] * row_centred
    return flat + weights_ref[row, 2 * STEP + b] * col_centred


def centred_axes(side, oy, ox):
    rows = lax.broadcasted_iota(jnp.int32, (side, 1), 0) + oy
    cols = lax.broadcasted_iota(jnp.int32, (1, side), 1) + ox
    return (
        (2 * rows + 1 - side).astype(jnp.float32) / side,
        (2 * cols + 1 - side).astype(jnp.float32) / side,
    )


def moved_by(image, down, across):
    side = image.shape[0]
    turned = pltpu.roll(image, lax.rem(across + side, side), 1)
    turned = pltpu.roll(turned, lax.rem(down + side, side), 0)
    row = lax.broadcasted_iota(jnp.int32, (side, side), 0) - down
    col = lax.broadcasted_iota(jnp.int32, (side, side), 1) - across
    inside = (row >= 0) & (row < side) & (col >= 0) & (col < side)
    return jnp.where(inside, turned, 0.0)


def dot(a, b):
    return jnp.dot(a, b, preferred_element_type=jnp.float32)


def contribution(slots_ref, weights_ref, basis_ref, row, base, place, image):
    side = image.shape[0]
    kinds = basis_ref.shape[0] // 2
    row_centred, col_centred = centred_axes(
        side, slots_ref[row, base + 1], slots_ref[row, base + 2]
    )
    total = jnp.zeros((side, side), jnp.float32)
    chosen = [slots_ref[row, base + HEAD + b] for b in range(NB)]
    half_blurs = dot(jnp.concatenate([basis_ref[k] for k in chosen], 0), image).astype(jnp.bfloat16)
    for b in range(NB):
        blurred = dot(half_blurs[b * side : (b + 1) * side], basis_ref[kinds + chosen[b]])
        total = total + weight(weights_ref, place, b, row_centred, col_centred) * blurred
    return total.astype(jnp.bfloat16)


def adjoint_term(slots_ref, weights_ref, basis_ref, row, base, place, moved):
    side = moved.shape[0]
    kinds = basis_ref.shape[0] // 2
    row_centred, col_centred = centred_axes(
        side, slots_ref[row, base + 1], slots_ref[row, base + 2]
    )
    total = jnp.zeros((side, side), jnp.float32)
    for b in range(NB):
        k = slots_ref[row, base + HEAD + b]
        w = weight(weights_ref, place, b, row_centred, col_centred)
        back_half = dot(basis_ref[k], (w * moved).astype(jnp.bfloat16)).astype(jnp.bfloat16)
        total = total + dot(back_half, basis_ref[kinds + k])
    return total


def source_of(own, move):
    distance, parity = move
    return own + jnp.where(lax.rem(own // distance, 2) == parity, distance, -distance)


def flipped(x, axis, move):
    distance, parity = move
    length = lax.axis_size(axis)
    firsts = [i for i in range(length - distance) if (i // distance) % 2 == parity]
    pairs = [(i, i + distance) for i in firsts] + [(i + distance, i) for i in firsts]
    return lax.ppermute(x, axis, pairs)


def relay_onward(near, count):
    length = lax.axis_size("tile")
    pairs = [(i, i + 2) for i in range(0, length - 2, 2)]
    pairs += [(i, i - 2) for i in range(3, length, 2)]
    return lax.ppermute(near[1, 0][:count], "tile", pairs)


def relay_across(near, count):
    own = lax.axis_index("tile")
    first = lax.rem(own, 2) == lax.rem(own // 2, 2)
    image = jnp.where(first, near[2, 0][count:], near[2, 1][count:])
    return flipped(image, "tile", (1, 0))


def gather_live(sizes, moves, backward, slots_ref, images, list_ref, held_ref):
    tiles, filters, local = sizes
    own = lax.axis_index("tile")
    live = jnp.int32(0)
    for (move, f_first), image_ref in zip(moves, images):
        far = own if move is None else source_of(own, move)
        inside = jnp.where((far >= 0) & (far < tiles), 1, 0)
        here, there = REACH * local, jnp.clip(far - own + REACH, 0, 2 * REACH) * local
        tile_at, expo_at = (here, there) if backward else (there, here)
        expo = far if backward else own
        for f in range(f_first, f_first + image_ref.shape[0]):
            found, base = find_slot(slots_ref, tile_at + f, expo)
            found = found * inside

            @pl.when(found == 1)
            def _():
                list_ref[0, live] = f
                list_ref[1, live] = tile_at + f
                list_ref[2, live] = base
                list_ref[3, live] = expo_at + f
                held_ref[live] = image_ref[f - f_first]

            live = live + found
    return live


def forward_slots(sizes, moves, slots_ref, weights_ref, basis_ref, images, pred_ref, scratch):
    list_ref, held_ref, ready_ref = scratch
    live = gather_live(sizes, moves, False, slots_ref, images, list_ref, held_ref)

    @pl.when(live > 0)
    def _():
        def blur(n):
            ready_ref[...] = contribution(
                slots_ref,
                weights_ref,
                basis_ref,
                list_ref[1, n],
                list_ref[2, n],
                list_ref[3, n],
                held_ref[n],
            )

        def settle(n):
            row, base = list_ref[1, n], list_ref[2, n]
            oy, ox = slots_ref[row, base + 1], slots_ref[row, base + 2]
            f = list_ref[0, n]
            pred_ref[f] = pred_ref[f] + moved_by(ready_ref[...].astype(jnp.float32), oy, ox)

        def one(n, carry):
            settle(n - 1)
            blur(n)
            return carry

        blur(0)
        lax.fori_loop(1, live, one, 0)
        settle(live - 1)


def backward_slots(sizes, moves, slots_ref, weights_ref, basis_ref, images, grad_ref, scratch):
    list_ref, held_ref, ready_ref = scratch
    live = gather_live(sizes, moves, True, slots_ref, images, list_ref, held_ref)

    @pl.when(live > 0)
    def _():
        def bring(n):
            row, base = list_ref[1, n], list_ref[2, n]
            oy, ox = slots_ref[row, base + 1], slots_ref[row, base + 2]
            return moved_by(held_ref[n].astype(jnp.float32), -oy, -ox)

        def take(n):
            f = list_ref[0, n]
            grad_ref[f] = grad_ref[f] + adjoint_term(
                slots_ref,
                weights_ref,
                basis_ref,
                list_ref[1, n],
                list_ref[2, n],
                list_ref[3, n],
                ready_ref[...],
            )

        def one(n, carry):
            following = bring(n)
            take(n - 1)
            ready_ref[...] = following
            return carry

        ready_ref[...] = bring(0)
        lax.fori_loop(1, live, one, 0)
        take(live - 1)


def prepare(sizes, inter_ref, counts_ref, coeff_ref, taps_ref, *refs):
    slots_ref, weights_ref, forth_ref, lines_ref = refs
    fill_tables(sizes, inter_ref, counts_ref, coeff_ref, slots_ref, weights_ref)
    build_basis(taps_ref, lines_ref, forth_ref, False)


def forward_own(sizes, slots_ref, weights_ref, basis_ref, image_ref, *refs):
    pred_ref, *scratch = refs
    pred_ref[...] = jnp.zeros_like(pred_ref)
    forward_slots(sizes, [(None, 0)], slots_ref, weights_ref, basis_ref, [image_ref], pred_ref, scratch)


def forward_next(sizes, moves, slots_ref, weights_ref, basis_ref, *refs):
    images, (before_ref, pred_ref, *scratch) = refs[: len(moves)], refs[len(moves) :]
    del before_ref
    forward_slots(sizes, moves, slots_ref, weights_ref, basis_ref, images, pred_ref, scratch)


def forward_last(sizes, moves, slots_ref, weights_ref, basis_ref, *refs):
    images, refs = refs[: len(moves)], refs[len(moves) :]
    before_ref, observed_ref, inv_ref, pred_ref, resid_ref, *scratch = refs
    del before_ref
    forward_slots(sizes, moves, slots_ref, weights_ref, basis_ref, images, pred_ref, scratch)
    for f in range(observed_ref.shape[0]):
        gap = observed_ref[f].astype(jnp.float32) - pred_ref[f]
        resid_ref[f] = (inv_ref[f].astype(jnp.float32) * gap).astype(jnp.bfloat16)


def subtract_prior(sizes, prec_ref, sample_ref, others, grad_ref):
    tiles, filters, local = sizes
    part = lax.axis_index("filt")
    parts = filters // local
    first = part * local
    for f in range(local):
        grad = grad_ref[f]
        for g in range(local):
            grad = grad - prec_ref[first + f, first + g] * sample_ref[g]
        for r in range(1, parts):
            source = lax.rem(part + parts - r, parts) * local
            for g in range(local):
                far = others[r - 1][g].astype(jnp.float32)
                grad = grad - prec_ref[first + f, source + g] * far
        grad_ref[f] = grad


def backward_own(sizes, samples, slots_ref, weights_ref, taps_ref, image_ref, scale_ref, *refs):
    noises, (grad_ref, basis_ref, *refs) = refs[:samples], refs[samples:]
    turns, (lines_ref, *scratch) = refs[:samples], refs[samples:]
    build_basis(taps_ref, lines_ref, basis_ref, True)
    for noise_ref, turn_ref in zip(noises, turns):
        turn_ref[...] = scale_ref[...] * noise_ref[...].astype(jnp.float32)
    grad_ref[...] = jnp.zeros_like(grad_ref)
    backward_slots(
        sizes, [(None, 0)], slots_ref, weights_ref, basis_ref, [image_ref], grad_ref, scratch
    )


def backward_next(sizes, moves, slots_ref, weights_ref, basis_ref, *refs):
    images, (before_ref, grad_ref, *scratch) = refs[: len(moves)], refs[len(moves) :]
    del before_ref
    backward_slots(sizes, moves, slots_ref, weights_ref, basis_ref, images, grad_ref, scratch)


def backward_last(sizes, moves, slots_ref, weights_ref, prec_ref, basis_ref, *refs):
    parts = sizes[1] // sizes[2]
    images, (before_ref, sample_ref, *refs) = refs[: len(moves)], refs[len(moves) :]
    others, (grad_ref, *scratch) = refs[: parts - 1], refs[parts - 1 :]
    del before_ref
    subtract_prior(sizes, prec_ref, sample_ref, others, grad_ref)
    backward_slots(sizes, moves, slots_ref, weights_ref, basis_ref, images, grad_ref, scratch)


def body(
    sky_mean,
    sky_log_scale,
    noise_draw,
    observed,
    inv_var,
    intersections,
    counts,
    kernels,
    psf_coeffs,
    prior_prec,
):
    side = sky_mean.shape[2]
    local = sky_mean.shape[1]
    tiles, filters = counts.shape
    sizes = (tiles, filters, local)
    kinds = kernels.shape[0]
    early, far_odd = [(1, 0), (2, 0), (2, 1)], (1, 1)
    early_moves = [(move, 0) for move in early]
    onward = local - local // 3
    last_moves = [(far_odd, 0)] + ([(far_odd, onward)] if onward < local else [])

    def last_images(near):
        across = [relay_across(near, onward)] if onward < local else []
        return [relay_onward(near, onward), *across]

    samples = lax.axis_size("mc")
    parts = lax.axis_size("filt")

    scale_map = jnp.exp(sky_log_scale[0])
    noise = noise_draw[0, 0]
    eps_float = noise.astype(jnp.float32)
    sample = sky_mean[0] + scale_map * eps_float
    sample_b = sample.astype(jnp.bfloat16)
    taps = kernels.reshape(2 * kinds, kernels.shape[2])

    image_f32 = jax.ShapeDtypeStruct((local, side, side), jnp.float32)
    image_b16 = jax.ShapeDtypeStruct((local, side, side), jnp.bfloat16)
    basis_type = jax.ShapeDtypeStruct((2 * kinds, side, side), jnp.bfloat16)
    cost = pl.CostEstimate(
        flops=2 * NB * 4 * side**3, bytes_accessed=8 * local * side * side, transcendentals=0
    )
    lines = pltpu.VMEM((2, 2 * kinds, side), jnp.float32)

    def slot_scratch(groups, ready):
        return [
            pltpu.SMEM((4, groups * local), jnp.int32),
            pltpu.VMEM((groups * local, side, side), jnp.bfloat16),
            pltpu.VMEM((side, side), ready),
        ]

    def call(kernel, name, outs, smem, vmem, scratch, aliases={}):
        return pl.pallas_call(
            kernel,
            out_shape=outs,
            in_specs=[SMEM] * len(smem) + [VMEM] * len(vmem),
            out_specs=[VMEM] * len(outs),
            scratch_shapes=scratch,
            input_output_aliases=aliases,
            compiler_params=pltpu.CompilerParams(vmem_limit_bytes=VMEM_BYTES),
            cost_estimate=cost,
            name=name,
        )(*smem, *vmem)

    near = {move: flipped(sample_b, "tile", move) for move in early}
    other_noise = [rotated(noise, "mc", r) for r in range(1, samples)]
    rows = -(-(2 * REACH + 1) * local // 8) * 8
    slots, weights, forth = call(
        functools.partial(prepare, sizes),
        "prepare",
        [
            jax.ShapeDtypeStruct((rows, LANES), jnp.int32),
            jax.ShapeDtypeStruct((rows, LANES), jnp.float32),
            basis_type,
        ],
        (),
        (intersections.transpose(1, 2, 0, 3), counts, psf_coeffs.transpose(1, 3, 0, 2), taps),
        [lines],
    )
    tables = (slots, weights)
    (pred,) = call(
        functools.partial(forward_own, sizes),
        "forward_own",
        [image_f32],
        tables,
        (forth, sample_b),
        slot_scratch(1, jnp.bfloat16),
    )
    near[1, 0], pred = lax.optimization_barrier((near[1, 0], pred))
    near_last = last_images(near)
    (pred,) = call(
        functools.partial(forward_next, sizes, early_moves),
        "forward_next",
        [image_f32],
        tables,
        (forth, *[near[move] for move in early], pred),
        slot_scratch(len(early), jnp.bfloat16),
        {len(tables) + 1 + len(early): 0},
    )
    _, residual = call(
        functools.partial(forward_last, sizes, last_moves),
        "forward_last",
        [image_f32, image_b16],
        tables,
        (forth, *near_last, pred, observed[0], inv_var[0]),
        slot_scratch(1, jnp.bfloat16),
        {len(tables) + 1 + len(near_last): 0},
    )
    near_resid = {move: flipped(residual, "tile", move) for move in [*early, far_odd]}
    late_b, residual = lax.optimization_barrier((sample_b, residual))
    other_samples = [rotated(late_b, "filt", r) for r in range(1, parts)]
    grad, back, turn, *other_turns = call(
        functools.partial(backward_own, sizes, samples),
        "backward_own",
        [image_f32, basis_type] + [image_f32] * samples,
        tables,
        (taps, residual, scale_map, noise, *other_noise),
        [lines] + slot_scratch(1, jnp.float32),
    )
    early = early[::-1]
    (grad,) = call(
        functools.partial(backward_next, sizes, [(move, 0) for move in early]),
        "backward_next",
        [image_f32],
        tables,
        (back, *[near_resid[move] for move in early], grad),
        slot_scratch(len(early), jnp.float32),
        {len(tables) + 1 + len(early): 0},
    )
    (grad,) = call(
        functools.partial(backward_last, sizes, [(far_odd, 0)]),
        "backward_last",
        [image_f32],
        tables + (prior_prec,),
        (back, near_resid[far_odd], grad, sample, *other_samples),
        slot_scratch(1, jnp.float32),
        {len(tables) + 3: 0},
    )
    mean_sum = grad
    scale_sum = grad * turn
    for r in range(1, samples):
        other_grad = rotated(grad, "mc", r)
        mean_sum = mean_sum + other_grad
        scale_sum = scale_sum + other_grad * other_turns[r - 1]
    return ((mean_sum / samples)[None], (scale_sum / samples + 1.0)[None])

def solution(mesh):
    placed = (
        P("tile", "filt", None, None),
        P("tile", "filt", None, None),
        P("mc", "tile", "filt", None, None),
        P("tile", "filt", None, None),
        P("tile", "filt", None, None),
        P(),
        P(),
        P(),
        P(),
        P(),
    )
    return jax.shard_map(
        body,
        mesh=mesh,
        in_specs=placed,
        out_specs=(P("tile", "filt", None, None), P("tile", "filt", None, None)),
        check_vma=False,
    )
```

```python
import functools

import jax
import jax.numpy as jnp
from jax import lax
from jax.experimental import pallas as pl
from jax.experimental.pallas import tpu as pltpu
from jax.sharding import PartitionSpec as P

NB = 6
K = 3
REACH = 2
HEAD = 3
STEP = 16
WEIGHTS = 64
PRIOR = 112
LANES = 128
VMEM_BYTES = 16 * 1024 * 1024
VMEM = pl.BlockSpec(memory_space=pltpu.VMEM)
SMEM = pl.BlockSpec(memory_space=pltpu.SMEM)


def shifted(x, axis, by):
    length = lax.axis_size(axis)
    pairs = [(i, i + by) for i in range(length) if 0 <= i + by < length]
    return lax.ppermute(x, axis, pairs)


def rotated(x, axis, by):
    length = lax.axis_size(axis)
    return lax.ppermute(x, axis, [(i, (i + by) % length) for i in range(length)])


def build_basis(taps_ref, lines_ref, basis_ref, adjoint):
    kinds, side = basis_ref.shape[0] // 2, basis_ref.shape[1]
    count = taps_ref.shape[1]
    half = (count - 1) // 2
    taps = taps_ref[...].astype(jnp.bfloat16)
    tap = lax.broadcasted_iota(jnp.int32, (count, side), 0)
    lane = lax.broadcasted_iota(jnp.int32, (count, side), 1)
    lane = jnp.where(lane < side // 2, lane, lane - side)
    plain = (lane == half - tap).astype(jnp.float32).astype(jnp.bfloat16)
    turned = (lane == tap - half).astype(jnp.float32).astype(jnp.bfloat16)
    lines_ref[0] = dot(taps, turned if adjoint else plain)
    lines_ref[1] = dot(taps, plain if adjoint else turned)
    apart = lax.broadcasted_iota(jnp.int32, (side, side), 0) - lax.broadcasted_iota(
        jnp.int32, (side, side), 1
    )
    band = jnp.abs(apart) <= half

    def one(k, carry):
        for c in range(2):
            line = jnp.broadcast_to(lines_ref[c, pl.ds(2 * k + c, 1), :], (side, side))
            rows = pltpu.roll(line, 0, 1, stride=1, stride_axis=0)
            basis_ref[c * kinds + k] = jnp.where(band, rows, 0.0).astype(jnp.bfloat16)
        return carry

    lax.fori_loop(0, kinds, one, 0)


def fill_table(sizes, inter_ref, counts_ref, coeff_ref, prec_ref, table_ref):
    tiles, filters, local = sizes
    fields = inter_ref.shape[3]
    own = lax.axis_index("tile")
    first = lax.axis_index("filt") * local
    row_id = lax.broadcasted_iota(jnp.int32, (tiles, NB), 0)
    lane_id = lax.broadcasted_iota(jnp.int32, (1, filters), 1)
    for w in range(2 * REACH + 1):
        tile = jnp.clip(own + w - REACH, 0, tiles - 1)
        live = counts_ref[pl.ds(tile, 1), :]
        for f in range(local):
            row = w * local + f
            for q in range(K):
                entry = inter_ref[first + f, q, pl.ds(tile, 1), :]
                table_ref[row : row + 1, STEP * q : STEP * q + fields] = entry.astype(jnp.float32)
            count = jnp.where(lane_id == first + f, live, 0).astype(jnp.float32)
            table_ref[row : row + 1, STEP * K : STEP * K + 1] = jnp.sum(count, 1, keepdims=True)
            for c in range(3):
                block = coeff_ref[first + f, c].astype(jnp.float32)
                picked = jnp.sum(jnp.where(row_id == tile, block, 0.0), 0, keepdims=True)
                at = WEIGHTS + STEP * c
                table_ref[row : row + 1, at : at + NB] = picked
    for f in range(local):
        table_ref[f : f + 1, PRIOR : PRIOR + filters] = prec_ref[pl.ds(first + f, 1), :]


def number(table_ref, row, at):
    return table_ref[row, at].astype(jnp.int32)


def find_slot(table_ref, row, expo):
    live = number(table_ref, row, STEP * K)
    base = jnp.int32(0)
    found = jnp.int32(0)
    for q in range(K):
        hit = (q < live) & (number(table_ref, row, STEP * q) == expo)
        base = jnp.where(hit, STEP * q, base)
        found = jnp.where(hit, 1, found)
    return found, base


def weight(table_ref, row, b, row_centred, col_centred):
    at = WEIGHTS + b
    flat = table_ref[row, at] + table_ref[row, at + STEP] * row_centred
    return flat + table_ref[row, at + 2 * STEP] * col_centred


def centred_axes(side, oy, ox):
    rows = lax.broadcasted_iota(jnp.int32, (side, 1), 0) + oy
    cols = lax.broadcasted_iota(jnp.int32, (1, side), 1) + ox
    return (
        (2 * rows + 1 - side).astype(jnp.float32) / side,
        (2 * cols + 1 - side).astype(jnp.float32) / side,
    )


def moved_by(image, down, across):
    side = image.shape[0]
    turned = pltpu.roll(image, lax.rem(across + side, side), 1)
    turned = pltpu.roll(turned, lax.rem(down + side, side), 0)
    row = lax.broadcasted_iota(jnp.int32, (side, side), 0) - down
    col = lax.broadcasted_iota(jnp.int32, (side, side), 1) - across
    inside = (row >= 0) & (row < side) & (col >= 0) & (col < side)
    return jnp.where(inside, turned, 0.0)


def dot(a, b):
    return jnp.dot(a, b, preferred_element_type=jnp.float32)


def contribution(table_ref, basis_ref, row, base, place, image):
    side = image.shape[0]
    kinds = basis_ref.shape[0] // 2
    row_centred, col_centred = centred_axes(
        side, number(table_ref, row, base + 1), number(table_ref, row, base + 2)
    )
    total = jnp.zeros((side, side), jnp.float32)
    chosen = [number(table_ref, row, base + HEAD + b) for b in range(NB)]
    half_blurs = dot(jnp.concatenate([basis_ref[k] for k in chosen], 0), image).astype(jnp.bfloat16)
    for b in range(NB):
        blurred = dot(half_blurs[b * side : (b + 1) * side], basis_ref[kinds + chosen[b]])
        total = total + weight(table_ref, place, b, row_centred, col_centred) * blurred
    return total.astype(jnp.bfloat16)


def adjoint_term(table_ref, basis_ref, row, base, place, moved):
    side = moved.shape[0]
    kinds = basis_ref.shape[0] // 2
    row_centred, col_centred = centred_axes(
        side, number(table_ref, row, base + 1), number(table_ref, row, base + 2)
    )
    total = jnp.zeros((side, side), jnp.float32)
    for b in range(NB):
        k = number(table_ref, row, base + HEAD + b)
        w = weight(table_ref, place, b, row_centred, col_centred)
        back_half = dot(basis_ref[k], (w * moved).astype(jnp.bfloat16)).astype(jnp.bfloat16)
        total = total + dot(back_half, basis_ref[kinds + k])
    return total


def source_of(own, move):
    distance, parity = move
    return own + jnp.where(lax.rem(own // distance, 2) == parity, distance, -distance)


def flipped(x, axis, move):
    distance, parity = move
    length = lax.axis_size(axis)
    firsts = [i for i in range(length - distance) if (i // distance) % 2 == parity]
    pairs = [(i, i + distance) for i in firsts] + [(i + distance, i) for i in firsts]
    return lax.ppermute(x, axis, pairs)


def relay_onward(near, count):
    length = lax.axis_size("tile")
    pairs = [(i, i + 2) for i in range(0, length - 2, 2)]
    pairs += [(i, i - 2) for i in range(3, length, 2)]
    return lax.ppermute(near[1, 0][:count], "tile", pairs)


def relay_across(near, count):
    own = lax.axis_index("tile")
    first = lax.rem(own, 2) == lax.rem(own // 2, 2)
    image = jnp.where(first, near[2, 0][count:], near[2, 1][count:])
    return flipped(image, "tile", (1, 0))


def gather_live(sizes, moves, backward, table_ref, images, list_ref, held_ref):
    tiles, filters, local = sizes
    own = lax.axis_index("tile")
    live = jnp.int32(0)
    for (move, f_first), image_ref in zip(moves, images):
        far = own if move is None else source_of(own, move)
        inside = jnp.where((far >= 0) & (far < tiles), 1, 0)
        here, there = REACH * local, jnp.clip(far - own + REACH, 0, 2 * REACH) * local
        tile_at, expo_at = (here, there) if backward else (there, here)
        expo = far if backward else own
        for f in range(f_first, f_first + image_ref.shape[0]):
            found, base = find_slot(table_ref, tile_at + f, expo)
            found = found * inside

            @pl.when(found == 1)
            def _():
                list_ref[0, live] = f
                list_ref[1, live] = tile_at + f
                list_ref[2, live] = base
                list_ref[3, live] = expo_at + f
                held_ref[live] = image_ref[f - f_first]

            live = live + found
    return live


def forward_slots(sizes, moves, table_ref, basis_ref, images, pred_ref, scratch):
    list_ref, held_ref, ready_ref = scratch
    live = gather_live(sizes, moves, False, table_ref, images, list_ref, held_ref)

    @pl.when(live > 0)
    def _():
        def blur(n):
            ready_ref[...] = contribution(
                table_ref,
                basis_ref,
                list_ref[1, n],
                list_ref[2, n],
                list_ref[3, n],
                held_ref[n],
            )

        def settle(n):
            row, base = list_ref[1, n], list_ref[2, n]
            oy, ox = number(table_ref, row, base + 1), number(table_ref, row, base + 2)
            f = list_ref[0, n]
            pred_ref[f] = pred_ref[f] + moved_by(ready_ref[...].astype(jnp.float32), oy, ox)

        def one(n, carry):
            settle(n - 1)
            blur(n)
            return carry

        blur(0)
        lax.fori_loop(1, live, one, 0)
        settle(live - 1)


def backward_slots(sizes, moves, table_ref, basis_ref, images, grad_ref, scratch):
    list_ref, held_ref, ready_ref = scratch
    live = gather_live(sizes, moves, True, table_ref, images, list_ref, held_ref)

    @pl.when(live > 0)
    def _():
        def bring(n):
            row, base = list_ref[1, n], list_ref[2, n]
            oy, ox = number(table_ref, row, base + 1), number(table_ref, row, base + 2)
            return moved_by(held_ref[n].astype(jnp.float32), -oy, -ox)

        def take(n):
            f = list_ref[0, n]
            grad_ref[f] = grad_ref[f] + adjoint_term(
                table_ref,
                basis_ref,
                list_ref[1, n],
                list_ref[2, n],
                list_ref[3, n],
                ready_ref[...],
            )

        def one(n, carry):
            following = bring(n)
            take(n - 1)
            ready_ref[...] = following
            return carry

        ready_ref[...] = bring(0)
        lax.fori_loop(1, live, one, 0)
        take(live - 1)


def prepare(sizes, inter_ref, counts_ref, coeff_ref, prec_ref, taps_ref, *refs):
    table_ref, forth_ref, back_ref, lines_ref = refs
    fill_table(sizes, inter_ref, counts_ref, coeff_ref, prec_ref, table_ref)
    build_basis(taps_ref, lines_ref, forth_ref, False)
    build_basis(taps_ref, lines_ref, back_ref, True)


def forward_own(sizes, table_ref, basis_ref, image_ref, *refs):
    pred_ref, *scratch = refs
    pred_ref[...] = jnp.zeros_like(pred_ref)
    forward_slots(sizes, [(None, 0)], table_ref, basis_ref, [image_ref], pred_ref, scratch)


def forward_next(sizes, moves, table_ref, basis_ref, *refs):
    images, (before_ref, pred_ref, *scratch) = refs[: len(moves)], refs[len(moves) :]
    del before_ref
    forward_slots(sizes, moves, table_ref, basis_ref, images, pred_ref, scratch)


def forward_last(sizes, moves, table_ref, basis_ref, *refs):
    images, refs = refs[: len(moves)], refs[len(moves) :]
    before_ref, observed_ref, inv_ref, pred_ref, resid_ref, *scratch = refs
    del before_ref
    forward_slots(sizes, moves, table_ref, basis_ref, images, pred_ref, scratch)
    for f in range(observed_ref.shape[0]):
        gap = observed_ref[f].astype(jnp.float32) - pred_ref[f]
        resid_ref[f] = (inv_ref[f].astype(jnp.float32) * gap).astype(jnp.bfloat16)


def subtract_prior(sizes, table_ref, sample_ref, others, grad_ref):
    tiles, filters, local = sizes
    part = lax.axis_index("filt")
    parts = filters // local
    first = part * local
    for f in range(local):
        grad = grad_ref[f]
        for g in range(local):
            grad = grad - table_ref[f, PRIOR + first + g] * sample_ref[g]
        for r in range(1, parts):
            source = lax.rem(part + parts - r, parts) * local
            for g in range(local):
                far = others[r - 1][g].astype(jnp.float32)
                grad = grad - table_ref[f, PRIOR + source + g] * far
        grad_ref[f] = grad


def backward_own(sizes, moves, samples, table_ref, basis_ref, *refs):
    images, (scale_ref, *refs) = refs[: len(moves)], refs[len(moves) :]
    noises, (grad_ref, *refs) = refs[:samples], refs[samples:]
    turns, scratch = refs[:samples], refs[samples:]
    for noise_ref, turn_ref in zip(noises, turns):
        turn_ref[...] = scale_ref[...] * noise_ref[...].astype(jnp.float32)
    grad_ref[...] = jnp.zeros_like(grad_ref)
    backward_slots(sizes, moves, table_ref, basis_ref, images, grad_ref, scratch)


def backward_next(sizes, moves, table_ref, basis_ref, *refs):
    images, (before_ref, grad_ref, *scratch) = refs[: len(moves)], refs[len(moves) :]
    del before_ref
    backward_slots(sizes, moves, table_ref, basis_ref, images, grad_ref, scratch)


def backward_last(sizes, moves, table_ref, basis_ref, *refs):
    parts = sizes[1] // sizes[2]
    images, (before_ref, sample_ref, *refs) = refs[: len(moves)], refs[len(moves) :]
    others, (grad_ref, *scratch) = refs[: parts - 1], refs[parts - 1 :]
    del before_ref
    subtract_prior(sizes, table_ref, sample_ref, others, grad_ref)
    backward_slots(sizes, moves, table_ref, basis_ref, images, grad_ref, scratch)


def body(
    sky_mean,
    sky_log_scale,
    noise_draw,
    observed,
    inv_var,
    intersections,
    counts,
    kernels,
    psf_coeffs,
    prior_prec,
):
    side = sky_mean.shape[2]
    local = sky_mean.shape[1]
    tiles, filters = counts.shape
    sizes = (tiles, filters, local)
    kinds = kernels.shape[0]
    early, far_odd = [(1, 0), (2, 0), (2, 1)], (1, 1)
    early_moves = [(move, 0) for move in early]
    onward = local - local // 3
    last_moves = [(far_odd, 0)] + ([(far_odd, onward)] if onward < local else [])

    def last_images(near):
        across = [relay_across(near, onward)] if onward < local else []
        return [relay_onward(near, onward), *across]

    samples = lax.axis_size("mc")
    parts = lax.axis_size("filt")

    scale_map = jnp.exp(sky_log_scale[0])
    noise = noise_draw[0, 0]
    eps_float = noise.astype(jnp.float32)
    sample = sky_mean[0] + scale_map * eps_float
    sample_b = sample.astype(jnp.bfloat16)
    taps = kernels.reshape(2 * kinds, kernels.shape[2])

    image_f32 = jax.ShapeDtypeStruct((local, side, side), jnp.float32)
    image_b16 = jax.ShapeDtypeStruct((local, side, side), jnp.bfloat16)
    basis_type = jax.ShapeDtypeStruct((2 * kinds, side, side), jnp.bfloat16)
    cost = pl.CostEstimate(
        flops=2 * NB * 4 * side**3, bytes_accessed=8 * local * side * side, transcendentals=0
    )
    lines = pltpu.VMEM((2, 2 * kinds, side), jnp.float32)

    def slot_scratch(groups, ready):
        return [
            pltpu.SMEM((4, groups * local), jnp.int32),
            pltpu.VMEM((groups * local, side, side), jnp.bfloat16),
            pltpu.VMEM((side, side), ready),
        ]

    def call(kernel, name, outs, smem, vmem, scratch, aliases={}):
        return pl.pallas_call(
            kernel,
            out_shape=outs,
            in_specs=[SMEM] * len(smem) + [VMEM] * len(vmem),
            out_specs=[VMEM] * len(outs),
            scratch_shapes=scratch,
            input_output_aliases=aliases,
            compiler_params=pltpu.CompilerParams(vmem_limit_bytes=VMEM_BYTES),
            cost_estimate=cost,
            name=name,
        )(*smem, *vmem)

    near = {move: flipped(sample_b, "tile", move) for move in early}
    other_noise = [rotated(noise, "mc", r) for r in range(1, samples)]
    rows = -(-(2 * REACH + 1) * local // 8) * 8
    table, forth, back = call(
        functools.partial(prepare, sizes),
        "prepare",
        [
            jax.ShapeDtypeStruct((rows, LANES), jnp.float32),
            basis_type,
            basis_type,
        ],
        (),
        (
            intersections.transpose(1, 2, 0, 3),
            counts,
            psf_coeffs.transpose(1, 3, 0, 2),
            prior_prec,
            taps,
        ),
        [lines],
    )
    tables = (table,)
    (pred,) = call(
        functools.partial(forward_own, sizes),
        "forward_own",
        [image_f32],
        tables,
        (forth, sample_b),
        slot_scratch(1, jnp.bfloat16),
    )
    near[1, 0], pred = lax.optimization_barrier((near[1, 0], pred))
    near_last = last_images(near)
    (pred,) = call(
        functools.partial(forward_next, sizes, early_moves),
        "forward_next",
        [image_f32],
        tables,
        (forth, *[near[move] for move in early], pred),
        slot_scratch(len(early), jnp.bfloat16),
        {len(tables) + 1 + len(early): 0},
    )
    _, residual = call(
        functools.partial(forward_last, sizes, last_moves),
        "forward_last",
        [image_f32, image_b16],
        tables,
        (forth, *near_last, pred, observed[0], inv_var[0]),
        slot_scratch(1, jnp.bfloat16),
        {len(tables) + 1 + len(near_last): 0},
    )
    near_resid = {move: flipped(residual, "tile", move) for move in [*early, far_odd]}
    late_b, residual = lax.optimization_barrier((sample_b, residual))
    other_samples = [rotated(late_b, "filt", r) for r in range(1, parts)]
    grad, turn, *other_turns = call(
        functools.partial(backward_own, sizes, [(None, 0), early_moves[0]], samples),
        "backward_own",
        [image_f32] * (1 + samples),
        tables,
        (back, residual, near_resid[early[0]], scale_map, noise, *other_noise),
        slot_scratch(2, jnp.float32),
    )
    (grad,) = call(
        functools.partial(backward_next, sizes, early_moves[1:]),
        "backward_next",
        [image_f32],
        tables,
        (back, *[near_resid[move] for move in early[1:]], grad),
        slot_scratch(len(early) - 1, jnp.float32),
        {len(tables) + len(early): 0},
    )
    (grad,) = call(
        functools.partial(backward_last, sizes, [(far_odd, 0)]),
        "backward_last",
        [image_f32],
        tables,
        (back, near_resid[far_odd], grad, sample, *other_samples),
        slot_scratch(1, jnp.float32),
        {len(tables) + 2: 0},
    )
    mean_sum = grad
    scale_sum = grad * turn
    for r in range(1, samples):
        other_grad = rotated(grad, "mc", r)
        mean_sum = mean_sum + other_grad
        scale_sum = scale_sum + other_grad * other_turns[r - 1]
    return ((mean_sum / samples)[None], (scale_sum / samples + 1.0)[None])

def solution(mesh):
    placed = (
        P("tile", "filt", None, None),
        P("tile", "filt", None, None),
        P("mc", "tile", "filt", None, None),
        P("tile", "filt", None, None),
        P("tile", "filt", None, None),
        P(),
        P(),
        P(),
        P(),
        P(),
    )
    return jax.shard_map(
        body,
        mesh=mesh,
        in_specs=placed,
        out_specs=(P("tile", "filt", None, None), P("tile", "filt", None, None)),
        check_vma=False,
    )
```

```python
import functools

import jax
import jax.numpy as jnp
from jax import lax
from jax.experimental import pallas as pl
from jax.experimental.pallas import tpu as pltpu
from jax.sharding import PartitionSpec as P

NB = 6
K = 3
REACH = 2
HEAD = 3
STEP = 16
WEIGHTS = 64
PRIOR = 112
LANES = 128
VMEM_BYTES = 16 * 1024 * 1024
VMEM = pl.BlockSpec(memory_space=pltpu.VMEM)
SMEM = pl.BlockSpec(memory_space=pltpu.SMEM)


def shifted(x, axis, by):
    length = lax.axis_size(axis)
    pairs = [(i, i + by) for i in range(length) if 0 <= i + by < length]
    return lax.ppermute(x, axis, pairs)


def rotated(x, axis, by):
    length = lax.axis_size(axis)
    return lax.ppermute(x, axis, [(i, (i + by) % length) for i in range(length)])


def build_basis(taps_ref, lines_ref, basis_ref, adjoint):
    kinds, side = basis_ref.shape[0] // 2, basis_ref.shape[1]
    count = taps_ref.shape[1]
    half = (count - 1) // 2
    taps = taps_ref[...].astype(jnp.bfloat16)
    tap = lax.broadcasted_iota(jnp.int32, (count, side), 0)
    lane = lax.broadcasted_iota(jnp.int32, (count, side), 1)
    lane = jnp.where(lane < side // 2, lane, lane - side)
    plain = (lane == half - tap).astype(jnp.float32).astype(jnp.bfloat16)
    turned = (lane == tap - half).astype(jnp.float32).astype(jnp.bfloat16)
    lines_ref[0] = dot(taps, turned if adjoint else plain)
    lines_ref[1] = dot(taps, plain if adjoint else turned)
    apart = lax.broadcasted_iota(jnp.int32, (side, side), 0) - lax.broadcasted_iota(
        jnp.int32, (side, side), 1
    )
    band = jnp.abs(apart) <= half

    def one(k, carry):
        for c in range(2):
            line = jnp.broadcast_to(lines_ref[c, pl.ds(2 * k + c, 1), :], (side, side))
            rows = pltpu.roll(line, 0, 1, stride=1, stride_axis=0)
            basis_ref[c * kinds + k] = jnp.where(band, rows, 0.0).astype(jnp.bfloat16)
        return carry

    lax.fori_loop(0, kinds, one, 0)


def fill_table(sizes, inter_ref, counts_ref, coeff_ref, prec_ref, table_ref):
    tiles, filters, local = sizes
    fields = inter_ref.shape[3]
    own = lax.axis_index("tile")
    first = lax.axis_index("filt") * local
    row_id = lax.broadcasted_iota(jnp.int32, (tiles, NB), 0)
    lane_id = lax.broadcasted_iota(jnp.int32, (1, filters), 1)
    for w in range(2 * REACH + 1):
        tile = jnp.clip(own + w - REACH, 0, tiles - 1)
        live = counts_ref[pl.ds(tile, 1), :]
        for f in range(local):
            row = w * local + f
            for q in range(K):
                entry = inter_ref[first + f, q, pl.ds(tile, 1), :]
                table_ref[row : row + 1, STEP * q : STEP * q + fields] = entry.astype(jnp.float32)
            count = jnp.where(lane_id == first + f, live, 0).astype(jnp.float32)
            table_ref[row : row + 1, STEP * K : STEP * K + 1] = jnp.sum(count, 1, keepdims=True)
            for c in range(3):
                block = coeff_ref[first + f, c].astype(jnp.float32)
                picked = jnp.sum(jnp.where(row_id == tile, block, 0.0), 0, keepdims=True)
                at = WEIGHTS + STEP * c
                table_ref[row : row + 1, at : at + NB] = picked
    for f in range(local):
        table_ref[f : f + 1, PRIOR : PRIOR + filters] = prec_ref[pl.ds(first + f, 1), :]


def number(table_ref, row, at):
    return table_ref[row, at].astype(jnp.int32)


def find_slot(table_ref, row, expo):
    live = number(table_ref, row, STEP * K)
    base = jnp.int32(0)
    found = jnp.int32(0)
    for q in range(K):
        hit = (q < live) & (number(table_ref, row, STEP * q) == expo)
        base = jnp.where(hit, STEP * q, base)
        found = jnp.where(hit, 1, found)
    return found, base


def weight(table_ref, row, b, row_centred, col_centred):
    at = WEIGHTS + b
    flat = table_ref[row, at] + table_ref[row, at + STEP] * row_centred
    return flat + table_ref[row, at + 2 * STEP] * col_centred


def centred_axes(side, oy, ox):
    rows = lax.broadcasted_iota(jnp.int32, (side, 1), 0) + oy
    cols = lax.broadcasted_iota(jnp.int32, (1, side), 1) + ox
    return (
        (2 * rows + 1 - side).astype(jnp.float32) / side,
        (2 * cols + 1 - side).astype(jnp.float32) / side,
    )


def moved_by(image, down, across):
    side = image.shape[0]
    turned = pltpu.roll(image, lax.rem(across + side, side), 1)
    turned = pltpu.roll(turned, lax.rem(down + side, side), 0)
    row = lax.broadcasted_iota(jnp.int32, (side, side), 0) - down
    col = lax.broadcasted_iota(jnp.int32, (side, side), 1) - across
    inside = (row >= 0) & (row < side) & (col >= 0) & (col < side)
    return jnp.where(inside, turned, 0.0)


def dot(a, b):
    return jnp.dot(a, b, preferred_element_type=jnp.float32)


def contribution(table_ref, basis_ref, row, base, place, image):
    side = image.shape[0]
    kinds = basis_ref.shape[0] // 2
    row_centred, col_centred = centred_axes(
        side, number(table_ref, row, base + 1), number(table_ref, row, base + 2)
    )
    total = jnp.zeros((side, side), jnp.float32)
    chosen = [number(table_ref, row, base + HEAD + b) for b in range(NB)]
    half_blurs = dot(jnp.concatenate([basis_ref[k] for k in chosen], 0), image).astype(jnp.bfloat16)
    for b in range(NB):
        blurred = dot(half_blurs[b * side : (b + 1) * side], basis_ref[kinds + chosen[b]])
        total = total + weight(table_ref, place, b, row_centred, col_centred) * blurred
    return total.astype(jnp.bfloat16)


def adjoint_term(table_ref, basis_ref, row, base, place, moved):
    side = moved.shape[0]
    kinds = basis_ref.shape[0] // 2
    row_centred, col_centred = centred_axes(
        side, number(table_ref, row, base + 1), number(table_ref, row, base + 2)
    )
    total = jnp.zeros((side, side), jnp.float32)
    for b in range(NB):
        k = number(table_ref, row, base + HEAD + b)
        w = weight(table_ref, place, b, row_centred, col_centred)
        back_half = dot(basis_ref[k], (w * moved).astype(jnp.bfloat16)).astype(jnp.bfloat16)
        total = total + dot(back_half, basis_ref[kinds + k])
    return total


def source_of(own, move):
    distance, parity = move
    return own + jnp.where(lax.rem(own // distance, 2) == parity, distance, -distance)


def flipped(x, axis, move):
    distance, parity = move
    length = lax.axis_size(axis)
    firsts = [i for i in range(length - distance) if (i // distance) % 2 == parity]
    pairs = [(i, i + distance) for i in firsts] + [(i + distance, i) for i in firsts]
    return lax.ppermute(x, axis, pairs)


def relay_onward(near, count):
    length = lax.axis_size("tile")
    pairs = [(i, i + 2) for i in range(0, length - 2, 2)]
    pairs += [(i, i - 2) for i in range(3, length, 2)]
    return lax.ppermute(near[1, 0][:count], "tile", pairs)


def relay_across(near, count):
    own = lax.axis_index("tile")
    first = lax.rem(own, 2) == lax.rem(own // 2, 2)
    image = jnp.where(first, near[2, 0][count:], near[2, 1][count:])
    return flipped(image, "tile", (1, 0))


def gather_live(sizes, moves, backward, table_ref, images, list_ref, held_ref):
    tiles, filters, local = sizes
    own = lax.axis_index("tile")
    live = jnp.int32(0)
    for (move, f_first), image_ref in zip(moves, images):
        far = own if move is None else source_of(own, move)
        inside = jnp.where((far >= 0) & (far < tiles), 1, 0)
        here, there = REACH * local, jnp.clip(far - own + REACH, 0, 2 * REACH) * local
        tile_at, expo_at = (here, there) if backward else (there, here)
        expo = far if backward else own
        for f in range(f_first, f_first + image_ref.shape[0]):
            found, base = find_slot(table_ref, tile_at + f, expo)
            found = found * inside

            @pl.when(found == 1)
            def _():
                list_ref[0, live] = f
                list_ref[1, live] = tile_at + f
                list_ref[2, live] = base
                list_ref[3, live] = expo_at + f
                held_ref[live] = image_ref[f - f_first]

            live = live + found
    return live


def forward_slots(sizes, moves, table_ref, basis_ref, images, pred_ref, scratch):
    list_ref, held_ref, ready_ref = scratch
    live = gather_live(sizes, moves, False, table_ref, images, list_ref, held_ref)

    @pl.when(live > 0)
    def _():
        def blur(n):
            ready_ref[...] = contribution(
                table_ref,
                basis_ref,
                list_ref[1, n],
                list_ref[2, n],
                list_ref[3, n],
                held_ref[n],
            )

        def settle(n):
            row, base = list_ref[1, n], list_ref[2, n]
            oy, ox = number(table_ref, row, base + 1), number(table_ref, row, base + 2)
            f = list_ref[0, n]
            pred_ref[f] = pred_ref[f] + moved_by(ready_ref[...].astype(jnp.float32), oy, ox)

        def one(n, carry):
            settle(n - 1)
            blur(n)
            return carry

        blur(0)
        lax.fori_loop(1, live, one, 0)
        settle(live - 1)


def backward_slots(sizes, moves, table_ref, basis_ref, images, grad_ref, scratch):
    list_ref, held_ref, ready_ref = scratch
    live = gather_live(sizes, moves, True, table_ref, images, list_ref, held_ref)

    @pl.when(live > 0)
    def _():
        def bring(n):
            row, base = list_ref[1, n], list_ref[2, n]
            oy, ox = number(table_ref, row, base + 1), number(table_ref, row, base + 2)
            return moved_by(held_ref[n].astype(jnp.float32), -oy, -ox)

        def take(n):
            f = list_ref[0, n]
            grad_ref[f] = grad_ref[f] + adjoint_term(
                table_ref,
                basis_ref,
                list_ref[1, n],
                list_ref[2, n],
                list_ref[3, n],
                ready_ref[...],
            )

        def one(n, carry):
            following = bring(n)
            take(n - 1)
            ready_ref[...] = following
            return carry

        ready_ref[...] = bring(0)
        lax.fori_loop(1, live, one, 0)
        take(live - 1)


def prepare(sizes, inter_ref, counts_ref, coeff_ref, prec_ref, taps_ref, *refs):
    table_ref, forth_ref, back_ref, lines_ref = refs
    fill_table(sizes, inter_ref, counts_ref, coeff_ref, prec_ref, table_ref)
    build_basis(taps_ref, lines_ref, forth_ref, False)
    build_basis(taps_ref, lines_ref, back_ref, True)


def forward_own(sizes, table_ref, basis_ref, image_ref, *refs):
    pred_ref, *scratch = refs
    pred_ref[...] = jnp.zeros_like(pred_ref)
    forward_slots(sizes, [(None, 0)], table_ref, basis_ref, [image_ref], pred_ref, scratch)


def forward_next(sizes, moves, table_ref, basis_ref, *refs):
    images, (before_ref, pred_ref, *scratch) = refs[: len(moves)], refs[len(moves) :]
    del before_ref
    forward_slots(sizes, moves, table_ref, basis_ref, images, pred_ref, scratch)


def forward_last(sizes, moves, table_ref, basis_ref, *refs):
    images, refs = refs[: len(moves)], refs[len(moves) :]
    before_ref, observed_ref, inv_ref, pred_ref, resid_ref, *scratch = refs
    del before_ref
    forward_slots(sizes, moves, table_ref, basis_ref, images, pred_ref, scratch)
    for f in range(observed_ref.shape[0]):
        gap = observed_ref[f].astype(jnp.float32) - pred_ref[f]
        resid_ref[f] = (inv_ref[f].astype(jnp.float32) * gap).astype(jnp.bfloat16)


def subtract_prior(sizes, table_ref, sample_ref, others, grad_ref):
    tiles, filters, local = sizes
    part = lax.axis_index("filt")
    parts = filters // local
    first = part * local
    for f in range(local):
        grad = grad_ref[f]
        for g in range(local):
            grad = grad - table_ref[f, PRIOR + first + g] * sample_ref[g]
        for r in range(1, parts):
            source = lax.rem(part + parts - r, parts) * local
            for g in range(local):
                far = others[r - 1][g].astype(jnp.float32)
                grad = grad - table_ref[f, PRIOR + source + g] * far
        grad_ref[f] = grad


def backward_own(sizes, moves, samples, table_ref, basis_ref, *refs):
    images, (scale_ref, *refs) = refs[: len(moves)], refs[len(moves) :]
    noises, (grad_ref, *refs) = refs[:samples], refs[samples:]
    turns, scratch = refs[:samples], refs[samples:]
    for noise_ref, turn_ref in zip(noises, turns):
        turn_ref[...] = scale_ref[...] * noise_ref[...].astype(jnp.float32)
    grad_ref[...] = jnp.zeros_like(grad_ref)
    backward_slots(sizes, moves, table_ref, basis_ref, images, grad_ref, scratch)


def backward_next(sizes, moves, table_ref, basis_ref, *refs):
    images, (before_ref, grad_ref, *scratch) = refs[: len(moves)], refs[len(moves) :]
    del before_ref
    backward_slots(sizes, moves, table_ref, basis_ref, images, grad_ref, scratch)


def backward_last(sizes, moves, table_ref, basis_ref, *refs):
    parts = sizes[1] // sizes[2]
    images, (before_ref, sample_ref, *refs) = refs[: len(moves)], refs[len(moves) :]
    others, (grad_ref, *scratch) = refs[: parts - 1], refs[parts - 1 :]
    del before_ref
    subtract_prior(sizes, table_ref, sample_ref, others, grad_ref)
    backward_slots(sizes, moves, table_ref, basis_ref, images, grad_ref, scratch)


def body(
    sky_mean,
    sky_log_scale,
    noise_draw,
    observed,
    inv_var,
    intersections,
    counts,
    kernels,
    psf_coeffs,
    prior_prec,
):
    side = sky_mean.shape[2]
    local = sky_mean.shape[1]
    tiles, filters = counts.shape
    sizes = (tiles, filters, local)
    kinds = kernels.shape[0]
    early, far_odd = [(1, 0), (2, 0), (2, 1)], (1, 1)
    early_moves = [(move, 0) for move in early]
    onward = local - local // 3
    last_moves = [(far_odd, 0)] + ([(far_odd, onward)] if onward < local else [])

    def last_images(near):
        across = [relay_across(near, onward)] if onward < local else []
        return [relay_onward(near, onward), *across]

    samples = lax.axis_size("mc")
    parts = lax.axis_size("filt")

    scale_map = jnp.exp(sky_log_scale[0])
    noise = noise_draw[0, 0]
    eps_float = noise.astype(jnp.float32)
    sample = sky_mean[0] + scale_map * eps_float
    sample_b = sample.astype(jnp.bfloat16)
    taps = kernels.reshape(2 * kinds, kernels.shape[2])

    image_f32 = jax.ShapeDtypeStruct((local, side, side), jnp.float32)
    image_b16 = jax.ShapeDtypeStruct((local, side, side), jnp.bfloat16)
    basis_type = jax.ShapeDtypeStruct((2 * kinds, side, side), jnp.bfloat16)
    cost = pl.CostEstimate(
        flops=2 * NB * 4 * side**3, bytes_accessed=8 * local * side * side, transcendentals=0
    )
    lines = pltpu.VMEM((2, 2 * kinds, side), jnp.float32)

    def slot_scratch(groups, ready):
        return [
            pltpu.SMEM((4, groups * local), jnp.int32),
            pltpu.VMEM((groups * local, side, side), jnp.bfloat16),
            pltpu.VMEM((side, side), ready),
        ]

    def call(kernel, name, outs, smem, vmem, scratch, aliases={}):
        return pl.pallas_call(
            kernel,
            out_shape=outs,
            in_specs=[SMEM] * len(smem) + [VMEM] * len(vmem),
            out_specs=[VMEM] * len(outs),
            scratch_shapes=scratch,
            input_output_aliases=aliases,
            compiler_params=pltpu.CompilerParams(vmem_limit_bytes=VMEM_BYTES),
            cost_estimate=cost,
            name=name,
        )(*smem, *vmem)

    near = {move: flipped(sample_b, "tile", move) for move in early}
    other_noise = [rotated(noise, "mc", r) for r in range(1, samples)]
    rows = -(-(2 * REACH + 1) * local // 8) * 8
    table, forth, back = call(
        functools.partial(prepare, sizes),
        "prepare",
        [
            jax.ShapeDtypeStruct((rows, LANES), jnp.float32),
            basis_type,
            basis_type,
        ],
        (),
        (
            intersections.transpose(1, 2, 0, 3),
            counts,
            psf_coeffs.transpose(1, 3, 0, 2),
            prior_prec,
            taps,
        ),
        [lines],
    )
    tables = (table,)
    (pred,) = call(
        functools.partial(forward_own, sizes),
        "forward_own",
        [image_f32],
        tables,
        (forth, sample_b),
        slot_scratch(1, jnp.bfloat16),
    )
    near[1, 0], pred = lax.optimization_barrier((near[1, 0], pred))
    near_last = last_images(near)
    (pred,) = call(
        functools.partial(forward_next, sizes, early_moves),
        "forward_next",
        [image_f32],
        tables,
        (forth, *[near[move] for move in early], pred),
        slot_scratch(len(early), jnp.bfloat16),
        {len(tables) + 1 + len(early): 0},
    )
    _, residual = call(
        functools.partial(forward_last, sizes, last_moves),
        "forward_last",
        [image_f32, image_b16],
        tables,
        (forth, *near_last, pred, observed[0], inv_var[0]),
        slot_scratch(1, jnp.bfloat16),
        {len(tables) + 1 + len(near_last): 0},
    )
    near_resid = {move: flipped(residual, "tile", move) for move in early}
    pieces = [(f, to) for f, to in [(0, onward), (onward, local)] if f < to]
    far_resid = [flipped(residual[f:to], "tile", far_odd) for f, to in pieces]
    late_b, residual = lax.optimization_barrier((sample_b, residual))
    other_samples = [rotated(late_b, "filt", r) for r in range(1, parts)]
    grad, turn, *other_turns = call(
        functools.partial(backward_own, sizes, [(None, 0), early_moves[0]], samples),
        "backward_own",
        [image_f32] * (1 + samples),
        tables,
        (back, residual, near_resid[early[0]], scale_map, noise, *other_noise),
        slot_scratch(2, jnp.float32),
    )
    (grad,) = call(
        functools.partial(backward_next, sizes, early_moves[1:]),
        "backward_next",
        [image_f32],
        tables,
        (back, *[near_resid[move] for move in early[1:]], grad),
        slot_scratch(len(early) - 1, jnp.float32),
        {len(tables) + len(early): 0},
    )
    for image, (f, to) in zip(far_resid[:-1], pieces[:-1]):
        (grad,) = call(
            functools.partial(backward_next, sizes, [(far_odd, f)]),
            f"backward_far_{f}",
            [image_f32],
            tables,
            (back, image, grad),
            slot_scratch(1, jnp.float32),
            {len(tables) + 2: 0},
        )
    (grad,) = call(
        functools.partial(backward_last, sizes, [(far_odd, pieces[-1][0])]),
        "backward_last",
        [image_f32],
        tables,
        (back, far_resid[-1], grad, sample, *other_samples),
        slot_scratch(1, jnp.float32),
        {len(tables) + 2: 0},
    )
    mean_sum = grad
    scale_sum = grad * turn
    for r in range(1, samples):
        other_grad = rotated(grad, "mc", r)
        mean_sum = mean_sum + other_grad
        scale_sum = scale_sum + other_grad * other_turns[r - 1]
    return ((mean_sum / samples)[None], (scale_sum / samples + 1.0)[None])

def solution(mesh):
    placed = (
        P("tile", "filt", None, None),
        P("tile", "filt", None, None),
        P("mc", "tile", "filt", None, None),
        P("tile", "filt", None, None),
        P("tile", "filt", None, None),
        P(),
        P(),
        P(),
        P(),
        P(),
    )
    return jax.shard_map(
        body,
        mesh=mesh,
        in_specs=placed,
        out_specs=(P("tile", "filt", None, None), P("tile", "filt", None, None)),
        check_vma=False,
    )
```

```python
import functools

import jax
import jax.numpy as jnp
from jax import lax
from jax.experimental import pallas as pl
from jax.experimental.pallas import tpu as pltpu
from jax.sharding import PartitionSpec as P

NB = 6
K = 3
REACH = 2
HEAD = 3
STEP = 16
WEIGHTS = 64
PRIOR = 112
LANES = 128
VMEM_BYTES = 16 * 1024 * 1024
VMEM = pl.BlockSpec(memory_space=pltpu.VMEM)
SMEM = pl.BlockSpec(memory_space=pltpu.SMEM)


def shifted(x, axis, by):
    length = lax.axis_size(axis)
    pairs = [(i, i + by) for i in range(length) if 0 <= i + by < length]
    return lax.ppermute(x, axis, pairs)


def rotated(x, axis, by):
    length = lax.axis_size(axis)
    return lax.ppermute(x, axis, [(i, (i + by) % length) for i in range(length)])


def build_basis(taps_ref, lines_ref, basis_ref, adjoint):
    kinds, side = basis_ref.shape[0] // 2, basis_ref.shape[1]
    count = taps_ref.shape[1]
    half = (count - 1) // 2
    taps = taps_ref[...].astype(jnp.bfloat16)
    tap = lax.broadcasted_iota(jnp.int32, (count, side), 0)
    lane = lax.broadcasted_iota(jnp.int32, (count, side), 1)
    lane = jnp.where(lane < side // 2, lane, lane - side)
    plain = (lane == half - tap).astype(jnp.float32).astype(jnp.bfloat16)
    turned = (lane == tap - half).astype(jnp.float32).astype(jnp.bfloat16)
    lines_ref[0] = dot(taps, turned if adjoint else plain)
    lines_ref[1] = dot(taps, plain if adjoint else turned)
    apart = lax.broadcasted_iota(jnp.int32, (side, side), 0) - lax.broadcasted_iota(
        jnp.int32, (side, side), 1
    )
    band = jnp.abs(apart) <= half

    def one(k, carry):
        for c in range(2):
            line = jnp.broadcast_to(lines_ref[c, pl.ds(2 * k + c, 1), :], (side, side))
            rows = pltpu.roll(line, 0, 1, stride=1, stride_axis=0)
            basis_ref[c * kinds + k] = jnp.where(band, rows, 0.0).astype(jnp.bfloat16)
        return carry

    lax.fori_loop(0, kinds, one, 0)


def fill_table(sizes, inter_ref, counts_ref, coeff_ref, prec_ref, table_ref):
    tiles, filters, local = sizes
    fields = inter_ref.shape[3]
    own = lax.axis_index("tile")
    first = lax.axis_index("filt") * local
    row_id = lax.broadcasted_iota(jnp.int32, (tiles, NB), 0)
    lane_id = lax.broadcasted_iota(jnp.int32, (1, filters), 1)
    for w in range(2 * REACH + 1):
        tile = jnp.clip(own + w - REACH, 0, tiles - 1)
        live = counts_ref[pl.ds(tile, 1), :]
        for f in range(local):
            row = w * local + f
            for q in range(K):
                entry = inter_ref[first + f, q, pl.ds(tile, 1), :]
                table_ref[row : row + 1, STEP * q : STEP * q + fields] = entry.astype(jnp.float32)
            count = jnp.where(lane_id == first + f, live, 0).astype(jnp.float32)
            table_ref[row : row + 1, STEP * K : STEP * K + 1] = jnp.sum(count, 1, keepdims=True)
            for c in range(3):
                block = coeff_ref[first + f, c].astype(jnp.float32)
                picked = jnp.sum(jnp.where(row_id == tile, block, 0.0), 0, keepdims=True)
                at = WEIGHTS + STEP * c
                table_ref[row : row + 1, at : at + NB] = picked
    for f in range(local):
        table_ref[f : f + 1, PRIOR : PRIOR + filters] = prec_ref[pl.ds(first + f, 1), :]


def number(table_ref, row, at):
    return table_ref[row, at].astype(jnp.int32)


def find_slot(table_ref, row, expo):
    live = number(table_ref, row, STEP * K)
    base = jnp.int32(0)
    found = jnp.int32(0)
    for q in range(K):
        hit = (q < live) & (number(table_ref, row, STEP * q) == expo)
        base = jnp.where(hit, STEP * q, base)
        found = jnp.where(hit, 1, found)
    return found, base


def weight(table_ref, row, b, row_centred, col_centred):
    at = WEIGHTS + b
    flat = table_ref[row, at] + table_ref[row, at + STEP] * row_centred
    return flat + table_ref[row, at + 2 * STEP] * col_centred


def centred_axes(side, oy, ox):
    rows = lax.broadcasted_iota(jnp.int32, (side, 1), 0) + oy
    cols = lax.broadcasted_iota(jnp.int32, (1, side), 1) + ox
    return (
        (2 * rows + 1 - side).astype(jnp.float32) / side,
        (2 * cols + 1 - side).astype(jnp.float32) / side,
    )


def moved_by(image, down, across):
    side = image.shape[0]
    turned = pltpu.roll(image, lax.rem(across + side, side), 1)
    turned = pltpu.roll(turned, lax.rem(down + side, side), 0)
    row = lax.broadcasted_iota(jnp.int32, (side, side), 0) - down
    col = lax.broadcasted_iota(jnp.int32, (side, side), 1) - across
    inside = (row >= 0) & (row < side) & (col >= 0) & (col < side)
    return jnp.where(inside, turned, 0.0)


def dot(a, b):
    return jnp.dot(a, b, preferred_element_type=jnp.float32)


def contribution(table_ref, basis_ref, row, base, place, image):
    side = image.shape[0]
    kinds = basis_ref.shape[0] // 2
    row_centred, col_centred = centred_axes(
        side, number(table_ref, row, base + 1), number(table_ref, row, base + 2)
    )
    total = jnp.zeros((side, side), jnp.float32)
    chosen = [number(table_ref, row, base + HEAD + b) for b in range(NB)]
    half_blurs = dot(jnp.concatenate([basis_ref[k] for k in chosen], 0), image).astype(jnp.bfloat16)
    for b in range(0, NB, 2):
        pair = jnp.zeros((side, side), jnp.float32)
        for c in range(b, min(b + 2, NB)):
            blurred = dot(half_blurs[c * side : (c + 1) * side], basis_ref[kinds + chosen[c]])
            pair = pair + weight(table_ref, place, c, row_centred, col_centred) * blurred
        total = total + pair
    return total.astype(jnp.bfloat16)


def adjoint_term(table_ref, basis_ref, row, base, place, moved):
    side = moved.shape[0]
    kinds = basis_ref.shape[0] // 2
    row_centred, col_centred = centred_axes(
        side, number(table_ref, row, base + 1), number(table_ref, row, base + 2)
    )
    chosen = [number(table_ref, row, base + HEAD + b) for b in range(NB)]
    back_halves = []
    for b in range(NB):
        w = weight(table_ref, place, b, row_centred, col_centred)
        back_half = dot(basis_ref[chosen[b]], (w * moved).astype(jnp.bfloat16))
        back_halves.append(back_half.astype(jnp.bfloat16))
    right = jnp.concatenate([basis_ref[kinds + k] for k in chosen], 0)
    return dot(jnp.concatenate(back_halves, 1), right)


def source_of(own, move):
    distance, parity = move
    return own + jnp.where(lax.rem(own // distance, 2) == parity, distance, -distance)


def flipped(x, axis, move):
    distance, parity = move
    length = lax.axis_size(axis)
    firsts = [i for i in range(length - distance) if (i // distance) % 2 == parity]
    pairs = [(i, i + distance) for i in firsts] + [(i + distance, i) for i in firsts]
    return lax.ppermute(x, axis, pairs)


def relay_onward(near, count):
    length = lax.axis_size("tile")
    pairs = [(i, i + 2) for i in range(0, length - 2, 2)]
    pairs += [(i, i - 2) for i in range(3, length, 2)]
    return lax.ppermute(near[1, 0][:count], "tile", pairs)


def relay_across(near, count):
    own = lax.axis_index("tile")
    first = lax.rem(own, 2) == lax.rem(own // 2, 2)
    image = jnp.where(first, near[2, 0][count:], near[2, 1][count:])
    return flipped(image, "tile", (1, 0))


def gather_live(sizes, moves, backward, table_ref, images, list_ref, held_ref):
    tiles, filters, local = sizes
    own = lax.axis_index("tile")
    live = jnp.int32(0)
    for (move, f_first), image_ref in zip(moves, images):
        far = own if move is None else source_of(own, move)
        inside = jnp.where((far >= 0) & (far < tiles), 1, 0)
        here, there = REACH * local, jnp.clip(far - own + REACH, 0, 2 * REACH) * local
        tile_at, expo_at = (here, there) if backward else (there, here)
        expo = far if backward else own
        for f in range(f_first, f_first + image_ref.shape[0]):
            found, base = find_slot(table_ref, tile_at + f, expo)
            found = found * inside

            @pl.when(found == 1)
            def _():
                list_ref[0, live] = f
                list_ref[1, live] = tile_at + f
                list_ref[2, live] = base
                list_ref[3, live] = expo_at + f
                held_ref[live] = image_ref[f - f_first]

            live = live + found
    return live


def forward_slots(sizes, moves, table_ref, basis_ref, images, pred_ref, scratch):
    list_ref, held_ref, ready_ref = scratch
    live = gather_live(sizes, moves, False, table_ref, images, list_ref, held_ref)

    @pl.when(live > 0)
    def _():
        def blur(n):
            ready_ref[...] = contribution(
                table_ref,
                basis_ref,
                list_ref[1, n],
                list_ref[2, n],
                list_ref[3, n],
                held_ref[n],
            )

        def settle(n):
            row, base = list_ref[1, n], list_ref[2, n]
            oy, ox = number(table_ref, row, base + 1), number(table_ref, row, base + 2)
            f = list_ref[0, n]
            pred_ref[f] = pred_ref[f] + moved_by(ready_ref[...].astype(jnp.float32), oy, ox)

        def one(n, carry):
            settle(n - 1)
            blur(n)
            return carry

        blur(0)
        lax.fori_loop(1, live, one, 0)
        settle(live - 1)


def backward_slots(sizes, moves, table_ref, basis_ref, images, grad_ref, scratch):
    list_ref, held_ref, ready_ref = scratch
    live = gather_live(sizes, moves, True, table_ref, images, list_ref, held_ref)

    @pl.when(live > 0)
    def _():
        def bring(n):
            row, base = list_ref[1, n], list_ref[2, n]
            oy, ox = number(table_ref, row, base + 1), number(table_ref, row, base + 2)
            return moved_by(held_ref[n].astype(jnp.float32), -oy, -ox)

        def take(n):
            f = list_ref[0, n]
            grad_ref[f] = grad_ref[f] + adjoint_term(
                table_ref,
                basis_ref,
                list_ref[1, n],
                list_ref[2, n],
                list_ref[3, n],
                ready_ref[...],
            )

        def one(n, carry):
            following = bring(n)
            take(n - 1)
            ready_ref[...] = following
            return carry

        ready_ref[...] = bring(0)
        lax.fori_loop(1, live, one, 0)
        take(live - 1)


def prepare(sizes, inter_ref, counts_ref, coeff_ref, prec_ref, taps_ref, *refs):
    table_ref, forth_ref, back_ref, lines_ref = refs
    fill_table(sizes, inter_ref, counts_ref, coeff_ref, prec_ref, table_ref)
    build_basis(taps_ref, lines_ref, forth_ref, False)
    build_basis(taps_ref, lines_ref, back_ref, True)


def forward_own(sizes, table_ref, basis_ref, image_ref, *refs):
    pred_ref, *scratch = refs
    pred_ref[...] = jnp.zeros_like(pred_ref)
    forward_slots(sizes, [(None, 0)], table_ref, basis_ref, [image_ref], pred_ref, scratch)


def forward_next(sizes, moves, table_ref, basis_ref, *refs):
    images, (before_ref, pred_ref, *scratch) = refs[: len(moves)], refs[len(moves) :]
    del before_ref
    forward_slots(sizes, moves, table_ref, basis_ref, images, pred_ref, scratch)


def forward_last(sizes, moves, table_ref, basis_ref, *refs):
    images, refs = refs[: len(moves)], refs[len(moves) :]
    before_ref, observed_ref, inv_ref, pred_ref, resid_ref, *scratch = refs
    del before_ref
    forward_slots(sizes, moves, table_ref, basis_ref, images, pred_ref, scratch)
    for f in range(observed_ref.shape[0]):
        gap = observed_ref[f].astype(jnp.float32) - pred_ref[f]
        resid_ref[f] = (inv_ref[f].astype(jnp.float32) * gap).astype(jnp.bfloat16)


def subtract_prior(sizes, table_ref, sample_ref, others, grad_ref):
    tiles, filters, local = sizes
    part = lax.axis_index("filt")
    parts = filters // local
    first = part * local
    for f in range(local):
        grad = grad_ref[f]
        for g in range(local):
            grad = grad - table_ref[f, PRIOR + first + g] * sample_ref[g]
        for r in range(1, parts):
            source = lax.rem(part + parts - r, parts) * local
            for g in range(local):
                far = others[r - 1][g].astype(jnp.float32)
                grad = grad - table_ref[f, PRIOR + source + g] * far
        grad_ref[f] = grad


def backward_own(sizes, moves, samples, table_ref, basis_ref, *refs):
    images, (scale_ref, *refs) = refs[: len(moves)], refs[len(moves) :]
    noises, (grad_ref, *refs) = refs[:samples], refs[samples:]
    turns, scratch = refs[:samples], refs[samples:]
    for noise_ref, turn_ref in zip(noises, turns):
        turn_ref[...] = scale_ref[...] * noise_ref[...].astype(jnp.float32)
    grad_ref[...] = jnp.zeros_like(grad_ref)
    backward_slots(sizes, moves, table_ref, basis_ref, images, grad_ref, scratch)


def backward_next(sizes, moves, table_ref, basis_ref, *refs):
    images, (before_ref, grad_ref, *scratch) = refs[: len(moves)], refs[len(moves) :]
    del before_ref
    backward_slots(sizes, moves, table_ref, basis_ref, images, grad_ref, scratch)


def backward_prior(sizes, table_ref, before_ref, sample_ref, *refs):
    others, (grad_ref,) = refs[:-1], refs[-1:]
    del before_ref
    subtract_prior(sizes, table_ref, sample_ref, others, grad_ref)


def body(
    sky_mean,
    sky_log_scale,
    noise_draw,
    observed,
    inv_var,
    intersections,
    counts,
    kernels,
    psf_coeffs,
    prior_prec,
):
    side = sky_mean.shape[2]
    local = sky_mean.shape[1]
    tiles, filters = counts.shape
    sizes = (tiles, filters, local)
    kinds = kernels.shape[0]
    early, far_odd = [(1, 0), (2, 0), (2, 1)], (1, 1)
    early_moves = [(move, 0) for move in early]
    onward = local - local // 3
    last_moves = [(far_odd, 0)] + ([(far_odd, onward)] if onward < local else [])

    def last_images(near):
        across = [relay_across(near, onward)] if onward < local else []
        return [relay_onward(near, onward), *across]

    samples = lax.axis_size("mc")
    parts = lax.axis_size("filt")

    scale_map = jnp.exp(sky_log_scale[0])
    noise = noise_draw[0, 0]
    eps_float = noise.astype(jnp.float32)
    sample = sky_mean[0] + scale_map * eps_float
    sample_b = sample.astype(jnp.bfloat16)
    taps = kernels.reshape(2 * kinds, kernels.shape[2])

    image_f32 = jax.ShapeDtypeStruct((local, side, side), jnp.float32)
    image_b16 = jax.ShapeDtypeStruct((local, side, side), jnp.bfloat16)
    basis_type = jax.ShapeDtypeStruct((2 * kinds, side, side), jnp.bfloat16)
    cost = pl.CostEstimate(
        flops=2 * NB * 4 * side**3, bytes_accessed=8 * local * side * side, transcendentals=0
    )
    lines = pltpu.VMEM((2, 2 * kinds, side), jnp.float32)

    def slot_scratch(groups, ready):
        return [
            pltpu.SMEM((4, groups * local), jnp.int32),
            pltpu.VMEM((groups * local, side, side), jnp.bfloat16),
            pltpu.VMEM((side, side), ready),
        ]

    def call(kernel, name, outs, smem, vmem, scratch, aliases={}):
        return pl.pallas_call(
            kernel,
            out_shape=outs,
            in_specs=[SMEM] * len(smem) + [VMEM] * len(vmem),
            out_specs=[VMEM] * len(outs),
            scratch_shapes=scratch,
            input_output_aliases=aliases,
            compiler_params=pltpu.CompilerParams(vmem_limit_bytes=VMEM_BYTES),
            cost_estimate=cost,
            name=name,
        )(*smem, *vmem)

    near = {move: flipped(sample_b, "tile", move) for move in early}
    other_noise = [rotated(noise, "mc", r) for r in range(1, samples)]
    rows = -(-(2 * REACH + 1) * local // 8) * 8
    table, forth, back = call(
        functools.partial(prepare, sizes),
        "prepare",
        [
            jax.ShapeDtypeStruct((rows, LANES), jnp.float32),
            basis_type,
            basis_type,
        ],
        (),
        (
            intersections.transpose(1, 2, 0, 3),
            counts,
            psf_coeffs.transpose(1, 3, 0, 2),
            prior_prec,
            taps,
        ),
        [lines],
    )
    tables = (table,)
    (pred,) = call(
        functools.partial(forward_own, sizes),
        "forward_own",
        [image_f32],
        tables,
        (forth, sample_b),
        slot_scratch(1, jnp.bfloat16),
    )
    near[1, 0], pred = lax.optimization_barrier((near[1, 0], pred))
    near_last = last_images(near)
    (pred,) = call(
        functools.partial(forward_next, sizes, early_moves),
        "forward_next",
        [image_f32],
        tables,
        (forth, *[near[move] for move in early], pred),
        slot_scratch(len(early), jnp.bfloat16),
        {len(tables) + 1 + len(early): 0},
    )
    _, residual = call(
        functools.partial(forward_last, sizes, last_moves),
        "forward_last",
        [image_f32, image_b16],
        tables,
        (forth, *near_last, pred, observed[0], inv_var[0]),
        slot_scratch(1, jnp.bfloat16),
        {len(tables) + 1 + len(near_last): 0},
    )
    near_resid = {move: flipped(residual, "tile", move) for move in [*early, far_odd]}
    late_b, residual = lax.optimization_barrier((sample_b, residual))
    other_samples = [rotated(late_b, "filt", r) for r in range(1, parts)]
    grad, turn, *other_turns = call(
        functools.partial(backward_own, sizes, [(None, 0), early_moves[0]], samples),
        "backward_own",
        [image_f32] * (1 + samples),
        tables,
        (back, residual, near_resid[early[0]], scale_map, noise, *other_noise),
        slot_scratch(2, jnp.float32),
    )
    (grad,) = call(
        functools.partial(backward_next, sizes, early_moves[1:]),
        "backward_next",
        [image_f32],
        tables,
        (back, *[near_resid[move] for move in early[1:]], grad),
        slot_scratch(len(early) - 1, jnp.float32),
        {len(tables) + len(early): 0},
    )
    (grad,) = call(
        functools.partial(backward_prior, sizes),
        "backward_prior",
        [image_f32],
        tables,
        (grad, sample, *other_samples),
        [],
        {len(tables): 0},
    )
    (grad,) = call(
        functools.partial(backward_next, sizes, [(far_odd, 0)]),
        "backward_last",
        [image_f32],
        tables,
        (back, near_resid[far_odd], grad),
        slot_scratch(1, jnp.float32),
        {len(tables) + 2: 0},
    )
    mean_sum = grad
    scale_sum = grad * turn
    for r in range(1, samples):
        other_grad = rotated(grad, "mc", r)
        mean_sum = mean_sum + other_grad
        scale_sum = scale_sum + other_grad * other_turns[r - 1]
    return ((mean_sum / samples)[None], (scale_sum / samples + 1.0)[None])

def solution(mesh):
    placed = (
        P("tile", "filt", None, None),
        P("tile", "filt", None, None),
        P("mc", "tile", "filt", None, None),
        P("tile", "filt", None, None),
        P("tile", "filt", None, None),
        P(),
        P(),
        P(),
        P(),
        P(),
    )
    return jax.shard_map(
        body,
        mesh=mesh,
        in_specs=placed,
        out_specs=(P("tile", "filt", None, None), P("tile", "filt", None, None)),
        check_vma=False,
    )
```

```python
import functools

import jax
import jax.numpy as jnp
from jax import lax
from jax.experimental import pallas as pl
from jax.experimental.pallas import tpu as pltpu
from jax.sharding import PartitionSpec as P

NB = 6
K = 3
REACH = 2
HEAD = 3
STEP = 16
WEIGHTS = 64
PRIOR = 112
LANES = 128
VMEM_BYTES = 16 * 1024 * 1024
VMEM = pl.BlockSpec(memory_space=pltpu.VMEM)
SMEM = pl.BlockSpec(memory_space=pltpu.SMEM)


def shifted(x, axis, by):
    length = lax.axis_size(axis)
    pairs = [(i, i + by) for i in range(length) if 0 <= i + by < length]
    return lax.ppermute(x, axis, pairs)


def rotated(x, axis, by):
    length = lax.axis_size(axis)
    return lax.ppermute(x, axis, [(i, (i + by) % length) for i in range(length)])


def build_basis(taps_ref, lines_ref, basis_ref, adjoint):
    kinds, side = basis_ref.shape[0] // 2, basis_ref.shape[1]
    count = taps_ref.shape[1]
    half = (count - 1) // 2
    taps = taps_ref[...].astype(jnp.bfloat16)
    tap = lax.broadcasted_iota(jnp.int32, (count, side), 0)
    lane = lax.broadcasted_iota(jnp.int32, (count, side), 1)
    lane = jnp.where(lane < side // 2, lane, lane - side)
    plain = (lane == half - tap).astype(jnp.float32).astype(jnp.bfloat16)
    turned = (lane == tap - half).astype(jnp.float32).astype(jnp.bfloat16)
    lines_ref[0] = dot(taps, turned if adjoint else plain)
    lines_ref[1] = dot(taps, plain if adjoint else turned)
    apart = lax.broadcasted_iota(jnp.int32, (side, side), 0) - lax.broadcasted_iota(
        jnp.int32, (side, side), 1
    )
    band = jnp.abs(apart) <= half

    def one(k, carry):
        for c in range(2):
            line = jnp.broadcast_to(lines_ref[c, pl.ds(2 * k + c, 1), :], (side, side))
            rows = pltpu.roll(line, 0, 1, stride=1, stride_axis=0)
            basis_ref[c * kinds + k] = jnp.where(band, rows, 0.0).astype(jnp.bfloat16)
        return carry

    lax.fori_loop(0, kinds, one, 0)


def fill_table(sizes, inter_ref, counts_ref, coeff_ref, prec_ref, table_ref):
    tiles, filters, local = sizes
    fields = inter_ref.shape[3]
    own = lax.axis_index("tile")
    first = lax.axis_index("filt") * local
    row_id = lax.broadcasted_iota(jnp.int32, (tiles, NB), 0)
    lane_id = lax.broadcasted_iota(jnp.int32, (1, filters), 1)
    for w in range(2 * REACH + 1):
        tile = jnp.clip(own + w - REACH, 0, tiles - 1)
        live = counts_ref[pl.ds(tile, 1), :]
        for f in range(local):
            row = w * local + f
            for q in range(K):
                entry = inter_ref[first + f, q, pl.ds(tile, 1), :]
                table_ref[row : row + 1, STEP * q : STEP * q + fields] = entry.astype(jnp.float32)
            count = jnp.where(lane_id == first + f, live, 0).astype(jnp.float32)
            table_ref[row : row + 1, STEP * K : STEP * K + 1] = jnp.sum(count, 1, keepdims=True)
            for c in range(3):
                block = coeff_ref[first + f, c].astype(jnp.float32)
                picked = jnp.sum(jnp.where(row_id == tile, block, 0.0), 0, keepdims=True)
                at = WEIGHTS + STEP * c
                table_ref[row : row + 1, at : at + NB] = picked
    for f in range(local):
        table_ref[f : f + 1, PRIOR : PRIOR + filters] = prec_ref[pl.ds(first + f, 1), :]


def number(table_ref, row, at):
    return table_ref[row, at].astype(jnp.int32)


def find_slot(table_ref, row, expo):
    live = number(table_ref, row, STEP * K)
    base = jnp.int32(0)
    found = jnp.int32(0)
    for q in range(K):
        hit = (q < live) & (number(table_ref, row, STEP * q) == expo)
        base = jnp.where(hit, STEP * q, base)
        found = jnp.where(hit, 1, found)
    return found, base


def weight(table_ref, row, b, row_centred, col_centred):
    at = WEIGHTS + b
    flat = table_ref[row, at] + table_ref[row, at + STEP] * row_centred
    return flat + table_ref[row, at + 2 * STEP] * col_centred


def centred_axes(side, oy, ox):
    rows = lax.broadcasted_iota(jnp.int32, (side, 1), 0) + oy
    cols = lax.broadcasted_iota(jnp.int32, (1, side), 1) + ox
    return (
        (2 * rows + 1 - side).astype(jnp.float32) / side,
        (2 * cols + 1 - side).astype(jnp.float32) / side,
    )


def moved_by(image, down, across):
    side = image.shape[0]
    turned = pltpu.roll(image, lax.rem(across + side, side), 1)
    turned = pltpu.roll(turned, lax.rem(down + side, side), 0)
    row = lax.broadcasted_iota(jnp.int32, (side, 1), 0) - down
    col = lax.broadcasted_iota(jnp.int32, (1, side), 1) - across
    row_inside = jnp.where((row >= 0) & (row < side), 1.0, 0.0)
    col_inside = jnp.where((col >= 0) & (col < side), 1.0, 0.0)
    return turned * row_inside * col_inside


def dot(a, b):
    return jnp.dot(a, b, preferred_element_type=jnp.float32)


def contribution(table_ref, basis_ref, row, base, place, image):
    side = image.shape[0]
    kinds = basis_ref.shape[0] // 2
    row_centred, col_centred = centred_axes(
        side, number(table_ref, row, base + 1), number(table_ref, row, base + 2)
    )
    total = jnp.zeros((side, side), jnp.float32)
    chosen = [number(table_ref, row, base + HEAD + b) for b in range(NB)]
    half_blurs = dot(jnp.concatenate([basis_ref[k] for k in chosen], 0), image).astype(jnp.bfloat16)
    for b in range(0, NB, 2):
        pair = jnp.zeros((side, side), jnp.float32)
        for c in range(b, min(b + 2, NB)):
            blurred = dot(half_blurs[c * side : (c + 1) * side], basis_ref[kinds + chosen[c]])
            pair = pair + weight(table_ref, place, c, row_centred, col_centred) * blurred
        total = total + pair
    return total.astype(jnp.bfloat16)


def adjoint_term(table_ref, basis_ref, row, base, place, moved):
    side = moved.shape[0]
    kinds = basis_ref.shape[0] // 2
    row_centred, col_centred = centred_axes(
        side, number(table_ref, row, base + 1), number(table_ref, row, base + 2)
    )
    chosen = [number(table_ref, row, base + HEAD + b) for b in range(NB)]
    back_halves = []
    for b in range(NB):
        w = weight(table_ref, place, b, row_centred, col_centred)
        back_half = dot(basis_ref[chosen[b]], (w * moved).astype(jnp.bfloat16))
        back_halves.append(back_half.astype(jnp.bfloat16))
    right = jnp.concatenate([basis_ref[kinds + k] for k in chosen], 0)
    return dot(jnp.concatenate(back_halves, 1), right)


def source_of(own, move):
    distance, parity = move
    return own + jnp.where(lax.rem(own // distance, 2) == parity, distance, -distance)


def flipped(x, axis, move):
    distance, parity = move
    length = lax.axis_size(axis)
    firsts = [i for i in range(length - distance) if (i // distance) % 2 == parity]
    pairs = [(i, i + distance) for i in firsts] + [(i + distance, i) for i in firsts]
    return lax.ppermute(x, axis, pairs)


def relay_onward(near, count):
    length = lax.axis_size("tile")
    pairs = [(i, i + 2) for i in range(0, length - 2, 2)]
    pairs += [(i, i - 2) for i in range(3, length, 2)]
    return lax.ppermute(near[1, 0][:count], "tile", pairs)


def relay_across(near, count):
    own = lax.axis_index("tile")
    first = lax.rem(own, 2) == lax.rem(own // 2, 2)
    image = jnp.where(first, near[2, 0][count:], near[2, 1][count:])
    return flipped(image, "tile", (1, 0))


def gather_live(sizes, moves, backward, table_ref, images, list_ref, held_ref):
    tiles, filters, local = sizes
    own = lax.axis_index("tile")
    live = jnp.int32(0)
    for (move, f_first), image_ref in zip(moves, images):
        far = own if move is None else source_of(own, move)
        inside = jnp.where((far >= 0) & (far < tiles), 1, 0)
        here, there = REACH * local, jnp.clip(far - own + REACH, 0, 2 * REACH) * local
        tile_at, expo_at = (here, there) if backward else (there, here)
        expo = far if backward else own
        for f in range(f_first, f_first + image_ref.shape[0]):
            found, base = find_slot(table_ref, tile_at + f, expo)
            found = found * inside

            @pl.when(found == 1)
            def _():
                list_ref[0, live] = f
                list_ref[1, live] = tile_at + f
                list_ref[2, live] = base
                list_ref[3, live] = expo_at + f
                held_ref[live] = image_ref[f - f_first]

            live = live + found
    return live


def forward_slots(sizes, moves, table_ref, basis_ref, images, pred_ref, scratch):
    list_ref, held_ref, ready_ref = scratch
    live = gather_live(sizes, moves, False, table_ref, images, list_ref, held_ref)

    @pl.when(live > 0)
    def _():
        def blur(n):
            ready_ref[...] = contribution(
                table_ref,
                basis_ref,
                list_ref[1, n],
                list_ref[2, n],
                list_ref[3, n],
                held_ref[n],
            )

        def settle(n):
            row, base = list_ref[1, n], list_ref[2, n]
            oy, ox = number(table_ref, row, base + 1), number(table_ref, row, base + 2)
            f = list_ref[0, n]
            pred_ref[f] = pred_ref[f] + moved_by(ready_ref[...].astype(jnp.float32), oy, ox)

        def one(n, carry):
            settle(n - 1)
            blur(n)
            return carry

        blur(0)
        lax.fori_loop(1, live, one, 0)
        settle(live - 1)


def backward_slots(sizes, moves, table_ref, basis_ref, images, grad_ref, scratch):
    list_ref, held_ref, ready_ref = scratch
    live = gather_live(sizes, moves, True, table_ref, images, list_ref, held_ref)

    @pl.when(live > 0)
    def _():
        def bring(n):
            row, base = list_ref[1, n], list_ref[2, n]
            oy, ox = number(table_ref, row, base + 1), number(table_ref, row, base + 2)
            return moved_by(held_ref[n].astype(jnp.float32), -oy, -ox)

        def take(n):
            f = list_ref[0, n]
            grad_ref[f] = grad_ref[f] + adjoint_term(
                table_ref,
                basis_ref,
                list_ref[1, n],
                list_ref[2, n],
                list_ref[3, n],
                ready_ref[...],
            )

        def one(n, carry):
            following = bring(n)
            take(n - 1)
            ready_ref[...] = following
            return carry

        ready_ref[...] = bring(0)
        lax.fori_loop(1, live, one, 0)
        take(live - 1)


def prepare(sizes, inter_ref, counts_ref, coeff_ref, prec_ref, taps_ref, *refs):
    table_ref, forth_ref, back_ref, lines_ref = refs
    fill_table(sizes, inter_ref, counts_ref, coeff_ref, prec_ref, table_ref)
    build_basis(taps_ref, lines_ref, forth_ref, False)
    build_basis(taps_ref, lines_ref, back_ref, True)


def forward_own(sizes, table_ref, basis_ref, image_ref, *refs):
    pred_ref, *scratch = refs
    pred_ref[...] = jnp.zeros_like(pred_ref)
    forward_slots(sizes, [(None, 0)], table_ref, basis_ref, [image_ref], pred_ref, scratch)


def forward_next(sizes, moves, table_ref, basis_ref, *refs):
    images, (before_ref, pred_ref, *scratch) = refs[: len(moves)], refs[len(moves) :]
    del before_ref
    forward_slots(sizes, moves, table_ref, basis_ref, images, pred_ref, scratch)


def forward_last(sizes, moves, table_ref, basis_ref, *refs):
    images, refs = refs[: len(moves)], refs[len(moves) :]
    before_ref, observed_ref, inv_ref, pred_ref, resid_ref, *scratch = refs
    del before_ref
    forward_slots(sizes, moves, table_ref, basis_ref, images, pred_ref, scratch)
    for f in range(observed_ref.shape[0]):
        gap = observed_ref[f].astype(jnp.float32) - pred_ref[f]
        resid_ref[f] = (inv_ref[f].astype(jnp.float32) * gap).astype(jnp.bfloat16)


def subtract_prior(sizes, table_ref, sample_ref, others, grad_ref):
    tiles, filters, local = sizes
    part = lax.axis_index("filt")
    parts = filters // local
    first = part * local
    for f in range(local):
        grad = grad_ref[f]
        for g in range(local):
            grad = grad - table_ref[f, PRIOR + first + g] * sample_ref[g]
        for r in range(1, parts):
            source = lax.rem(part + parts - r, parts) * local
            for g in range(local):
                far = others[r - 1][g].astype(jnp.float32)
                grad = grad - table_ref[f, PRIOR + source + g] * far
        grad_ref[f] = grad


def backward_own(sizes, moves, samples, table_ref, basis_ref, *refs):
    images, (scale_ref, *refs) = refs[: len(moves)], refs[len(moves) :]
    noises, (grad_ref, *refs) = refs[:samples], refs[samples:]
    turns, scratch = refs[:samples], refs[samples:]
    for noise_ref, turn_ref in zip(noises, turns):
        turn_ref[...] = scale_ref[...] * noise_ref[...].astype(jnp.float32)
    grad_ref[...] = jnp.zeros_like(grad_ref)
    backward_slots(sizes, moves, table_ref, basis_ref, images, grad_ref, scratch)


def backward_next(sizes, moves, table_ref, basis_ref, *refs):
    images, (before_ref, grad_ref, *scratch) = refs[: len(moves)], refs[len(moves) :]
    del before_ref
    backward_slots(sizes, moves, table_ref, basis_ref, images, grad_ref, scratch)


def backward_prior(sizes, table_ref, before_ref, sample_ref, *refs):
    others, (grad_ref,) = refs[:-1], refs[-1:]
    del before_ref
    subtract_prior(sizes, table_ref, sample_ref, others, grad_ref)


def body(
    sky_mean,
    sky_log_scale,
    noise_draw,
    observed,
    inv_var,
    intersections,
    counts,
    kernels,
    psf_coeffs,
    prior_prec,
):
    side = sky_mean.shape[2]
    local = sky_mean.shape[1]
    tiles, filters = counts.shape
    sizes = (tiles, filters, local)
    kinds = kernels.shape[0]
    early, far_odd = [(1, 0), (2, 0), (2, 1)], (1, 1)
    early_moves = [(move, 0) for move in early]
    onward = local - local // 3
    last_moves = [(far_odd, 0)] + ([(far_odd, onward)] if onward < local else [])

    def last_images(near):
        across = [relay_across(near, onward)] if onward < local else []
        return [relay_onward(near, onward), *across]

    samples = lax.axis_size("mc")
    parts = lax.axis_size("filt")

    scale_map = jnp.exp(sky_log_scale[0])
    noise = noise_draw[0, 0]
    eps_float = noise.astype(jnp.float32)
    sample = sky_mean[0] + scale_map * eps_float
    sample_b = sample.astype(jnp.bfloat16)
    taps = kernels.reshape(2 * kinds, kernels.shape[2])

    image_f32 = jax.ShapeDtypeStruct((local, side, side), jnp.float32)
    image_b16 = jax.ShapeDtypeStruct((local, side, side), jnp.bfloat16)
    basis_type = jax.ShapeDtypeStruct((2 * kinds, side, side), jnp.bfloat16)
    cost = pl.CostEstimate(
        flops=2 * NB * 4 * side**3, bytes_accessed=8 * local * side * side, transcendentals=0
    )
    lines = pltpu.VMEM((2, 2 * kinds, side), jnp.float32)

    def slot_scratch(groups, ready):
        return [
            pltpu.SMEM((4, groups * local), jnp.int32),
            pltpu.VMEM((groups * local, side, side), jnp.bfloat16),
            pltpu.VMEM((side, side), ready),
        ]

    def call(kernel, name, outs, smem, vmem, scratch, aliases={}):
        return pl.pallas_call(
            kernel,
            out_shape=outs,
            in_specs=[SMEM] * len(smem) + [VMEM] * len(vmem),
            out_specs=[VMEM] * len(outs),
            scratch_shapes=scratch,
            input_output_aliases=aliases,
            compiler_params=pltpu.CompilerParams(vmem_limit_bytes=VMEM_BYTES),
            cost_estimate=cost,
            name=name,
        )(*smem, *vmem)

    near = {move: flipped(sample_b, "tile", move) for move in early}
    other_noise = [rotated(noise, "mc", r) for r in range(1, samples)]
    rows = -(-(2 * REACH + 1) * local // 8) * 8
    table, forth, back = call(
        functools.partial(prepare, sizes),
        "prepare",
        [
            jax.ShapeDtypeStruct((rows, LANES), jnp.float32),
            basis_type,
            basis_type,
        ],
        (),
        (
            intersections.transpose(1, 2, 0, 3),
            counts,
            psf_coeffs.transpose(1, 3, 0, 2),
            prior_prec,
            taps,
        ),
        [lines],
    )
    tables = (table,)
    (pred,) = call(
        functools.partial(forward_own, sizes),
        "forward_own",
        [image_f32],
        tables,
        (forth, sample_b),
        slot_scratch(1, jnp.bfloat16),
    )
    near[1, 0], pred = lax.optimization_barrier((near[1, 0], pred))
    near_last = last_images(near)
    (pred,) = call(
        functools.partial(forward_next, sizes, early_moves),
        "forward_next",
        [image_f32],
        tables,
        (forth, *[near[move] for move in early], pred),
        slot_scratch(len(early), jnp.bfloat16),
        {len(tables) + 1 + len(early): 0},
    )
    _, residual = call(
        functools.partial(forward_last, sizes, last_moves),
        "forward_last",
        [image_f32, image_b16],
        tables,
        (forth, *near_last, pred, observed[0], inv_var[0]),
        slot_scratch(1, jnp.bfloat16),
        {len(tables) + 1 + len(near_last): 0},
    )
    near_resid = {move: flipped(residual, "tile", move) for move in [*early, far_odd]}
    late_b, residual = lax.optimization_barrier((sample_b, residual))
    other_samples = [rotated(late_b, "filt", r) for r in range(1, parts)]
    grad, turn, *other_turns = call(
        functools.partial(backward_own, sizes, [(None, 0), early_moves[0]], samples),
        "backward_own",
        [image_f32] * (1 + samples),
        tables,
        (back, residual, near_resid[early[0]], scale_map, noise, *other_noise),
        slot_scratch(2, jnp.float32),
    )
    (grad,) = call(
        functools.partial(backward_next, sizes, early_moves[1:]),
        "backward_next",
        [image_f32],
        tables,
        (back, *[near_resid[move] for move in early[1:]], grad),
        slot_scratch(len(early) - 1, jnp.float32),
        {len(tables) + len(early): 0},
    )
    (grad,) = call(
        functools.partial(backward_prior, sizes),
        "backward_prior",
        [image_f32],
        tables,
        (grad, sample, *other_samples),
        [],
        {len(tables): 0},
    )
    (grad,) = call(
        functools.partial(backward_next, sizes, [(far_odd, 0)]),
        "backward_last",
        [image_f32],
        tables,
        (back, near_resid[far_odd], grad),
        slot_scratch(1, jnp.float32),
        {len(tables) + 2: 0},
    )
    mean_sum = grad
    scale_sum = grad * turn
    for r in range(1, samples):
        other_grad = rotated(grad, "mc", r)
        mean_sum = mean_sum + other_grad
        scale_sum = scale_sum + other_grad * other_turns[r - 1]
    return ((mean_sum / samples)[None], (scale_sum / samples + 1.0)[None])

def solution(mesh):
    placed = (
        P("tile", "filt", None, None),
        P("tile", "filt", None, None),
        P("mc", "tile", "filt", None, None),
        P("tile", "filt", None, None),
        P("tile", "filt", None, None),
        P(),
        P(),
        P(),
        P(),
        P(),
    )
    return jax.shard_map(
        body,
        mesh=mesh,
        in_specs=placed,
        out_specs=(P("tile", "filt", None, None), P("tile", "filt", None, None)),
        check_vma=False,
    )
```

```python
import functools

import jax
import jax.numpy as jnp
from jax import lax
from jax.experimental import pallas as pl
from jax.experimental.pallas import tpu as pltpu
from jax.sharding import PartitionSpec as P

NB = 6
K = 3
REACH = 2
HEAD = 3
STEP = 16
WEIGHTS = 64
PRIOR = 112
LANES = 128
VMEM_BYTES = 16 * 1024 * 1024
VMEM = pl.BlockSpec(memory_space=pltpu.VMEM)
SMEM = pl.BlockSpec(memory_space=pltpu.SMEM)


def shifted(x, axis, by):
    length = lax.axis_size(axis)
    pairs = [(i, i + by) for i in range(length) if 0 <= i + by < length]
    return lax.ppermute(x, axis, pairs)


def rotated(x, axis, by):
    length = lax.axis_size(axis)
    return lax.ppermute(x, axis, [(i, (i + by) % length) for i in range(length)])


def build_basis(taps_ref, lines_ref, basis_ref, adjoint):
    kinds, side = basis_ref.shape[0] // 2, basis_ref.shape[1]
    count = taps_ref.shape[1]
    half = (count - 1) // 2
    taps = taps_ref[...].astype(jnp.bfloat16)
    tap = lax.broadcasted_iota(jnp.int32, (count, side), 0)
    lane = lax.broadcasted_iota(jnp.int32, (count, side), 1)
    lane = jnp.where(lane < side // 2, lane, lane - side)
    plain = (lane == half - tap).astype(jnp.float32).astype(jnp.bfloat16)
    turned = (lane == tap - half).astype(jnp.float32).astype(jnp.bfloat16)
    lines_ref[0] = dot(taps, turned if adjoint else plain)
    lines_ref[1] = dot(taps, plain if adjoint else turned)
    apart = lax.broadcasted_iota(jnp.int32, (side, side), 0) - lax.broadcasted_iota(
        jnp.int32, (side, side), 1
    )
    band = jnp.abs(apart) <= half

    def one(k, carry):
        for c in range(2):
            line = jnp.broadcast_to(lines_ref[c, pl.ds(2 * k + c, 1), :], (side, side))
            rows = pltpu.roll(line, 0, 1, stride=1, stride_axis=0)
            basis_ref[c * kinds + k] = jnp.where(band, rows, 0.0).astype(jnp.bfloat16)
        return carry

    lax.fori_loop(0, kinds, one, 0)


def fill_table(sizes, inter_ref, counts_ref, coeff_ref, prec_ref, table_ref):
    tiles, filters, local = sizes
    fields = inter_ref.shape[3]
    own = lax.axis_index("tile")
    first = lax.axis_index("filt") * local
    row_id = lax.broadcasted_iota(jnp.int32, (tiles, NB), 0)
    lane_id = lax.broadcasted_iota(jnp.int32, (1, filters), 1)
    for w in range(2 * REACH + 1):
        tile = jnp.clip(own + w - REACH, 0, tiles - 1)
        live = counts_ref[pl.ds(tile, 1), :]
        for f in range(local):
            row = w * local + f
            for q in range(K):
                entry = inter_ref[first + f, q, pl.ds(tile, 1), :]
                table_ref[row : row + 1, STEP * q : STEP * q + fields] = entry.astype(jnp.float32)
            count = jnp.where(lane_id == first + f, live, 0).astype(jnp.float32)
            table_ref[row : row + 1, STEP * K : STEP * K + 1] = jnp.sum(count, 1, keepdims=True)
            for c in range(3):
                block = coeff_ref[first + f, c].astype(jnp.float32)
                picked = jnp.sum(jnp.where(row_id == tile, block, 0.0), 0, keepdims=True)
                at = WEIGHTS + STEP * c
                table_ref[row : row + 1, at : at + NB] = picked
    for f in range(local):
        table_ref[f : f + 1, PRIOR : PRIOR + filters] = prec_ref[pl.ds(first + f, 1), :]


def number(table_ref, row, at):
    return table_ref[row, at].astype(jnp.int32)


def find_slot(table_ref, row, expo):
    live = number(table_ref, row, STEP * K)
    base = jnp.int32(0)
    found = jnp.int32(0)
    for q in range(K):
        hit = (q < live) & (number(table_ref, row, STEP * q) == expo)
        base = jnp.where(hit, STEP * q, base)
        found = jnp.where(hit, 1, found)
    return found, base


def weight(table_ref, row, b, row_centred, col_centred):
    at = WEIGHTS + b
    flat = table_ref[row, at] + table_ref[row, at + STEP] * row_centred
    return flat + table_ref[row, at + 2 * STEP] * col_centred


def centred_axes(side, oy, ox):
    rows = lax.broadcasted_iota(jnp.int32, (side, 1), 0) + oy
    cols = lax.broadcasted_iota(jnp.int32, (1, side), 1) + ox
    return (
        (2 * rows + 1 - side).astype(jnp.float32) / side,
        (2 * cols + 1 - side).astype(jnp.float32) / side,
    )


def moved_by(image, down, across):
    side = image.shape[0]
    turned = pltpu.roll(image, lax.rem(across + side, side), 1)
    turned = pltpu.roll(turned, lax.rem(down + side, side), 0)
    row = lax.broadcasted_iota(jnp.int32, (side, side), 0) - down
    col = lax.broadcasted_iota(jnp.int32, (side, side), 1) - across
    inside = (row >= 0) & (row < side) & (col >= 0) & (col < side)
    return jnp.where(inside, turned, 0.0)


def dot(a, b):
    return jnp.dot(a, b, preferred_element_type=jnp.float32)


def contribution(table_ref, basis_ref, row, base, place, image):
    side = image.shape[0]
    kinds = basis_ref.shape[0] // 2
    row_centred, col_centred = centred_axes(
        side, number(table_ref, row, base + 1), number(table_ref, row, base + 2)
    )
    total = jnp.zeros((side, side), jnp.float32)
    chosen = [number(table_ref, row, base + HEAD + b) for b in range(NB)]
    half_blurs = dot(jnp.concatenate([basis_ref[k] for k in chosen], 0), image).astype(jnp.bfloat16)
    for b in range(0, NB, 2):
        pair = jnp.zeros((side, side), jnp.float32)
        for c in range(b, min(b + 2, NB)):
            blurred = dot(half_blurs[c * side : (c + 1) * side], basis_ref[kinds + chosen[c]])
            pair = pair + weight(table_ref, place, c, row_centred, col_centred) * blurred
        total = total + pair
    return total.astype(jnp.bfloat16)


def adjoint_term(table_ref, basis_ref, row, base, place, moved):
    side = moved.shape[0]
    kinds = basis_ref.shape[0] // 2
    row_centred, col_centred = centred_axes(
        side, number(table_ref, row, base + 1), number(table_ref, row, base + 2)
    )
    chosen = [number(table_ref, row, base + HEAD + b) for b in range(NB)]
    back_halves = []
    for b in range(NB):
        w = weight(table_ref, place, b, row_centred, col_centred)
        back_half = dot(basis_ref[chosen[b]], (w * moved).astype(jnp.bfloat16))
        back_halves.append(back_half.astype(jnp.bfloat16))
    right = jnp.concatenate([basis_ref[kinds + k] for k in chosen], 0)
    return dot(jnp.concatenate(back_halves, 1), right)


def source_of(own, move):
    distance, parity = move
    return own + jnp.where(lax.rem(own // distance, 2) == parity, distance, -distance)


def flipped(x, axis, move):
    distance, parity = move
    length = lax.axis_size(axis)
    firsts = [i for i in range(length - distance) if (i // distance) % 2 == parity]
    pairs = [(i, i + distance) for i in firsts] + [(i + distance, i) for i in firsts]
    return lax.ppermute(x, axis, pairs)


def relay_onward(near, count):
    length = lax.axis_size("tile")
    pairs = [(i, i + 2) for i in range(0, length - 2, 2)]
    pairs += [(i, i - 2) for i in range(3, length, 2)]
    return lax.ppermute(near[1, 0][:count], "tile", pairs)


def relay_across(near, count):
    own = lax.axis_index("tile")
    first = lax.rem(own, 2) == lax.rem(own // 2, 2)
    image = jnp.where(first, near[2, 0][count:], near[2, 1][count:])
    return flipped(image, "tile", (1, 0))


def gather_live(sizes, moves, backward, table_ref, images, list_ref, held_ref):
    tiles, filters, local = sizes
    own = lax.axis_index("tile")
    live = jnp.int32(0)
    for (move, f_first), image_ref in zip(moves, images):
        far = own if move is None else source_of(own, move)
        inside = jnp.where((far >= 0) & (far < tiles), 1, 0)
        here, there = REACH * local, jnp.clip(far - own + REACH, 0, 2 * REACH) * local
        tile_at, expo_at = (here, there) if backward else (there, here)
        expo = far if backward else own
        for f in range(f_first, f_first + image_ref.shape[0]):
            found, base = find_slot(table_ref, tile_at + f, expo)
            found = found * inside

            @pl.when(found == 1)
            def _():
                list_ref[0, live] = f
                list_ref[1, live] = tile_at + f
                list_ref[2, live] = base
                list_ref[3, live] = expo_at + f
                held_ref[live] = image_ref[f - f_first]

            live = live + found
    return live


def forward_slots(sizes, moves, table_ref, basis_ref, images, pred_ref, scratch):
    list_ref, held_ref, ready_ref = scratch
    live = gather_live(sizes, moves, False, table_ref, images, list_ref, held_ref)

    @pl.when(live > 0)
    def _():
        def blur(n):
            ready_ref[...] = contribution(
                table_ref,
                basis_ref,
                list_ref[1, n],
                list_ref[2, n],
                list_ref[3, n],
                held_ref[n],
            )

        def settle(n):
            row, base = list_ref[1, n], list_ref[2, n]
            oy, ox = number(table_ref, row, base + 1), number(table_ref, row, base + 2)
            f = list_ref[0, n]
            pred_ref[f] = pred_ref[f] + moved_by(ready_ref[...].astype(jnp.float32), oy, ox)

        def one(n, carry):
            settle(n - 1)
            blur(n)
            return carry

        blur(0)
        lax.fori_loop(1, live, one, 0)
        settle(live - 1)


def backward_slots(sizes, moves, table_ref, basis_ref, images, grad_ref, scratch):
    list_ref, held_ref, ready_ref = scratch
    live = gather_live(sizes, moves, True, table_ref, images, list_ref, held_ref)

    @pl.when(live > 0)
    def _():
        def bring(n):
            row, base = list_ref[1, n], list_ref[2, n]
            oy, ox = number(table_ref, row, base + 1), number(table_ref, row, base + 2)
            return moved_by(held_ref[n].astype(jnp.float32), -oy, -ox)

        def take(n):
            f = list_ref[0, n]
            grad_ref[f] = grad_ref[f] + adjoint_term(
                table_ref,
                basis_ref,
                list_ref[1, n],
                list_ref[2, n],
                list_ref[3, n],
                ready_ref[...],
            )

        def one(n, carry):
            following = bring(n)
            take(n - 1)
            ready_ref[...] = following
            return carry

        ready_ref[...] = bring(0)
        lax.fori_loop(1, live, one, 0)
        take(live - 1)


def prepare(sizes, inter_ref, counts_ref, coeff_ref, prec_ref, taps_ref, *refs):
    table_ref, forth_ref, back_ref, lines_ref = refs
    fill_table(sizes, inter_ref, counts_ref, coeff_ref, prec_ref, table_ref)
    build_basis(taps_ref, lines_ref, forth_ref, False)
    build_basis(taps_ref, lines_ref, back_ref, True)


def forward_own(sizes, table_ref, basis_ref, image_ref, *refs):
    pred_ref, *scratch = refs
    pred_ref[...] = jnp.zeros_like(pred_ref)
    forward_slots(sizes, [(None, 0)], table_ref, basis_ref, [image_ref], pred_ref, scratch)


def forward_next(sizes, moves, table_ref, basis_ref, *refs):
    images, (before_ref, pred_ref, *scratch) = refs[: len(moves)], refs[len(moves) :]
    del before_ref
    forward_slots(sizes, moves, table_ref, basis_ref, images, pred_ref, scratch)


def forward_last(sizes, moves, table_ref, basis_ref, *refs):
    images, refs = refs[: len(moves)], refs[len(moves) :]
    before_ref, observed_ref, inv_ref, pred_ref, resid_ref, *scratch = refs
    del before_ref
    forward_slots(sizes, moves, table_ref, basis_ref, images, pred_ref, scratch)
    for f in range(observed_ref.shape[0]):
        gap = observed_ref[f].astype(jnp.float32) - pred_ref[f]
        resid_ref[f] = (inv_ref[f].astype(jnp.float32) * gap).astype(jnp.bfloat16)


def subtract_prior(sizes, table_ref, sample_ref, others, grad_ref):
    tiles, filters, local = sizes
    part = lax.axis_index("filt")
    parts = filters // local
    first = part * local
    for f in range(local):
        grad = grad_ref[f]
        for g in range(local):
            grad = grad - table_ref[f, PRIOR + first + g] * sample_ref[g]
        for r in range(1, parts):
            source = lax.rem(part + parts - r, parts) * local
            for g in range(local):
                far = others[r - 1][g].astype(jnp.float32)
                grad = grad - table_ref[f, PRIOR + source + g] * far
        grad_ref[f] = grad


def backward_own(sizes, moves, samples, table_ref, basis_ref, *refs):
    images, (scale_ref, *refs) = refs[: len(moves)], refs[len(moves) :]
    noises, (grad_ref, *refs) = refs[:samples], refs[samples:]
    turns, scratch = refs[:samples], refs[samples:]
    for noise_ref, turn_ref in zip(noises, turns):
        turn_ref[...] = scale_ref[...] * noise_ref[...].astype(jnp.float32)
    grad_ref[...] = jnp.zeros_like(grad_ref)
    backward_slots(sizes, moves, table_ref, basis_ref, images, grad_ref, scratch)


def backward_next(sizes, moves, table_ref, basis_ref, *refs):
    images, (before_ref, grad_ref, *scratch) = refs[: len(moves)], refs[len(moves) :]
    del before_ref
    backward_slots(sizes, moves, table_ref, basis_ref, images, grad_ref, scratch)


def backward_prior(sizes, table_ref, before_ref, sample_ref, *refs):
    others, (grad_ref,) = refs[:-1], refs[-1:]
    del before_ref
    subtract_prior(sizes, table_ref, sample_ref, others, grad_ref)


def body(
    sky_mean,
    sky_log_scale,
    noise_draw,
    observed,
    inv_var,
    intersections,
    counts,
    kernels,
    psf_coeffs,
    prior_prec,
):
    side = sky_mean.shape[2]
    local = sky_mean.shape[1]
    tiles, filters = counts.shape
    sizes = (tiles, filters, local)
    kinds = kernels.shape[0]
    early, far_odd = [(1, 0), (2, 0), (2, 1)], (1, 1)
    early_moves = [(move, 0) for move in early]
    onward = local - local // 3
    last_moves = [(far_odd, 0)] + ([(far_odd, onward)] if onward < local else [])

    def last_images(near):
        across = [relay_across(near, onward)] if onward < local else []
        return [relay_onward(near, onward), *across]

    samples = lax.axis_size("mc")
    parts = lax.axis_size("filt")

    scale_map = jnp.exp(sky_log_scale[0])
    noise = noise_draw[0, 0]
    eps_float = noise.astype(jnp.float32)
    sample = sky_mean[0] + scale_map * eps_float
    sample_b = sample.astype(jnp.bfloat16)
    taps = kernels.reshape(2 * kinds, kernels.shape[2])

    image_f32 = jax.ShapeDtypeStruct((local, side, side), jnp.float32)
    image_b16 = jax.ShapeDtypeStruct((local, side, side), jnp.bfloat16)
    basis_type = jax.ShapeDtypeStruct((2 * kinds, side, side), jnp.bfloat16)
    cost = pl.CostEstimate(
        flops=2 * NB * 4 * side**3, bytes_accessed=8 * local * side * side, transcendentals=0
    )
    lines = pltpu.VMEM((2, 2 * kinds, side), jnp.float32)

    def slot_scratch(groups, ready):
        return [
            pltpu.SMEM((4, groups * local), jnp.int32),
            pltpu.VMEM((groups * local, side, side), jnp.bfloat16),
            pltpu.VMEM((side, side), ready),
        ]

    def call(kernel, name, outs, smem, vmem, scratch, aliases={}):
        return pl.pallas_call(
            kernel,
            out_shape=outs,
            in_specs=[SMEM] * len(smem) + [VMEM] * len(vmem),
            out_specs=[VMEM] * len(outs),
            scratch_shapes=scratch,
            input_output_aliases=aliases,
            compiler_params=pltpu.CompilerParams(vmem_limit_bytes=VMEM_BYTES),
            cost_estimate=cost,
            name=name,
        )(*smem, *vmem)

    near = {move: flipped(sample_b, "tile", move) for move in early}
    other_noise = [rotated(noise, "mc", r) for r in range(1, samples)]
    rows = -(-(2 * REACH + 1) * local // 8) * 8
    table, forth, back = call(
        functools.partial(prepare, sizes),
        "prepare",
        [
            jax.ShapeDtypeStruct((rows, LANES), jnp.float32),
            basis_type,
            basis_type,
        ],
        (),
        (
            intersections.transpose(1, 2, 0, 3),
            counts,
            psf_coeffs.transpose(1, 3, 0, 2),
            prior_prec,
            taps,
        ),
        [lines],
    )
    tables = (table,)
    (pred,) = call(
        functools.partial(forward_own, sizes),
        "forward_own",
        [image_f32],
        tables,
        (forth, sample_b),
        slot_scratch(1, jnp.bfloat16),
    )
    near[1, 0], pred = lax.optimization_barrier((near[1, 0], pred))
    near_last = last_images(near)
    (pred,) = call(
        functools.partial(forward_next, sizes, early_moves),
        "forward_next",
        [image_f32],
        tables,
        (forth, *[near[move] for move in early], pred),
        slot_scratch(len(early), jnp.bfloat16),
        {len(tables) + 1 + len(early): 0},
    )
    _, residual = call(
        functools.partial(forward_last, sizes, last_moves),
        "forward_last",
        [image_f32, image_b16],
        tables,
        (forth, *near_last, pred, observed[0], inv_var[0]),
        slot_scratch(1, jnp.bfloat16),
        {len(tables) + 1 + len(near_last): 0},
    )
    mean_late, scale_late, noise_late, residual = lax.optimization_barrier(
        (sky_mean[0], sky_log_scale[0], noise, residual)
    )
    scale_map = jnp.exp(scale_late)
    sample = mean_late + scale_map * noise_late.astype(jnp.float32)
    near_resid = {move: flipped(residual, "tile", move) for move in [*early, far_odd]}
    late_b, residual = lax.optimization_barrier((sample_b, residual))
    other_samples = [rotated(late_b, "filt", r) for r in range(1, parts)]
    grad, turn, *other_turns = call(
        functools.partial(backward_own, sizes, [(None, 0), early_moves[0]], samples),
        "backward_own",
        [image_f32] * (1 + samples),
        tables,
        (back, residual, near_resid[early[0]], scale_map, noise, *other_noise),
        slot_scratch(2, jnp.float32),
    )
    (grad,) = call(
        functools.partial(backward_next, sizes, early_moves[1:]),
        "backward_next",
        [image_f32],
        tables,
        (back, *[near_resid[move] for move in early[1:]], grad),
        slot_scratch(len(early) - 1, jnp.float32),
        {len(tables) + len(early): 0},
    )
    (grad,) = call(
        functools.partial(backward_prior, sizes),
        "backward_prior",
        [image_f32],
        tables,
        (grad, sample, *other_samples),
        [],
        {len(tables): 0},
    )
    (grad,) = call(
        functools.partial(backward_next, sizes, [(far_odd, 0)]),
        "backward_last",
        [image_f32],
        tables,
        (back, near_resid[far_odd], grad),
        slot_scratch(1, jnp.float32),
        {len(tables) + 2: 0},
    )
    mean_sum = grad
    scale_sum = grad * turn
    for r in range(1, samples):
        other_grad = rotated(grad, "mc", r)
        mean_sum = mean_sum + other_grad
        scale_sum = scale_sum + other_grad * other_turns[r - 1]
    return ((mean_sum / samples)[None], (scale_sum / samples + 1.0)[None])

def solution(mesh):
    placed = (
        P("tile", "filt", None, None),
        P("tile", "filt", None, None),
        P("mc", "tile", "filt", None, None),
        P("tile", "filt", None, None),
        P("tile", "filt", None, None),
        P(),
        P(),
        P(),
        P(),
        P(),
    )
    return jax.shard_map(
        body,
        mesh=mesh,
        in_specs=placed,
        out_specs=(P("tile", "filt", None, None), P("tile", "filt", None, None)),
        check_vma=False,
    )
```
